128 devices in a mesh: ctx: 32 (over x_hi, y, z), fsdp: 4 (over x_lo, core).
Axes of the slice: x: 4 (x_hi: 2, x_lo: 2; x = x_hi * 2 + x_lo), y: 4, z: 4, core: 2. Of those that a mesh axis runs over, the one named last changes fastest.
Arguments:
- hidden_in: bfloat16 [4, 4096, 1024], P('fsdp', 'ctx'), may hold values from -6 to 6
- segment_ids: int32 [4, 4096], P('fsdp', 'ctx'), may hold values from 0 to 514, as said below
- block_order: int32 [4, 64], P('fsdp'), may hold values from 0 to 63, as said below
- expert_ids: int32 [4, 4096, 8], P('fsdp', 'ctx'), may hold values from 0 to 31, all different within a row
- pair_order: int32 [4, 32, 1024], P('fsdp', 'ctx'), may hold values from 0 to 1023, each once within a row
- attn_norm: bfloat16 [1024], P(('ctx', 'fsdp')), may hold values from 0.5 to 1.5
- w_query: bfloat16 [1024, 1024], P(('ctx', 'fsdp')), may hold values from -0.1875 to 0.1875
- w_key: bfloat16 [1024, 512], P(('ctx', 'fsdp')), may hold values from -0.1875 to 0.1875
- w_value: bfloat16 [1024, 512], P(('ctx', 'fsdp')), may hold values from -0.1875 to 0.1875
- query_norm: bfloat16 [1024], P(('ctx', 'fsdp')), may hold values from 0.5 to 1.5
- key_norm: bfloat16 [512], P(('ctx', 'fsdp')), may hold values from 0.5 to 1.5
- w_out: bfloat16 [1024, 1024], P(('ctx', 'fsdp')), may hold values from -0.75 to 0.75
- ffn_norm: bfloat16 [1024], P(('ctx', 'fsdp')), may hold values from 0.5 to 1.5
- w_router: bfloat16 [1024, 32], P(('ctx', 'fsdp')), may hold values from -0.09375 to 0.09375
- w_gate: bfloat16 [32, 1024, 512], P('ctx', 'fsdp'), may hold values from -0.1875 to 0.1875
- w_up: bfloat16 [32, 1024, 512], P('ctx', 'fsdp'), may hold values from -0.1875 to 0.1875
- w_down: bfloat16 [32, 512, 1024], P('ctx', 'fsdp'), may hold values from -0.75 to 0.75
- cotangent: bfloat16 [4, 4096, 1024], P('fsdp', 'ctx'), may hold values from -6 to 6
Outputs:
- layer_out: bfloat16 [4, 4096, 1024], P('fsdp', 'ctx')
- input_grad: float32 [4, 4096, 1024], P('fsdp', 'ctx')
- grad_attn_norm: float32 [1024], P(('ctx', 'fsdp'))
- grad_query: float32 [1024, 1024], P(('ctx', 'fsdp'))
- grad_key: float32 [1024, 512], P(('ctx', 'fsdp'))
- grad_value: float32 [1024, 512], P(('ctx', 'fsdp'))
- grad_query_norm: float32 [1024], P(('ctx', 'fsdp'))
- grad_key_norm: float32 [512], P(('ctx', 'fsdp'))
- grad_out: float32 [1024, 1024], P(('ctx', 'fsdp'))
- grad_ffn_norm: float32 [1024], P(('ctx', 'fsdp'))
- grad_router: float32 [1024, 32], P(('ctx', 'fsdp'))
- grad_gate: float32 [32, 1024, 512], P('ctx', 'fsdp')
- grad_up: float32 [32, 1024, 512], P('ctx', 'fsdp')
- grad_down: float32 [32, 512, 1024], P('ctx', 'fsdp')
The draws below stay inside these ranges and needn't reach their ends.
Inputs may be any that keep to these rules, and one draw needn't show every extreme that they name: `block_order`: for each sequence, entries 2 c and 2 c + 1 are a half-block b of the first half and 2 * 32 - 1 - b; each half-block appears once. `segment_ids`: in sequence-position order the ids of a sequence never fall; document 0 holds more than the first half of the sequence; the last document of each sequence has the largest id. `expert_ids`: each token names 8 different experts. `pair_order`: in each routing group the 1024 pairs, token-major, hold each priority once.
All inputs are finite; a program needn't handle non-finite values.
Results may differ from the reference program's by a relative error of at most 0.04.
Values may be sent and summed in bfloat16 or wider, within the bound.
No kernel may reach another device: no remote copies, remote signals or barrier semaphores. Data moves between devices by JAX's collectives and lax.ppermute only.
A program may use at most 192 MiB of HBM per device.

```python
import jax
import jax.numpy as jnp
from jax import lax

D = 1024
HEADS = 16
KVH = 8
HD = 64
FF = 512
EXPERTS = 32
TOPK = 8
TOK_DEV = 128
QD = 1024
KVD = 512
CAP = 32
SEQS = 4
SEQLEN = 4096
N_CTX = 32


def block_layout(key):
    seq_keys = jax.random.split(key, SEQS)
    shuffled = jax.vmap(lambda single: jax.random.permutation(single, N_CTX))(seq_keys).astype(jnp.int32)
    paired = jnp.stack([shuffled, 2 * N_CTX - 1 - shuffled], axis=-1)
    return paired.reshape(SEQS, 2 * N_CTX)


def draw_block_order(key, part):
    layout = block_layout(key)
    return layout.astype(jnp.int32)


def draw_segment_ids(key, part):
    layout = block_layout(key)
    key = jax.random.fold_in(key, 7)
    key_first, key_power, key_length = jax.random.split(key, 3)
    first_len = SEQLEN // 2 + jax.random.randint(key_first, (SEQS, 1), 1, SEQLEN // 4 + 1)
    doc_count = SEQLEN // 8 + 1
    top_power = max((SEQLEN // 4).bit_length(), 1)
    powers = jax.random.randint(key_power, (SEQS, doc_count), 0, top_power)
    lengths = 1 + jax.random.randint(key_length, (SEQS, doc_count), 0, jnp.left_shift(1, powers))
    ends = jnp.cumsum(lengths, axis=1)
    places = jnp.arange(SEQLEN, dtype=jnp.int32)[None, :]
    beyond = places - first_len
    later = 1 + jnp.sum((ends[:, None, :] <= beyond[:, :, None]).astype(jnp.int32), axis=2)
    seq_ids = jnp.where(beyond < 0, 0, later).astype(jnp.int32)
    last_doc = seq_ids[:, -1:]
    seq_ids = jnp.where(seq_ids == last_doc, SEQLEN // 8 + 2, seq_ids).astype(jnp.int32)
    half = TOK_DEV // 2
    lay = jnp.arange(SEQLEN, dtype=jnp.int32)
    seq_pos = jnp.take(layout, lay // half, axis=1) * half + lay % half
    return jnp.take_along_axis(seq_ids, seq_pos, axis=1).astype(jnp.int32)


def block_levels(own_key, dims, cuts, smallest, high):
    level = 1.0
    for axis_at, blocks in cuts:
        heights = jax.random.uniform(jax.random.fold_in(jax.random.fold_in(own_key, 6), axis_at), (blocks,), jnp.float32, smallest / len(cuts), high / len(cuts))
        level = level * jnp.repeat(jnp.exp(heights), dims[axis_at] // blocks).reshape((-1,) + (1,) * (len(dims) - 1 - axis_at))
    return level


def different_ones(own_key, rows, number_of, top, lift):
    sequence = jax.random.permutation(jax.random.fold_in(own_key, 1), number_of)
    pull = sequence
    for power in range(3):
        pull = pull * pull // number_of
    pull = pull * lift // number_of
    chance = jax.random.randint(jax.random.fold_in(own_key, 2), (rows, number_of), 0, 4096) + pull
    sure = jax.random.permutation(jax.random.fold_in(own_key, 3), rows)[jnp.arange(number_of) % rows]
    chance = jnp.where(jnp.arange(rows)[:, None] == sure[None, :], 1 << 14, chance)
    merit = chance * number_of + jnp.arange(number_of)
    return lax.top_k(merit.astype(jnp.int32), top)[1].astype(jnp.int32)


def scatter_about(own_key, shape, width, reach, pieces=(), held_as=jnp.bfloat16):
    level = block_levels(own_key, shape, pieces, -0.22, 0.18) if pieces else 1.0
    entries = jax.random.normal(own_key, shape, jnp.float32) * width * level
    return jnp.minimum(jnp.maximum(entries, -reach), reach).astype(held_as)


def setup_inputs(seed: int = 0) -> dict:
    arg_keys = jax.random.split(jax.random.key(seed), 19)
    hidden_in = scatter_about(arg_keys[0], (SEQS, SEQLEN, D), 1.0, 6.0, ((0, 4), (1, 32)))
    segment_ids = draw_segment_ids(jax.random.fold_in(arg_keys[18], 71), 0)
    block_order = draw_block_order(jax.random.fold_in(arg_keys[18], 71), 0)
    expert_ids = different_ones(arg_keys[3], SEQS * SEQLEN, EXPERTS, TOPK, 2048).reshape((SEQS, SEQLEN, TOPK))
    pair_order = jax.vmap(lambda own: jax.random.permutation(own, TOK_DEV * TOPK))(jax.random.split(arg_keys[4], SEQS * N_CTX)).reshape((SEQS, N_CTX, TOK_DEV * TOPK)).astype(jnp.int32)
    attn_norm = jnp.clip(1.0 + 0.1 * jax.random.normal(arg_keys[5], (D,), jnp.float32), 0.5, 1.5).astype(jnp.bfloat16)
    w_query = scatter_about(arg_keys[6], (D, QD), D ** -0.5, 0.1875, ((0, 128),))
    w_key = scatter_about(arg_keys[7], (D, KVD), D ** -0.5, 0.1875, ((0, 128),))
    w_value = scatter_about(arg_keys[8], (D, KVD), D ** -0.5, 0.1875, ((0, 128),))
    query_norm = jnp.clip(1.0 + 0.1 * jax.random.normal(arg_keys[9], (QD,), jnp.float32), 0.5, 1.5).astype(jnp.bfloat16)
    key_norm = jnp.clip(1.0 + 0.1 * jax.random.normal(arg_keys[10], (KVD,), jnp.float32), 0.5, 1.5).astype(jnp.bfloat16)
    w_out = scatter_about(arg_keys[11], (QD, D), (QD // 16) ** -0.5, 0.75, ((0, 128),))
    ffn_norm = jnp.clip(1.0 + 0.1 * jax.random.normal(arg_keys[12], (D,), jnp.float32), 0.5, 1.5).astype(jnp.bfloat16)
    w_router = scatter_about(arg_keys[13], (D, EXPERTS), (4 * D) ** -0.5, 0.09375, ((0, 128),))
    w_gate = scatter_about(arg_keys[14], (EXPERTS, D, FF), D ** -0.5, 0.1875, ((0, 32), (1, 4)))
    w_up = scatter_about(arg_keys[15], (EXPERTS, D, FF), D ** -0.5, 0.1875, ((0, 32), (1, 4)))
    w_down = scatter_about(arg_keys[16], (EXPERTS, FF, D), (FF // 8) ** -0.5, 0.75, ((0, 32), (1, 4)))
    cotangent = scatter_about(arg_keys[17], (SEQS, SEQLEN, D), 1.0, 6.0, ((0, 4), (1, 32)))
    return dict(hidden_in=hidden_in, segment_ids=segment_ids, block_order=block_order, expert_ids=expert_ids, pair_order=pair_order, attn_norm=attn_norm, w_query=w_query, w_key=w_key, w_value=w_value, query_norm=query_norm, key_norm=key_norm, w_out=w_out, ffn_norm=ffn_norm, w_router=w_router, w_gate=w_gate, w_up=w_up, w_down=w_down, cotangent=cotangent)


@jax.custom_vjp
def low(v):
    return lax.optimization_barrier(v.astype(jnp.bfloat16)).astype(jnp.float32)

@jax.custom_vjp
def low_back(v):
    return v

def low_keep(v):
    return (low(v), None)

def low_pass(kept, grad):
    return (grad,)

def back_keep(v):
    return (v, None)

def back_low(kept, grad):
    return (low(grad),)
low.defvjp(low_keep, low_pass)
low_back.defvjp(back_keep, back_low)
EPSILON = 1e-05
THETA = 10000.0
HIGHEST = lax.Precision.HIGHEST

def matmul(left, right):
    return jnp.dot(left, right, precision=HIGHEST)

def rms_scale(value, gain):
    return value * lax.rsqrt(lax.optimization_barrier(jnp.mean(value * value, axis=-1, keepdims=True)) + EPSILON) * gain

def angles(positions):
    freq = THETA ** (-jnp.arange(0, HD, 2).astype(jnp.float32) / HD)
    turned = positions.astype(jnp.float32)[:, None] * freq[None, :]
    return (jnp.cos(turned)[:, None, :], jnp.sin(turned)[:, None, :])

def rotate(value, cosine, sine):
    middle = value.shape[-1] // 2
    first = value[..., :middle]
    second = value[..., middle:]
    return jnp.concatenate([first * cosine - second * sine, second * cosine + first * sine], axis=-1)

def group_slots(pair):
    experts, ranks = pair
    earlier = (experts[:, None] == experts[None, :]) & (ranks[None, :] < ranks[:, None])
    return lax.optimization_barrier(jnp.sum(earlier.astype(jnp.int32), axis=1))

def layer_one(weights, inputs, positions, segments, target, kept, chosen):
    attn_norm, w_query, w_key, w_value, query_norm, key_norm, w_out, ffn_norm, w_router, w_gate, w_up, w_down = weights
    groups = HEADS // KVH
    cosine, sine = angles(positions)
    normed = low(rms_scale(inputs, attn_norm))
    query = low_back(matmul(normed, w_query))
    key_proj = low_back(matmul(normed, w_key))
    value_proj = low_back(matmul(normed, w_value))
    query_rot = rotate(rms_scale(query, query_norm).reshape(SEQLEN, HEADS, HD), cosine, sine)
    key_rot = rotate(rms_scale(key_proj, key_norm).reshape(SEQLEN, KVH, HD), cosine, sine)
    queries = low(query_rot).reshape(SEQLEN, KVH, groups, HD)
    keys = low(key_rot)
    values = low(value_proj).reshape(SEQLEN, KVH, HD)
    rows = min(512, SEQLEN)
    blocks = SEQLEN // rows

    def attend(block):
        query_block, segment_block = block
        scores = jnp.einsum('qkgd,tkd->kgqt', query_block, keys, precision=HIGHEST) * HD ** (-0.5)
        scores = low_back(scores)
        scores = jnp.where(segment_block[:, None] == segments[None, :], scores, -1e+30)
        probs = low(jax.nn.softmax(scores, axis=-1))
        return jnp.einsum('kgqt,tkd->qkgd', probs, values, precision=HIGHEST)
    mixed = lax.map(jax.checkpoint(attend), (queries.reshape(blocks, rows, KVH, groups, HD), segments.reshape(blocks, rows)))
    mixed = mixed.reshape(SEQLEN, QD)
    attended = low(low_back(mixed))
    middle = inputs + low_back(matmul(attended, w_out))
    routed_in = low(rms_scale(middle, ffn_norm))
    logits = low_back(matmul(routed_in, w_router))
    gates = jax.nn.softmax(jnp.take_along_axis(logits, chosen, axis=1), axis=-1)
    pairs = jnp.repeat(routed_in, TOPK, axis=0) * kept[:, None]
    buffer = jnp.zeros((EXPERTS * N_CTX * CAP + 1, D), jnp.float32).at[target].add(pairs)
    rows_in = low_back(buffer[:-1].reshape(EXPERTS, N_CTX * CAP, D))
    gate_act = low_back(jnp.einsum('erd,edf->erf', rows_in, w_gate, precision=HIGHEST))
    up_act = low_back(jnp.einsum('erd,edf->erf', rows_in, w_up, precision=HIGHEST))
    inner = low(jax.nn.silu(gate_act) * up_act)
    produced = low(low_back(jnp.einsum('erf,efd->erd', inner, w_down, precision=HIGHEST)))
    table = jnp.concatenate([produced.reshape(EXPERTS * N_CTX * CAP, D), jnp.zeros((1, D), jnp.float32)], axis=0)
    picked = table[target].reshape(SEQLEN, TOPK, D)
    share = gates * kept.reshape(SEQLEN, TOPK)
    return middle + lax.optimization_barrier(jnp.sum(picked * share[..., None], axis=1))

def reference(hidden_in, segment_ids, block_order, expert_ids, pair_order, attn_norm, w_query, w_key, w_value, query_norm, key_norm, w_out, ffn_norm, w_router, w_gate, w_up, w_down, cotangent):
    half = TOK_DEV // 2
    places = jnp.arange(SEQLEN)
    positions = (jnp.take(block_order, places // half, axis=1) * half + places % half).astype(jnp.int32)
    flat_ids = expert_ids.reshape(SEQS * N_CTX, TOK_DEV * TOPK)
    flat_ranks = pair_order.reshape(SEQS * N_CTX, TOK_DEV * TOPK)
    slots = lax.map(group_slots, (flat_ids, flat_ranks)).reshape(SEQS, N_CTX, TOK_DEV * TOPK)
    kept_mask = slots < CAP
    group_index = jnp.arange(N_CTX).astype(jnp.int32)[None, :, None]
    experts_here = expert_ids.reshape(SEQS, N_CTX, TOK_DEV * TOPK)
    target = jnp.where(kept_mask, experts_here * (N_CTX * CAP) + group_index * CAP + slots, EXPERTS * N_CTX * CAP)
    target = target.reshape(SEQS, SEQLEN * TOPK).astype(jnp.int32)
    kept = kept_mask.reshape(SEQS, SEQLEN * TOPK).astype(jnp.float32)
    weights = tuple((w.astype(jnp.float32) for w in (attn_norm, w_query, w_key, w_value, query_norm, key_norm, w_out, ffn_norm, w_router, w_gate, w_up, w_down)))

    def forward(inputs, params):

        def visit(carry, items):
            return (carry, layer_one(params, *items))
        _, outputs = lax.scan(visit, None, (inputs, positions, segment_ids, target, kept, expert_ids))
        return outputs
    result, pullback = jax.vjp(forward, hidden_in.astype(jnp.float32), weights)
    grad_input, grads = pullback(cotangent.astype(jnp.float32))
    return (result.astype(jnp.bfloat16), grad_input, grads[0], grads[1], grads[2], grads[3], grads[4], grads[5], grads[6], grads[7], grads[8], grads[9], grads[10], grads[11])
```

```python
import jax
import jax.numpy as jnp
from jax import lax
from jax.experimental import pallas as pl
from jax.experimental.pallas import tpu as pltpu
from jax.sharding import PartitionSpec as P

D = 1024
HEADS = 16
KVH = 8
HD = 64
EXPERTS = 32
TOPK = 8
TOK = 128
CAP = 32
N_CTX = 32
EPSILON = 1e-05
THETA = 10000.0
BF = jnp.bfloat16
F32 = jnp.float32

PAIR = ((0, 1), (1, 0), (2, 3), (3, 2))
HALF_HEADS = KVH // 2
QUARTERS = 4
ROWS = 2 * TOK
PACK = TOK + TOK // QUARTERS
KEYS = N_CTX * TOK
QUERIES = KEYS // QUARTERS
KEY_TILE = 512
TOK_TILE = 128


def dot(a, b, dims=((1,), (0,))):
    return lax.dot_general(a, b, (dims, ((), ())), preferred_element_type=F32)


def other(array):
    return lax.ppermute(array, "fsdp", PAIR)


def exchange(array, axis):
    return lax.all_to_all(array, axis, split_axis=0, concat_axis=0, tiled=True)


def lanes(shape):
    return lax.broadcasted_iota(jnp.int32, shape, len(shape) - 1)


def swap_halves(value):
    first = lanes(value.shape) % HD < HD // 2
    up = pltpu.roll(value, value.shape[1] - HD // 2, 1)
    down = pltpu.roll(value, HD // 2, 1)
    return jnp.where(first, up, down)


def vmem(count):
    return [pl.BlockSpec(memory_space=pltpu.VMEM)] * count


def params(mib=48):
    return pltpu.CompilerParams(vmem_limit_bytes=mib << 20)


def pack_kernel(qkv, scale_q, scale_k, gain, cosine, sine, out):
    for sl in range(2):
        rows = slice(sl * TOK, (sl + 1) * TOK)
        turn_c, turn_s = cosine[rows], sine[rows]
        cq, ck = scale_q[rows], scale_k[rows]
        for h in range(HALF_HEADS):
            at = h * 256
            q = qkv[rows, at : at + 128] * cq * gain[:, at : at + 128]
            q = (q * turn_c + swap_halves(q) * turn_s).astype(BF)
            kv = qkv[rows, at + 128 : at + 256]
            k = kv * ck * gain[:, at + 128 : at + 256]
            k = k * turn_c + swap_halves(k) * turn_s
            kv = jnp.where(lanes(kv.shape) < HD, k, kv).astype(BF)
            for qd in range(QUARTERS):
                to = (sl * HALF_HEADS + h) * QUARTERS + qd
                out[to, 0:TOK, :] = kv
                out[to, TOK : TOK + 16, :] = q[qd * 16 : qd * 16 + 16]
                out[to, TOK + 16 : TOK + 32, :] = q[64 + qd * 16 : 64 + qd * 16 + 16]


def unpack_kernel(grads, qkv, scale_q, scale_k, gain, cosine, sine, out, sums, gain_grad):
    for sl in range(2):
        rows = slice(sl * TOK, (sl + 1) * TOK)
        turn_c, turn_s = cosine[rows], sine[rows]
        cq, ck = scale_q[rows], scale_k[rows]
        sum_q = jnp.zeros((TOK, 128), F32)
        sum_k = jnp.zeros((TOK, 128), F32)
        for h in range(HALF_HEADS):
            at = h * 256
            base = (sl * HALF_HEADS + h) * QUARTERS
            pieces = [
                grads[base + qd, TOK + 16 * half : TOK + 16 * half + 16, :]
                for half in range(2)
                for qd in range(QUARTERS)
            ]
            dq = jnp.concatenate(pieces, axis=0).astype(F32)
            dq = dq * turn_c - swap_halves(dq) * turn_s
            dkv = sum(grads[base + qd, 0:TOK, :].astype(F32) for qd in range(QUARTERS))
            dk = dkv * turn_c - swap_halves(dkv) * turn_s
            is_k = lanes(dkv.shape) < HD
            dkv = jnp.where(is_k, dk, dkv)
            a_q = qkv[rows, at : at + 128] * cq
            a_k = qkv[rows, at + 128 : at + 256] * ck
            through_q = dq * a_q
            through_k = jnp.where(is_k, dkv * a_k, 0.0)
            g_q = gain[:, at : at + 128]
            g_k = gain[:, at + 128 : at + 256]
            out[rows, at : at + 128] = dq * g_q
            out[rows, at + 128 : at + 256] = dkv * g_k
            sum_q = sum_q + through_q * g_q
            sum_k = sum_k + through_k * g_k
            line_q = jnp.sum(through_q, axis=0, keepdims=True)
            line_k = jnp.sum(through_k, axis=0, keepdims=True)
            if sl == 0:
                gain_grad[:, at : at + 128] = line_q
                gain_grad[:, at + 128 : at + 256] = line_k
            else:
                gain_grad[:, at : at + 128] += line_q
                gain_grad[:, at + 128 : at + 256] += line_k
        total_q = jnp.sum(sum_q, axis=1, keepdims=True)
        total_k = jnp.sum(sum_k, axis=1, keepdims=True)
        sums[rows, :] = jnp.where(lanes((TOK, 128)) == 0, total_q, total_k)


def pick(first, rows_out):
    i = lax.broadcasted_iota(jnp.int32, (128, 128), 1 if rows_out else 0)
    j = lax.broadcasted_iota(jnp.int32, (128, 128), 0 if rows_out else 1)
    return (i == j % HD + first).astype(BF)


def head_rows(block):
    low_half = lanes(block.shape) < HD
    zero = jnp.zeros_like(block)
    return jnp.concatenate([jnp.where(low_half, block, zero), jnp.where(low_half, zero, block)], 0)


def forward_kernel(packed, seg_key, seg_query, mixed, lse, k2, v2t, score):
    @pl.when(pl.program_id(0) == 0)
    def _():
        kv = packed[:, 0:TOK, :].reshape(KEYS, 128)
        k2[...] = dot(kv, pick(0, False)).astype(BF)
        v2t[...] = dot(pick(HD, True), kv, ((1,), (1,))).astype(BF)

    tile = pl.program_id(0)
    src = TOK_TILE // 32
    q = packed[pl.ds(tile * src, src), TOK:PACK, :].reshape(TOK_TILE, 128)
    rows = head_rows(q * BF(HD**-0.5))
    seg_q = jnp.concatenate([seg_query[tile], seg_query[tile]], axis=1)
    newest = jnp.full((8, 2 * TOK_TILE), -1e30, F32)
    for j in range(KEYS // KEY_TILE):
        at = j * KEY_TILE
        s = dot(k2[at : at + KEY_TILE, :], rows, ((1,), (1,)))
        seg_k = seg_key[at : at + KEY_TILE, :]
        seg_k = jnp.concatenate([seg_k] * (2 * TOK_TILE // 128), axis=1)
        s = jnp.where(seg_k == seg_q, s, -1e30)
        score[at : at + KEY_TILE, :] = s
        newest = jnp.maximum(newest, jnp.max(s.reshape(KEY_TILE // 8, 8, 2 * TOK_TILE), axis=0))
    top = jnp.max(newest, axis=0, keepdims=True)
    total = jnp.zeros((8, 2 * TOK_TILE), F32)
    accum = jnp.zeros((128, 2 * TOK_TILE), F32)
    for j in range(KEYS // KEY_TILE):
        at = j * KEY_TILE
        p = jnp.exp(score[at : at + KEY_TILE, :] - top)
        total = total + jnp.sum(p.reshape(KEY_TILE // 8, 8, 2 * TOK_TILE), axis=0)
        accum = accum + dot(v2t[:, at : at + KEY_TILE], p.astype(BF))
    total = jnp.sum(total, axis=0, keepdims=True)
    out = (accum / total).T
    out = jnp.where(lanes((TOK_TILE, 128)) < HD, out[:TOK_TILE], out[TOK_TILE:])
    mixed[...] = out
    lse[0] = top + jnp.log(total)


def backward_kernel(packed, seg_key, seg_query, upper, lse, delta, dq_out, dkv_out, k2, k2t, v2, dk, dv):
    @pl.when(pl.program_id(0) == 0)
    def _():
        kv = packed[:, 0:TOK, :].reshape(KEYS, 128)
        k2[...] = dot(kv, pick(0, False)).astype(BF)
        k2t[...] = dot(pick(0, True), kv, ((1,), (1,))).astype(BF)
        v2[...] = dot(kv, pick(HD, False)).astype(BF)
        dk[...] = jnp.zeros_like(dk)
        dv[...] = jnp.zeros_like(dv)

    tile = pl.program_id(0)
    src = TOK_TILE // 32
    q = packed[pl.ds(tile * src, src), TOK:PACK, :].reshape(TOK_TILE, 128)
    rows = head_rows(q * BF(HD**-0.5))
    up = head_rows(upper[...].reshape(TOK_TILE, 128))
    seg_q = jnp.concatenate([seg_query[tile], seg_query[tile]], axis=1)
    dq = jnp.zeros((128, 2 * TOK_TILE), F32)
    for j in range(KEYS // KEY_TILE):
        at = j * KEY_TILE
        keys = slice(at, at + KEY_TILE)
        s = dot(k2[keys, :], rows, ((1,), (1,)))
        seg_k = jnp.concatenate([seg_key[keys, :]] * (2 * TOK_TILE // 128), axis=1)
        p = jnp.where(seg_k == seg_q, jnp.exp(s - lse[0]), 0.0)
        dp = dot(v2[keys, :], up, ((1,), (1,)))
        ds = (p * (dp - delta[0])).astype(BF)
        dv[keys, :] += dot(p.astype(BF), up)
        dk[keys, :] += dot(ds, rows)
        dq = dq + dot(k2t[:, keys], ds)
    dq = (dq * HD**-0.5).T
    dq = jnp.where(lanes((TOK_TILE, 128)) < HD, dq[:TOK_TILE], dq[TOK_TILE:])
    dq_out[...] = dq.astype(BF).reshape(src, 32, 128)

    @pl.when(tile == pl.num_programs(0) - 1)
    def _():
        for j in range(KEYS // KEY_TILE):
            keys = slice(j * KEY_TILE, (j + 1) * KEY_TILE)
            low_half = lanes((KEY_TILE, 128)) < HD
            both_k = dk[keys, :] + pltpu.roll(dk[keys, :], HD, 1)
            both_v = dv[keys, :] + pltpu.roll(dv[keys, :], HD, 1)
            both = jnp.where(low_half, both_k, both_v).astype(BF)
            dkv_out[j * KEY_TILE // TOK : (j + 1) * KEY_TILE // TOK] = both.reshape(-1, TOK, 128)


def whole(shape):
    return pl.BlockSpec(shape, lambda i: (0,) * len(shape))


def attend(packed, seg_key, seg_query):
    tiles = QUERIES // TOK_TILE
    return pl.pallas_call(
        forward_kernel,
        grid=(tiles,),
        in_specs=[
            whole((N_CTX, PACK, 128)),
            whole((KEYS, 128)),
            whole((tiles, 1, TOK_TILE)),
        ],
        out_specs=[
            pl.BlockSpec((TOK_TILE, 128), lambda i: (i, 0)),
            pl.BlockSpec((1, 1, 2 * TOK_TILE), lambda i: (i, 0, 0)),
        ],
        out_shape=[
            jax.ShapeDtypeStruct((QUERIES, 128), F32),
            jax.ShapeDtypeStruct((tiles, 1, 2 * TOK_TILE), F32),
        ],
        scratch_shapes=[
            pltpu.VMEM((KEYS, 128), BF),
            pltpu.VMEM((128, KEYS), BF),
            pltpu.VMEM((KEYS, 2 * TOK_TILE), F32),
        ],
        compiler_params=params(),
        name="attend",
    )(packed, seg_key, seg_query)


def attend_back(packed, seg_key, seg_query, upper, lse, delta):
    tiles = QUERIES // TOK_TILE
    src = TOK_TILE // 32
    line = pl.BlockSpec((1, 1, 2 * TOK_TILE), lambda i: (i, 0, 0))
    return pl.pallas_call(
        backward_kernel,
        grid=(tiles,),
        in_specs=[
            whole((N_CTX, PACK, 128)),
            whole((KEYS, 128)),
            whole((tiles, 1, TOK_TILE)),
            pl.BlockSpec((src, 32, 128), lambda i: (i, 0, 0)),
            line,
            line,
        ],
        out_specs=[
            pl.BlockSpec((src, 32, 128), lambda i: (i, 0, 0)),
            whole((N_CTX, TOK, 128)),
        ],
        out_shape=[
            jax.ShapeDtypeStruct((N_CTX, 32, 128), BF),
            jax.ShapeDtypeStruct((N_CTX, TOK, 128), BF),
        ],
        scratch_shapes=[
            pltpu.VMEM((KEYS, 128), BF),
            pltpu.VMEM((128, KEYS), BF),
            pltpu.VMEM((KEYS, 128), BF),
            pltpu.VMEM((KEYS, 128), F32),
            pltpu.VMEM((KEYS, 128), F32),
        ],
        compiler_params=params(),
        name="attend_back",
    )(packed, seg_key, seg_query, upper, lse, delta)


def pack(qkv, scale_q, scale_k, gain, cosine, sine):
    return pl.pallas_call(
        pack_kernel,
        in_specs=vmem(6),
        out_specs=pl.BlockSpec(memory_space=pltpu.VMEM),
        out_shape=jax.ShapeDtypeStruct((N_CTX, PACK, 128), BF),
        compiler_params=params(),
        name="pack",
    )(qkv, scale_q, scale_k, gain, cosine, sine)


def unpack(grads, qkv, scale_q, scale_k, gain, cosine, sine):
    return pl.pallas_call(
        unpack_kernel,
        in_specs=vmem(7),
        out_specs=vmem(3),
        out_shape=[
            jax.ShapeDtypeStruct((ROWS, D), F32),
            jax.ShapeDtypeStruct((ROWS, 128), F32),
            jax.ShapeDtypeStruct((1, D), F32),
        ],
        compiler_params=params(),
        name="unpack",
    )(grads, qkv, scale_q, scale_k, gain, cosine, sine)


def inverse_rms(value):
    return lax.rsqrt(jnp.mean(value * value, axis=-1, keepdims=True) + EPSILON)


def by_quarter(value):
    value = value.reshape(2, 2, QUARTERS, 16, HALF_HEADS, 128)
    return jnp.transpose(value, (0, 4, 2, 1, 3, 5)).reshape(N_CTX, 32, 128)


def from_quarters(value):
    value = value.reshape(2, HALF_HEADS, QUARTERS, 2, 16, 128)
    return jnp.transpose(value, (0, 3, 2, 4, 1, 5)).reshape(2, TOK, HALF_HEADS * 128)


def shards(
    hidden_in,
    segment_ids,
    block_order,
    expert_ids,
    pair_order,
    attn_norm,
    w_query,
    w_key,
    w_value,
    query_norm,
    key_norm,
    w_out,
    ffn_norm,
    w_router,
    w_gate,
    w_up,
    w_down,
    cotangent,
):
    place = lax.axis_index("ctx")
    core = lax.axis_index("fsdp") % 2
    both_axes = ("ctx", "fsdp")

    heads_w = jnp.concatenate(
        [
            w_query.reshape(8, 2, HALF_HEADS, 128),
            w_key.reshape(8, 2, HALF_HEADS, HD),
            w_value.reshape(8, 2, HALF_HEADS, HD),
        ],
        axis=-1,
    ).reshape(8, 2, D)
    small = jnp.concatenate(
        [
            w_router,
            attn_norm[:, None],
            query_norm[:, None],
            ffn_norm[:, None],
            jnp.pad(key_norm, (0, 4))[:, None],
        ],
        axis=1,
    )
    small = jnp.pad(small, ((0, 0), (0, 128 - small.shape[1])))
    outgoing_w = jnp.concatenate(
        [jnp.moveaxis(heads_w, 1, 0), jnp.broadcast_to(small, (2, 8, 128))], axis=-1
    )
    outgoing_w = jnp.broadcast_to(outgoing_w, (64, 2, 8, D + 128)).reshape(128, 8, D + 128)
    gathered = exchange(outgoing_w, both_axes).reshape(D, D + 128)

    tokens = hidden_in[0]
    tokens_2 = jnp.concatenate([tokens, other(tokens)], axis=0)
    order = block_order[0]
    order_2 = jnp.stack([order, other(order)])
    own_segments = segment_ids[0]
    segments_2 = jnp.stack([own_segments, other(own_segments)])
    outgoing_seg = jnp.broadcast_to(segments_2[:, None, None], (2, 16, 1, TOK)).reshape(N_CTX, 1, TOK)
    seg_all = exchange(outgoing_seg, "ctx").reshape(N_CTX, TOK)
    seg_key = jnp.broadcast_to(seg_all.reshape(KEYS, 1), (KEYS, 128))
    quarter = place % QUARTERS
    seg_query = lax.dynamic_index_in_dim(
        seg_all.reshape(N_CTX, 2, QUARTERS, 16), quarter, axis=2, keepdims=False
    ).reshape(QUERIES // TOK_TILE, 1, TOK_TILE)

    ids = expert_ids[0]
    experts = jnp.arange(EXPERTS, dtype=jnp.int32)
    named = ids.T[None, :, :] == experts[:, None, None]
    chosen = jnp.any(named, axis=1)
    ranks = pair_order[0, 0].reshape(TOK, TOPK).T
    rank = jnp.sum(jnp.where(named, ranks[None], 0), axis=1)
    earlier = chosen[:, :, None] & (rank[:, :, None] < rank[:, None, :])
    slot = jnp.sum(earlier.astype(jnp.int32), axis=1)
    kept = chosen & (slot < CAP)
    slot = jnp.where(kept, slot, -1)
    places = slot[:, None, :] == jnp.arange(CAP, dtype=jnp.int32)[None, :, None]
    one_hot = places.astype(BF).reshape(EXPERTS * CAP, TOK)

    lay = jnp.arange(TOK, dtype=jnp.int32)
    half = TOK // 2
    blocks = lax.dynamic_slice_in_dim(order_2, place * 2, 2, axis=1)
    positions = (jnp.repeat(blocks, half, axis=1) * half + lay % half).reshape(ROWS)
    freq = THETA ** (-jnp.arange(0, HD, 2).astype(F32) / HD)
    turned = positions.astype(F32)[:, None] * freq[None, :]
    cosine = jnp.tile(jnp.cos(turned), (1, 4))
    sine = jnp.sin(turned)
    sine = jnp.concatenate([-sine, sine, -sine, sine], axis=1)

    columns = gathered[:, D:].T.astype(F32)
    proj = gathered[:, :D]
    proj_router = gathered[:, D : D + EXPERTS]
    gain_attn = columns[EXPERTS][None]
    gain_query = columns[EXPERTS + 1]
    gain_ffn = columns[EXPERTS + 2][None]
    gain_key = columns[EXPERTS + 3].reshape(128, 8)[:, :4].reshape(512)
    gain_heads = jnp.concatenate(
        [
            lax.dynamic_slice_in_dim(gain_query, core * 512, 512).reshape(HALF_HEADS, 128),
            lax.dynamic_slice_in_dim(gain_key, core * 256, 256).reshape(HALF_HEADS, HD),
            jnp.ones((HALF_HEADS, HD), F32),
        ],
        axis=1,
    ).reshape(1, D)

    inputs_2 = tokens_2.astype(F32)
    scale_in = inverse_rms(inputs_2)
    normed_low = (inputs_2 * scale_in * gain_attn).astype(BF)
    qkv = dot(normed_low, proj)
    lane = jnp.arange(D)[None] % 256
    is_q, is_k = lane < 128, (lane >= 128) & (lane < 192)
    squares = qkv * qkv
    square_sums = jnp.stack(
        [
            jnp.sum(jnp.where(is_q, squares, 0.0), axis=1),
            jnp.sum(jnp.where(is_k, squares, 0.0), axis=1),
        ]
    )
    square_sums = square_sums + other(jnp.roll(square_sums, TOK, axis=1))
    scale_q = lax.rsqrt(square_sums[0] / 1024 + EPSILON)[:, None]
    scale_k = lax.rsqrt(square_sums[1] / 512 + EPSILON)[:, None]
    packed = exchange(pack(qkv, scale_q, scale_k, gain_heads, cosine, sine), "ctx")

    w_out_late, packed = lax.optimization_barrier((w_out, packed))
    proj_out = exchange(jnp.broadcast_to(w_out_late, (128, 8, D)), both_axes).reshape(D, D)
    gate_up = lax.all_gather(jnp.concatenate([w_gate, w_up], axis=0), "fsdp", axis=1, tiled=True)
    gate_w, up_w = gate_up[0], gate_up[1]
    down_w = lax.all_gather(w_down, "fsdp", axis=1, tiled=True)[0]

    mixed, lse = attend(packed, seg_key, seg_query)
    returned = from_quarters(exchange(mixed.astype(BF).reshape(N_CTX, 32, 128), "ctx"))
    mine, theirs = returned[0], other(returned[1])
    attended = jnp.where(
        core == 0,
        jnp.concatenate([mine, theirs], axis=1),
        jnp.concatenate([theirs, mine], axis=1),
    )
    inputs = tokens.astype(F32)
    middle = inputs + dot(attended, proj_out)
    scale_mid = inverse_rms(middle)
    scaled_mid = middle * scale_mid
    routed_in = (scaled_mid * gain_ffn).astype(BF)
    logits = dot(proj_router, routed_in, ((0,), (1,)))
    logits = jnp.where(chosen, logits, -1e30)
    raised = jnp.where(chosen, jnp.exp(logits - jnp.max(logits, axis=0, keepdims=True)), 0.0)
    gates = raised / jnp.sum(raised, axis=0, keepdims=True)

    upstream_low = cotangent[0]
    upstream = upstream_low.astype(F32)
    rows_out = dot(one_hot, routed_in).astype(BF).reshape(EXPERTS, CAP, D)
    arrived = exchange(rows_out, "ctx").reshape(N_CTX * CAP, D)
    share = jnp.where(places, gates[:, None, :], 0.0)
    row_share = jnp.sum(share, axis=2).reshape(EXPERTS * CAP, 1)
    grads_out = (dot(one_hot, upstream_low) * row_share).astype(BF).reshape(EXPERTS, CAP, D)
    arrived_grad = exchange(grads_out, "ctx").reshape(N_CTX * CAP, D)

    gate_act = dot(arrived, gate_w)
    up_act = dot(arrived, up_w)
    sigma = jax.nn.sigmoid(gate_act)
    silu_gate = gate_act * sigma
    inner = (silu_gate * up_act).astype(BF)
    produced = dot(inner, down_w).astype(BF).reshape(N_CTX, CAP, D)
    produced_home = exchange(produced, "ctx").reshape(EXPERTS * CAP, D)

    grad_inner = dot(arrived_grad, down_w, ((1,), (1,)))
    grad_gate_act = (grad_inner * up_act * sigma * (1.0 + gate_act * (1.0 - sigma))).astype(BF)
    grad_up_act = (grad_inner * silu_gate).astype(BF)
    grad_rows = dot(grad_gate_act, gate_w, ((1,), (1,))) + dot(grad_up_act, up_w, ((1,), (1,)))
    grad_rows = grad_rows.astype(BF).reshape(N_CTX, CAP, D)
    grad_home = exchange(grad_rows, "ctx").reshape(EXPERTS * CAP, D)

    grad_gate_w = dot(arrived, grad_gate_act, ((0,), (0,))).astype(BF)
    grad_up_w = dot(arrived, grad_up_act, ((0,), (0,))).astype(BF)
    grad_down_w = dot(inner, arrived_grad, ((0,), (0,))).astype(BF)
    grad_gate_up = lax.psum_scatter(
        jnp.stack([grad_gate_w, grad_up_w]), "fsdp", scatter_dimension=1, tiled=True
    ).astype(F32)
    grad_down = lax.psum_scatter(
        grad_down_w[None], "fsdp", scatter_dimension=1, tiled=True
    ).astype(F32)

    share = share.reshape(EXPERTS * CAP, TOK)
    share_high = share.astype(BF)
    share_low = (share - share_high.astype(F32)).astype(BF)
    shares = jnp.concatenate([share_high, share_low], axis=1)
    combined = dot(shares, produced_home, ((0,), (0,)))
    layer_out = (middle + (combined[:TOK] + combined[TOK:])).astype(BF)[None]
    along = dot(produced_home, upstream_low, ((1,), (1,))).reshape(EXPERTS, CAP, TOK)
    grad_gates = jnp.sum(jnp.where(places, along, 0.0), axis=1)
    grad_chosen = gates * (grad_gates - jnp.sum(gates * grad_gates, axis=0, keepdims=True))
    grad_logits = grad_chosen.astype(BF)
    grad_router = dot(routed_in, grad_logits, ((0,), (1,)))
    grad_routed = dot(grad_logits, proj_router, ((0,), (1,)))
    grad_routed = grad_routed + dot(one_hot, grad_home, ((0,), (0,)))
    grad_ffn_gain = jnp.sum(grad_routed * scaled_mid, axis=0)
    through = grad_routed * gain_ffn
    grad_middle = upstream + scale_mid * (
        through - scaled_mid * jnp.mean(through * scaled_mid, axis=1, keepdims=True)
    )
    grad_branch = grad_middle.astype(BF)
    grad_mixed = dot(grad_branch, proj_out, ((1,), (1,))).astype(BF)
    low_heads, high_heads = grad_mixed[:, :512], grad_mixed[:, 512:]
    own_heads = jnp.where(core == 0, low_heads, high_heads)
    other_heads = jnp.where(core == 0, high_heads, low_heads)
    heads_2 = jnp.stack([own_heads, other(other_heads)])
    upper = exchange(by_quarter(heads_2), "ctx")

    late = (
        dot(attended, grad_branch, ((0,), (0,))).astype(BF),
        grad_router.astype(BF),
        grad_ffn_gain[:, None].astype(BF),
        jnp.zeros((D, 95), BF),
    )
    late, upper = lax.optimization_barrier((late, upper))
    first_sums = exchange(jnp.concatenate(late, axis=1).reshape(128, 8, D + 128), both_axes)

    delta = jnp.sum(
        (upper.reshape(QUERIES, 128).astype(F32) * mixed).reshape(QUERIES, 2, HD), axis=2
    )
    tiles = QUERIES // TOK_TILE
    delta = jnp.transpose(delta.reshape(tiles, TOK_TILE, 2), (0, 2, 1)).reshape(tiles, 1, 2 * TOK_TILE)
    dq, dkv = attend_back(packed, seg_key, seg_query, upper, lse, delta)
    grads_home = exchange(jnp.concatenate([dkv, dq], axis=1), "ctx")

    through_heads, sums, grad_gain_heads = unpack(
        grads_home, qkv, scale_q, scale_k, gain_heads, cosine, sine
    )
    sums = sums[:, :2].T
    sums = sums + other(jnp.roll(sums, TOK, axis=1))
    scale_heads = jnp.where(is_q, scale_q, jnp.where(is_k, scale_k, 1.0))
    mean_heads = jnp.where(
        is_q, sums[0][:, None] / 1024, jnp.where(is_k, sums[1][:, None] / 512, 0.0)
    )
    grad_qkv = (scale_heads * (through_heads - qkv * scale_heads * mean_heads)).astype(BF)
    grad_proj = dot(normed_low, grad_qkv, ((0,), (0,))).astype(BF)
    grad_normed = dot(grad_qkv, proj, ((1,), (1,)))
    grad_normed = grad_normed[:TOK] + other(grad_normed[TOK:])
    scaled_in = inputs * scale_in[:TOK]
    grad_attn_gain = jnp.sum(grad_normed * scaled_in, axis=0)
    through_in = grad_normed * gain_attn
    input_grad = grad_middle + scale_in[:TOK] * (
        through_in - scaled_in * jnp.mean(through_in * scaled_in, axis=1, keepdims=True)
    )

    gain_lines = grad_gain_heads.reshape(HALF_HEADS, 256)
    query_line = gain_lines[:, :128].reshape(512)
    key_line = gain_lines[:, 128:192].reshape(256)
    query_line = lax.dynamic_update_slice_in_dim(jnp.zeros((1024,), F32), query_line, core * 512, 0)
    key_line = lax.dynamic_update_slice_in_dim(jnp.zeros((512,), F32), key_line, core * 256, 0)
    key_line = jnp.pad(key_line.reshape(128, 4), ((0, 0), (0, 4))).reshape(1024)
    lines = jnp.stack([grad_attn_gain, query_line, key_line], axis=1).astype(BF)
    last = jnp.concatenate([grad_proj, lines, jnp.zeros((D, 125), BF)], axis=1)
    last_sums = exchange(last.reshape(128, 8, D + 128), both_axes)

    first_sums = jnp.sum(first_sums.astype(F32), axis=0)
    last_sums = jnp.sum(last_sums.reshape(64, 2, 8, D + 128).astype(F32), axis=0)
    heads_g = last_sums[:, :, :D].reshape(2, 8, HALF_HEADS, 256)
    heads_g = jnp.transpose(heads_g, (1, 0, 2, 3))
    lines_g = last_sums[0, :, D : D + 3] + last_sums[1, :, D : D + 3]
    return (
        layer_out,
        input_grad[None],
        lines_g[:, 0],
        heads_g[..., :128].reshape(8, 1024),
        heads_g[..., 128:192].reshape(8, 512),
        heads_g[..., 192:].reshape(8, 512),
        lines_g[:, 1],
        lines_g[:4, 2],
        first_sums[:, :D],
        first_sums[:, D + EXPERTS],
        first_sums[:, D : D + EXPERTS],
        grad_gate_up[0][None],
        grad_gate_up[1][None],
        grad_down,
    )


def solution(mesh):
    row = P("fsdp", "ctx", None)
    flat = P(("ctx", "fsdp"))
    dense = P(("ctx", "fsdp"), None)
    expert = P("ctx", "fsdp", None)
    in_specs = (
        row,
        P("fsdp", "ctx"),
        P("fsdp", None),
        row,
        row,
        flat,
        dense,
        dense,
        dense,
        flat,
        flat,
        dense,
        flat,
        dense,
        expert,
        expert,
        expert,
        row,
    )
    out_specs = (
        row,
        row,
        flat,
        dense,
        dense,
        dense,
        flat,
        flat,
        dense,
        flat,
        dense,
        expert,
        expert,
        expert,
    )
    return jax.shard_map(shards, mesh=mesh, in_specs=in_specs, out_specs=out_specs, check_vma=False)
```

```python
import jax
import jax.numpy as jnp
from jax import lax
from jax.experimental import pallas as pl
from jax.experimental.pallas import tpu as pltpu
from jax.sharding import PartitionSpec as P

D = 1024
HEADS = 16
KVH = 8
HD = 64
EXPERTS = 32
TOPK = 8
TOK = 128
CAP = 32
N_CTX = 32
EPSILON = 1e-05
THETA = 10000.0
BF = jnp.bfloat16
F32 = jnp.float32

PARTS = 2
PART_HEADS = KVH // PARTS
COLS = PART_HEADS * 256
FEATURES = PART_HEADS * 128
ROWS = PARTS * TOK
QUARTERS = 4
PACK = TOK + TOK // QUARTERS
KEYS = N_CTX * TOK
QUERIES = KEYS // QUARTERS
KEY_TILE = 512
TOK_TILE = 128
TILES = QUERIES // TOK_TILE


def dot(a, b, dims=((1,), (0,))):
    return lax.dot_general(a, b, (dims, ((), ())), preferred_element_type=F32)


def swap(array, j):
    return lax.ppermute(array, "fsdp", [(i, i ^ j) for i in range(4)]) if j else array


def swapped(pieces):
    return [swap(piece, j) for j, piece in enumerate(pieces)]


def sum_parts(value):
    step = 1
    while step < PARTS:
        value = value + swap(jnp.stack([value[:, j ^ step] for j in range(PARTS)], 1), step)
        step *= 2
    return value


def exchange(array, axis):
    return lax.all_to_all(array, axis, split_axis=0, concat_axis=0, tiled=True)


def lanes(shape):
    return lax.broadcasted_iota(jnp.int32, shape, len(shape) - 1)


def swap_halves(value):
    first = lanes(value.shape) % HD < HD // 2
    up = pltpu.roll(value, value.shape[1] - HD // 2, 1)
    down = pltpu.roll(value, HD // 2, 1)
    return jnp.where(first, up, down)


def call(kernel, inputs, outputs, name, micros=2, mib=12):
    vmem = pl.BlockSpec(memory_space=pltpu.VMEM)
    return pl.pallas_call(
        kernel,
        in_specs=[vmem] * len(inputs),
        out_specs=[pl.BlockSpec() if sent else vmem for _, _, sent in outputs],
        out_shape=[jax.ShapeDtypeStruct(shape, dtype) for shape, dtype, _ in outputs],
        compiler_params=pltpu.CompilerParams(vmem_limit_bytes=mib << 20),
        cost_estimate=estimate(micros),
        name=name,
    )(*inputs)


def estimate(micros):
    return pl.CostEstimate(flops=int(micros * 1.1e9), bytes_accessed=1 << 16, transcendentals=0)


def weights_kernel(w_query, w_key, w_value, w_router, gains, segments, out):
    row = lax.broadcasted_iota(jnp.int32, (8, 128), 0)
    lane = lanes((8, 128))
    middle = (lane >= 32) & (lane < 96)
    seg = segments[...]
    low, high = (seg & 255).astype(F32), (seg >> 8).astype(F32)
    small = jnp.zeros((8, 128), F32)
    lines = (
        pltpu.roll(low, 32, 1),
        pltpu.roll(low, 96, 1),
        pltpu.roll(high, 32, 1),
        pltpu.roll(high, 96, 1),
    )
    for r, line in enumerate(lines):
        small = jnp.where((row == r + 1) & middle, line, small)
    small = jnp.where((row == 0) & (lane >= 32), pltpu.roll(gains[...], 32, 1), small)
    router = jnp.concatenate([w_router[...].astype(F32), jnp.zeros((8, 96), F32)], axis=1)
    small = jnp.where(lane < 32, router, small)
    parts = []
    for p in range(PARTS):
        columns = []
        for h in range(PART_HEADS):
            at = p * PART_HEADS + h
            columns.append(w_query[:, at * 128 : at * 128 + 128].astype(F32))
            columns.append(w_key[:, at * HD : at * HD + HD].astype(F32))
            columns.append(w_value[:, at * HD : at * HD + HD].astype(F32))
        parts.append(jnp.concatenate(columns + [small], axis=1).astype(BF))
    for to in range(4 * N_CTX):
        out[to] = parts[to % PARTS]


def pack_kernel(qkv, scale_q, scale_k, gain, cosine, sine, out):
    for j in range(PARTS):
        rows = slice(j * TOK, (j + 1) * TOK)
        turn_c, turn_s = cosine[rows], sine[rows]
        cq, ck = scale_q[rows], scale_k[rows]
        for h in range(PART_HEADS):
            at = h * 256
            q = qkv[rows, at : at + 128] * cq * gain[:, at : at + 128]
            q = (q * turn_c + swap_halves(q) * turn_s).astype(BF)
            kv = qkv[rows, at + 128 : at + 256]
            k = kv * ck * gain[:, at + 128 : at + 256]
            k = k * turn_c + swap_halves(k) * turn_s
            kv = jnp.where(lanes(kv.shape) < HD, k, kv).astype(BF)
            for qd in range(QUARTERS):
                to = (j * PART_HEADS + h) * QUARTERS + qd
                out[to, 0:TOK, :] = kv
                out[to, TOK : TOK + 16, :] = q[qd * 16 : qd * 16 + 16]
                out[to, TOK + 16 : TOK + 32, :] = q[64 + qd * 16 : 64 + qd * 16 + 16]


def unpack_kernel(grads_q, qkv, scale_q, scale_k, gain, cosine, sine, out, sums, gain_grad):
    grads = grads_q
    for j in range(PARTS):
        rows = slice(j * TOK, (j + 1) * TOK)
        turn_c, turn_s = cosine[rows], sine[rows]
        cq, ck = scale_q[rows], scale_k[rows]
        sum_q = jnp.zeros((TOK, 128), F32)
        sum_k = jnp.zeros((TOK, 128), F32)
        for h in range(PART_HEADS):
            at = h * 256
            base = (j * PART_HEADS + h) * QUARTERS
            pieces = [
                grads[base + qd, TOK + 16 * half : TOK + 16 * half + 16, :]
                for half in range(2)
                for qd in range(QUARTERS)
            ]
            dq = jnp.concatenate(pieces, axis=0).astype(F32)
            dq = dq * turn_c - swap_halves(dq) * turn_s
            dkv = sum(grads[base + qd, 0:TOK, :].astype(F32) for qd in range(QUARTERS))
            dk = dkv * turn_c - swap_halves(dkv) * turn_s
            is_k = lanes(dkv.shape) < HD
            dkv = jnp.where(is_k, dk, dkv)
            a_q = qkv[rows, at : at + 128] * cq
            a_k = qkv[rows, at + 128 : at + 256] * ck
            through_q = dq * a_q
            through_k = jnp.where(is_k, dkv * a_k, 0.0)
            g_q = gain[:, at : at + 128]
            g_k = gain[:, at + 128 : at + 256]
            out[rows, at : at + 128] = dq * g_q
            out[rows, at + 128 : at + 256] = dkv * g_k
            sum_q = sum_q + through_q * g_q
            sum_k = sum_k + through_k * g_k
            line_q = jnp.sum(through_q, axis=0, keepdims=True)
            line_k = jnp.sum(through_k, axis=0, keepdims=True)
            if j == 0:
                gain_grad[:, at : at + 128] = line_q
                gain_grad[:, at + 128 : at + 256] = line_k
            else:
                gain_grad[:, at : at + 128] += line_q
                gain_grad[:, at + 128 : at + 256] += line_k
        total_q = jnp.sum(sum_q, axis=1, keepdims=True)
        total_k = jnp.sum(sum_k, axis=1, keepdims=True)
        sums[rows, :] = jnp.where(lanes((TOK, 128)) == 0, total_q, total_k)


def heads_in_kernel(received, out):
    for j in range(PARTS):
        for h in range(PART_HEADS):
            for qd in range(QUARTERS):
                block = received[(j * PART_HEADS + h) * QUARTERS + qd]
                columns = slice(h * 128, h * 128 + 128)
                out[j, qd * 16 : qd * 16 + 16, columns] = block[:16]
                out[j, 64 + qd * 16 : 80 + qd * 16, columns] = block[16:]


def heads_out_kernel(*refs):
    out = refs[-1]
    for j in range(PARTS):
        for h in range(PART_HEADS):
            for qd in range(QUARTERS):
                to = (j * PART_HEADS + h) * QUARTERS + qd
                columns = slice(h * 128, h * 128 + 128)
                out[to, :16] = refs[j][qd * 16 : qd * 16 + 16, columns]
                out[to, 16:] = refs[j][64 + qd * 16 : 80 + qd * 16, columns]


def finish_kernel(through, qkv, scale_q, scale_k, sum_q, sum_k, normed, proj, scaled_in, small, last, grad_normed):
    lane = lanes((TOK, COLS)) % 256
    is_q, is_k = lane < 128, (lane >= 128) & (lane < 192)
    grads = []
    for j in range(PARTS):
        rows = slice(j * TOK, (j + 1) * TOK)
        scale = jnp.where(is_q, scale_q[rows], jnp.where(is_k, scale_k[rows], 1.0))
        mean = jnp.where(is_q, sum_q[rows] / 1024, jnp.where(is_k, sum_k[rows] / 512, 0.0))
        grads.append((scale * (through[rows, :] - qkv[rows, :] * scale * mean)).astype(BF))
    grad = jnp.concatenate(grads, axis=0)
    normed_grad = dot(grad, proj[...], ((1,), (1,)))
    grad_normed[...] = normed_grad
    products = (normed_grad * scaled_in[...]).astype(BF)
    ones = jnp.where(lanes((ROWS, 128)) == 64, 1.0, 0.0).astype(BF)
    last[:, :COLS] = dot(normed[...], grad, ((0,), (0,))).astype(BF)
    last[:, COLS:] = (small[...].astype(F32) + dot(products, ones, ((0,), (0,)))).astype(BF)


def finish_out_kernel(attended, branch, routed, logits, products, out):
    out[:, :512] = dot(attended[...], branch[...], ((0,), (0,))).astype(BF)
    ones = jnp.where(lanes((TOK, 128)) == 64, 1.0, 0.0).astype(BF)
    small = dot(routed[...], logits[...], ((0,), (0,))) + dot(products[...], ones, ((0,), (0,)))
    out[:, 512:] = small.astype(BF)


def pick(first, rows_out):
    i = lax.broadcasted_iota(jnp.int32, (128, 128), 1 if rows_out else 0)
    j = lax.broadcasted_iota(jnp.int32, (128, 128), 0 if rows_out else 1)
    return (i == j % HD + first).astype(BF)


def head_rows(block):
    low_half = lanes(block.shape) < HD
    zero = jnp.zeros_like(block)
    return jnp.concatenate([jnp.where(low_half, block, zero), jnp.where(low_half, zero, block)], 0)


def query_rows(block):
    low_half = lanes(block.shape) < HD
    block = block.astype(F32) * HD**-0.5
    return jnp.concatenate(
        [
            jnp.where(low_half, block, 0.0),
            jnp.where(low_half, pltpu.roll(block, HD, 1), 0.0),
        ],
        axis=0,
    ).astype(BF)


def key_segments(seg_key, columns):
    for src in range(N_CTX):
        line = jnp.broadcast_to(seg_key[src : src + 1, :], (TOK, TOK))
        columns[src * TOK : (src + 1) * TOK, :] = line.T


def forward_kernel(packed, seg_key, seg_query, mixed, mixed_low, lse, kv, kv_t, columns, limits):
    src = TOK_TILE // 32
    kv[...] = packed[:, 0:TOK, :].reshape(KEYS, 128)
    i = lax.broadcasted_iota(jnp.int32, (128, 128), 0)
    kv_t[...] = dot((i == lanes((128, 128))).astype(BF), kv[...], ((1,), (1,))).astype(BF)
    key_segments(seg_key, columns)
    limits[...] = jnp.ones_like(limits)

    def tile_rows(tile):
        q = packed[pl.ds(tile * src, src), TOK:PACK, :].reshape(TOK_TILE, 128)
        return query_rows(q), jnp.concatenate([seg_query[tile], seg_query[tile]], axis=1)

    def scores(rows, seg_q, keys):
        s = dot(kv[keys, :], rows, ((1,), (1,)))
        seg_k = jnp.concatenate([columns[keys, :]] * (2 * TOK_TILE // 128), axis=1)
        return jnp.where(seg_k == seg_q, s, -1e30)

    def sums(p):
        return jnp.sum(p.reshape(KEY_TILE // 8, 8, 2 * TOK_TILE), axis=0)

    def store(tile, accum, total, top):
        out = (accum / total).T
        out = jnp.where(
            lanes((TOK_TILE, 128)) < HD, pltpu.roll(out[:TOK_TILE], HD, 1), out[TOK_TILE:]
        )
        mixed[pl.ds(tile * TOK_TILE, TOK_TILE), :] = out
        mixed_low[pl.ds(tile * src, src)] = out.astype(BF).reshape(src, 32, 128)
        lse[tile] = top + jnp.log(total)

    for tile in range(TILES):
        rows, seg_q = tile_rows(tile)
        total = jnp.zeros((8, 2 * TOK_TILE), F32)
        accum = jnp.zeros((128, 2 * TOK_TILE), F32)
        for t in range(KEYS // KEY_TILE):
            keys = slice(t * KEY_TILE, (t + 1) * KEY_TILE)
            p = jnp.exp(scores(rows, seg_q, keys))
            total = total + sums(p)
            accum = accum + dot(kv_t[:, keys], p.astype(BF))
        total = jnp.sum(total, axis=0, keepdims=True)
        store(tile, accum, total, jnp.zeros_like(total))
        limits[...] = jnp.maximum(limits[...], jnp.maximum(total, 1.0 / total))

    @pl.when(jnp.logical_not(jnp.max(limits[...]) < 1e25))
    def _():
        @pl.loop(0, TILES)
        def _(tile):
            rows, seg_q = tile_rows(tile)
            top = jnp.full((1, 2 * TOK_TILE), -1e30, F32)
            total = jnp.zeros((8, 2 * TOK_TILE), F32)
            accum = jnp.zeros((128, 2 * TOK_TILE), F32)
            for t in range(KEYS // KEY_TILE):
                keys = slice(t * KEY_TILE, (t + 1) * KEY_TILE)
                s = scores(rows, seg_q, keys)
                newest = jnp.maximum(top, jnp.max(s, axis=0, keepdims=True))
                fade = jnp.exp(top - newest)
                p = jnp.exp(s - newest)
                p = jnp.where(s > -1e29, p, 0.0)
                top = newest
                total = total * fade + sums(p)
                accum = accum * fade + dot(kv_t[:, keys], p.astype(BF))
            store(tile, accum, jnp.sum(total, axis=0, keepdims=True), top)


def backward_kernel(packed, seg_key, seg_query, upper, mixed, lse, out, k2, k2t, v2, dk, dv, columns):
    @pl.when(pl.program_id(0) == 0)
    def _():
        kv = packed[:, 0:TOK, :].reshape(KEYS, 128)
        k2[...] = dot(kv, pick(0, False)).astype(BF)
        k2t[...] = dot(pick(0, True), kv, ((1,), (1,))).astype(BF)
        v2[...] = dot(kv, pick(HD, False)).astype(BF)
        dk[...] = jnp.zeros_like(dk)
        dv[...] = jnp.zeros_like(dv)
        key_segments(seg_key, columns)

    tile = pl.program_id(0)
    src = TOK_TILE // 32
    q = packed[pl.ds(tile * src, src), TOK:PACK, :].reshape(TOK_TILE, 128)
    rows = head_rows(q * BF(HD**-0.5))
    upper_now = upper[...].reshape(TOK_TILE, 128)
    up = head_rows(upper_now)
    along = (upper_now.astype(F32) * mixed[...]).T
    delta = jnp.concatenate(
        [
            jnp.sum(along[:HD], axis=0, keepdims=True),
            jnp.sum(along[HD:], axis=0, keepdims=True),
        ],
        axis=1,
    )
    seg_q = jnp.concatenate([seg_query[tile], seg_query[tile]], axis=1)
    dq = jnp.zeros((128, 2 * TOK_TILE), F32)
    for t in range(KEYS // KEY_TILE):
        at = t * KEY_TILE
        keys = slice(at, at + KEY_TILE)
        s = dot(k2[keys, :], rows, ((1,), (1,)))
        seg_k = jnp.concatenate([columns[keys, :]] * (2 * TOK_TILE // 128), axis=1)
        p = jnp.where(seg_k == seg_q, jnp.exp(s - lse[0]), 0.0)
        dp = dot(v2[keys, :], up, ((1,), (1,)))
        ds = (p * (dp - delta)).astype(BF)
        dv[keys, :] += dot(p.astype(BF), up)
        dk[keys, :] += dot(ds, rows)
        dq = dq + dot(k2t[:, keys], ds)
    dq = (dq * HD**-0.5).T
    dq = jnp.where(lanes((TOK_TILE, 128)) < HD, dq[:TOK_TILE], dq[TOK_TILE:])
    out[pl.ds(tile * src, src), TOK:PACK, :] = dq.astype(BF).reshape(src, 32, 128)

    @pl.when(tile == pl.num_programs(0) - 1)
    def _():
        for t in range(KEYS // KEY_TILE):
            keys = slice(t * KEY_TILE, (t + 1) * KEY_TILE)
            low_half = lanes((KEY_TILE, 128)) < HD
            both_k = dk[keys, :] + pltpu.roll(dk[keys, :], HD, 1)
            both_v = dv[keys, :] + pltpu.roll(dv[keys, :], HD, 1)
            both = jnp.where(low_half, both_k, both_v).astype(BF).reshape(-1, TOK, 128)
            out[t * KEY_TILE // TOK : (t + 1) * KEY_TILE // TOK, 0:TOK, :] = both


def whole(shape):
    return pl.BlockSpec(shape, lambda i: (0,) * len(shape))


def attend(packed, seg_key, seg_query):
    vmem = pl.BlockSpec(memory_space=pltpu.VMEM)
    return pl.pallas_call(
        forward_kernel,
        in_specs=[vmem] * 3,
        out_specs=[vmem, pl.BlockSpec(), vmem],
        out_shape=[
            jax.ShapeDtypeStruct((QUERIES, 128), F32),
            jax.ShapeDtypeStruct((N_CTX, 32, 128), BF),
            jax.ShapeDtypeStruct((TILES, 1, 2 * TOK_TILE), F32),
        ],
        scratch_shapes=[
            pltpu.VMEM((KEYS, 128), BF),
            pltpu.VMEM((128, KEYS), BF),
            pltpu.VMEM((KEYS, 128), jnp.int32),
            pltpu.VMEM((1, 2 * TOK_TILE), F32),
        ],
        compiler_params=pltpu.CompilerParams(vmem_limit_bytes=24 << 20),
        cost_estimate=estimate(12),
        name="attend",
    )(packed, seg_key, seg_query)


def attend_back(packed, seg_key, seg_query, upper, mixed, lse):
    src = TOK_TILE // 32
    return pl.pallas_call(
        backward_kernel,
        grid=(TILES,),
        in_specs=[
            whole((N_CTX, PACK, 128)),
            whole((N_CTX, TOK)),
            whole((TILES, 1, TOK_TILE)),
            pl.BlockSpec((src, 32, 128), lambda i: (i, 0, 0)),
            pl.BlockSpec((TOK_TILE, 128), lambda i: (i, 0)),
            pl.BlockSpec((1, 1, 2 * TOK_TILE), lambda i: (i, 0, 0)),
        ],
        out_specs=whole((N_CTX, PACK, 128)),
        out_shape=jax.ShapeDtypeStruct((N_CTX, PACK, 128), BF),
        scratch_shapes=[
            pltpu.VMEM((KEYS, 128), BF),
            pltpu.VMEM((128, KEYS), BF),
            pltpu.VMEM((KEYS, 128), BF),
            pltpu.VMEM((KEYS, 128), F32),
            pltpu.VMEM((KEYS, 128), F32),
            pltpu.VMEM((KEYS, 128), jnp.int32),
        ],
        compiler_params=pltpu.CompilerParams(vmem_limit_bytes=32 << 20),
        cost_estimate=estimate(25),
        name="attend_back",
    )(packed, seg_key, seg_query, upper, mixed, lse)


def in_order(pieces, fsdp):
    pieces = jnp.stack(pieces)
    return jnp.concatenate(
        [lax.dynamic_index_in_dim(pieces, fsdp ^ p, keepdims=False) for p in range(4)], axis=0
    )


def inverse_rms(value):
    return lax.rsqrt(jnp.mean(value * value, axis=-1, keepdims=True) + EPSILON)


def after(value, *others):
    return lax.optimization_barrier((value, *others))[0]


def shards(
    hidden_in,
    segment_ids,
    block_order,
    expert_ids,
    pair_order,
    attn_norm,
    w_query,
    w_key,
    w_value,
    query_norm,
    key_norm,
    w_out,
    ffn_norm,
    w_router,
    w_gate,
    w_up,
    w_down,
    cotangent,
):
    place = lax.axis_index("ctx")
    fsdp = lax.axis_index("fsdp")
    core = fsdp % 2
    part = fsdp % PARTS
    both_axes = ("ctx", "fsdp")

    gains = jnp.concatenate([attn_norm, query_norm, ffn_norm, key_norm, jnp.zeros((100,), BF)])
    outgoing_w = call(
        weights_kernel,
        (w_query, w_key, w_value, w_router, gains.astype(F32)[None], segment_ids),
        [((4 * N_CTX, 8, COLS + 128), BF, True)],
        "weights",
    )[0]
    out_rows, outgoing_w = lax.optimization_barrier(
        ([swap(w_out, j) for j in range(4)], outgoing_w)
    )
    gathered = exchange(outgoing_w, both_axes)
    small = gathered[:, :, COLS:]

    tokens = hidden_in[0]
    order = block_order[0]
    blocks = lax.dynamic_slice_in_dim(order, place * 2, 2)
    if PARTS == 2:
        tokens_all = [tokens, swap(tokens, 1)]
        blocks_all = [blocks, swap(blocks, 1)]
    else:
        far, far_blocks = swap(tokens, 2), swap(blocks, 2)
        tokens_all = [tokens, swap(tokens, 1), far, swap(far, 1)]
        blocks_all = [blocks, swap(blocks, 1), far_blocks, swap(far_blocks, 1)]
    tokens_all = jnp.concatenate(tokens_all, axis=0)

    proj_out = lax.all_gather(in_order(out_rows, fsdp), "ctx", axis=0, tiled=True)

    ids = expert_ids[0]
    experts = jnp.arange(EXPERTS, dtype=jnp.int32)
    named = ids.T[None, :, :] == experts[:, None, None]
    chosen = jnp.any(named, axis=1)
    ranks = pair_order[0, 0].reshape(TOK, TOPK).T
    rank = jnp.sum(jnp.where(named, ranks[None], 0), axis=1)
    earlier = chosen[:, :, None] & (rank[:, :, None] < rank[:, None, :])
    slot = jnp.sum(earlier.astype(jnp.int32), axis=1)
    kept = chosen & (slot < CAP)
    slot = jnp.where(kept, slot, -1)
    places = slot[:, None, :] == jnp.arange(CAP, dtype=jnp.int32)[None, :, None]
    one_hot = places.astype(BF).reshape(EXPERTS * CAP, TOK)

    lay = jnp.arange(TOK, dtype=jnp.int32)
    half = TOK // 2
    positions = (jnp.repeat(jnp.stack(blocks_all), half, axis=1) * half + lay % half).reshape(ROWS)
    freq = THETA ** (-jnp.arange(0, HD, 2).astype(F32) / HD)
    turned = positions.astype(F32)[:, None] * freq[None, :]
    cosine = jnp.tile(jnp.cos(turned), (1, 4))
    sine = jnp.sin(turned)
    sine = jnp.concatenate([-sine, sine, -sine, sine], axis=1)

    lines = small[:, 0, 32:60].astype(F32)
    gain_attn = lines[:, 0:8].reshape(1, D)
    gain_query = lines[:, 8:16].reshape(D)
    gain_ffn = lines[:, 16:24].reshape(1, D)
    gain_key = lines[:, 24:28].reshape(512)
    gain_heads = jnp.concatenate(
        [
            lax.dynamic_slice_in_dim(gain_query, part * FEATURES, FEATURES).reshape(PART_HEADS, 128),
            lax.dynamic_slice_in_dim(gain_key, part * FEATURES // 2, FEATURES // 2).reshape(
                PART_HEADS, HD
            ),
            jnp.ones((PART_HEADS, HD), F32),
        ],
        axis=1,
    ).reshape(1, COLS)
    proj = gathered[:, :, :COLS].reshape(D, COLS)
    proj_router = small[:, :, :EXPERTS].reshape(D, EXPERTS)

    inputs_all = tokens_all.astype(F32)
    scale_in = inverse_rms(inputs_all)
    scaled_in = inputs_all * scale_in
    normed_low = (scaled_in * gain_attn).astype(BF)
    qkv = dot(normed_low, proj)
    lane = jnp.arange(COLS)[None] % 256
    is_q, is_k = lane < 128, (lane >= 128) & (lane < 192)
    squares = qkv * qkv
    square_sums = jnp.stack(
        [
            jnp.sum(jnp.where(is_q, squares, 0.0), axis=1),
            jnp.sum(jnp.where(is_k, squares, 0.0), axis=1),
        ]
    )
    square_sums = sum_parts(square_sums.reshape(2, PARTS, TOK)).reshape(2, ROWS)
    scale_q = lax.rsqrt(square_sums[0] / 1024 + EPSILON)[:, None]
    scale_k = lax.rsqrt(square_sums[1] / 512 + EPSILON)[:, None]
    packed = call(
        pack_kernel,
        (qkv, scale_q, scale_k, gain_heads, cosine, sine),
        [((N_CTX, PACK, 128), BF, True)],
        "pack",
    )[0]
    packed = exchange(packed, "ctx")

    sequence = fsdp ^ (place // (N_CTX // PARTS))
    seg_small = lax.dynamic_index_in_dim(
        small.reshape(N_CTX, 4, 8, 128), sequence, axis=1, keepdims=False
    )[:, 1:5, 32:96].astype(jnp.int32)
    seg_all = (seg_small[:, 0:2] + 256 * seg_small[:, 2:4]).reshape(N_CTX, TOK)
    seg_query = lax.dynamic_index_in_dim(
        seg_all.reshape(N_CTX, 2, QUARTERS, 16), place % QUARTERS, axis=2, keepdims=False
    ).reshape(TILES, 1, TOK_TILE)

    packed, shard_gate, shard_up, shard_down = lax.optimization_barrier(
        (packed, w_gate[0], w_up[0], w_down[0])
    )
    shards_far = [swap(shard, 2) for shard in (shard_gate, shard_up, shard_down)]
    gate_w, up_w, down_w = [
        in_order([own, swap(own, 1), far, swap(far, 1)], fsdp)
        for own, far in zip((shard_gate, shard_up, shard_down), shards_far)
    ]

    mixed, mixed_low, lse = attend(packed, seg_all, seg_query)
    returned = exchange(mixed_low, "ctx")
    returned = call(heads_in_kernel, (returned,), [((PARTS, TOK, FEATURES), BF, False)], "heads_in", 1)[0]
    pieces = swapped([returned[j] for j in range(PARTS)])
    out_parts = proj_out.reshape(PARTS, FEATURES, D)
    out_parts = [
        lax.dynamic_index_in_dim(out_parts, part ^ j, keepdims=False) for j in range(PARTS)
    ]
    inputs = tokens.astype(F32)
    middle = inputs
    for piece, out_part in zip(pieces, out_parts):
        middle = middle + dot(piece, out_part)
    scale_mid = inverse_rms(middle)
    scaled_mid = middle * scale_mid
    routed_in = (scaled_mid * gain_ffn).astype(BF)
    logits = dot(proj_router, routed_in, ((0,), (1,)))
    logits = jnp.where(chosen, logits, -1e30)
    raised = jnp.where(chosen, jnp.exp(logits - jnp.max(logits, axis=0, keepdims=True)), 0.0)
    gates = raised / jnp.sum(raised, axis=0, keepdims=True)

    upstream_low = cotangent[0]
    upstream = upstream_low.astype(F32)
    rows_out = dot(one_hot, routed_in).astype(BF).reshape(EXPERTS, CAP, D)
    arrived = exchange(rows_out, "ctx").reshape(N_CTX * CAP, D)
    share = jnp.where(places, gates[:, None, :], 0.0)
    row_share = jnp.sum(share, axis=2).reshape(EXPERTS * CAP, 1)
    grads_out = (dot(one_hot, upstream_low) * row_share).astype(BF).reshape(EXPERTS, CAP, D)
    arrived, grads_out, gate_w, up_w, down_w = lax.optimization_barrier(
        (arrived, grads_out, gate_w, up_w, down_w)
    )
    arrived_grad = exchange(grads_out, "ctx").reshape(N_CTX * CAP, D)

    gate_act = dot(arrived, gate_w)
    up_act = dot(arrived, up_w)
    sigma = jax.nn.sigmoid(gate_act)
    silu_gate = gate_act * sigma
    inner = (silu_gate * up_act).astype(BF)
    produced = dot(inner, down_w).astype(BF).reshape(N_CTX, CAP, D)
    produced, arrived_grad = lax.optimization_barrier((produced, arrived_grad))
    produced_home = exchange(produced, "ctx").reshape(EXPERTS * CAP, D)

    grad_inner = dot(arrived_grad, down_w, ((1,), (1,)))
    grad_gate_act = (grad_inner * up_act * sigma * (1.0 + gate_act * (1.0 - sigma))).astype(BF)
    grad_up_act = (grad_inner * silu_gate).astype(BF)
    grad_rows = dot(grad_gate_act, gate_w, ((1,), (1,))) + dot(grad_up_act, up_w, ((1,), (1,)))
    grad_rows = grad_rows.astype(BF).reshape(N_CTX, CAP, D)
    produced_home, grad_rows = lax.optimization_barrier((produced_home, grad_rows))
    grad_home = exchange(grad_rows, "ctx").reshape(EXPERTS * CAP, D)

    share = share.reshape(EXPERTS * CAP, TOK)
    share_high = share.astype(BF)
    share_low = (share - share_high.astype(F32)).astype(BF)
    combined = dot(share_high, produced_home, ((0,), (0,)))
    combined = combined + dot(share_low, produced_home, ((0,), (0,)))
    layer_out = (middle + combined).astype(BF)[None]
    along = dot(produced_home, upstream_low, ((1,), (1,))).reshape(EXPERTS, CAP, TOK)
    grad_gates = jnp.sum(jnp.where(places, along, 0.0), axis=1)
    grad_chosen = gates * (grad_gates - jnp.sum(gates * grad_gates, axis=0, keepdims=True))
    grad_logits = grad_chosen.astype(BF)
    grad_routed = dot(grad_logits, proj_router, ((0,), (1,)))
    grad_routed = grad_routed + dot(one_hot, grad_home, ((0,), (0,)))
    through = grad_routed * gain_ffn
    grad_middle = upstream + scale_mid * (
        through - scaled_mid * jnp.mean(through * scaled_mid, axis=1, keepdims=True)
    )
    grad_branch = grad_middle.astype(BF)
    grad_mixed = [dot(grad_branch, out_part, ((1,), (1,))).astype(BF) for out_part in out_parts]
    upper = call(
        heads_out_kernel, tuple(swapped(grad_mixed)), [((N_CTX, 32, 128), BF, True)], "heads_out", 1
    )[0]
    upper, arrived, arrived_grad = lax.optimization_barrier((upper, arrived, arrived_grad))
    upper = exchange(upper, "ctx")

    grad_gate_w = dot(arrived, grad_gate_act, ((0,), (0,))).astype(BF)
    grad_up_w = dot(arrived, grad_up_act, ((0,), (0,))).astype(BF)
    grad_down_w = dot(inner, arrived_grad, ((0,), (0,))).astype(BF)
    grad_gate_up = lax.psum_scatter(
        jnp.stack([grad_gate_w, grad_up_w]), "fsdp", scatter_dimension=1, tiled=True
    ).astype(F32)
    grad_down = lax.psum_scatter(
        grad_down_w[None], "fsdp", scatter_dimension=1, tiled=True
    ).astype(F32)

    sorted_pieces = jnp.stack(pieces)
    attended = jnp.concatenate(
        [
            lax.dynamic_index_in_dim(sorted_pieces, part ^ p, keepdims=False)
            for p in range(PARTS)
        ],
        axis=1,
    )
    attended_2 = jnp.concatenate([attended, swap(attended, 1)], axis=0)
    branch_halves = jnp.stack([grad_branch[:, :512], grad_branch[:, 512:]])
    own_half = lax.dynamic_index_in_dim(branch_halves, core, keepdims=False)
    other_half = lax.dynamic_index_in_dim(branch_halves, 1 - core, keepdims=False)
    branch_2 = jnp.concatenate([own_half, swap(other_half, 1)], axis=0)
    late = call(
        finish_out_kernel,
        (
            attended_2,
            branch_2,
            routed_in,
            jnp.pad(grad_logits.T, ((0, 0), (0, 128 - EXPERTS))),
            (grad_routed * scaled_mid).astype(BF),
        ),
        [((D, 640), BF, True)],
        "finish_out",
    )[0]
    late, upper = lax.optimization_barrier((late, upper))
    first_sums = exchange(late.reshape(4 * N_CTX, 8, 640), both_axes)

    grads_home = attend_back(packed, seg_all, seg_query, upper, mixed, lse)
    grads_home, first_sums = lax.optimization_barrier((grads_home, first_sums))
    grads_home = exchange(grads_home, "ctx")

    through_heads, sums, grad_gain_heads = call(
        unpack_kernel,
        (grads_home, qkv, scale_q, scale_k, gain_heads, cosine, sine),
        [((ROWS, COLS), F32, False), ((ROWS, 128), F32, False), ((1, COLS), F32, False)],
        "unpack",
    )
    sums = sum_parts(sums[:, :2].T.reshape(2, PARTS, TOK)).reshape(2, ROWS)
    gain_lines = grad_gain_heads.reshape(PART_HEADS, 256)
    query_line = gain_lines[:, :128].reshape(FEATURES)
    key_line = gain_lines[:, 128:192].reshape(FEATURES // 2)
    query_line = lax.dynamic_update_slice_in_dim(
        jnp.zeros((1024,), F32), query_line, part * FEATURES, 0
    )
    key_line = lax.dynamic_update_slice_in_dim(
        jnp.zeros((512,), F32), key_line, part * FEATURES // 2, 0
    )
    small_grads = jnp.concatenate([query_line.reshape(128, 8), key_line.reshape(128, 4)], axis=1)
    small_grads = jnp.pad(small_grads.astype(BF)[:, None, :], ((0, 0), (0, 7), (0, 116)))
    last, grad_normed = call(
        finish_kernel,
        (
            through_heads,
            qkv,
            scale_q,
            scale_k,
            sums[0][:, None],
            sums[1][:, None],
            normed_low,
            proj,
            scaled_in,
            small_grads.reshape(D, 128),
        ),
        [((D, COLS + 128), BF, True), ((ROWS, D), F32, False)],
        "finish",
        3,
        24,
    )
    last_sums = exchange(last.reshape(4 * N_CTX, 8, COLS + 128), both_axes)

    grad_normed = grad_normed.reshape(PARTS, TOK, D)
    if PARTS == 4:
        grad_normed = grad_normed.astype(BF)
    grad_normed = sum(
        piece.astype(F32) for piece in swapped([grad_normed[j] for j in range(PARTS)])
    )
    through_in = grad_normed * gain_attn
    scaled_own = scaled_in[:TOK]
    input_grad = grad_middle + scale_in[:TOK] * (
        through_in - scaled_own * jnp.mean(through_in * scaled_own, axis=1, keepdims=True)
    )

    first_sums = jnp.sum(first_sums.reshape(2 * N_CTX, 2, 8, 640).astype(F32), axis=0)
    grad_out = jnp.concatenate([first_sums[0, :, :512], first_sums[1, :, :512]], axis=1)
    first_small = first_sums[0, :, 512:] + first_sums[1, :, 512:]
    last_sums = jnp.sum(
        last_sums.reshape(4 * N_CTX // PARTS, PARTS, 8, COLS + 128).astype(F32), axis=0
    )
    heads_g = last_sums[:, :, :COLS].reshape(PARTS, 8, PART_HEADS, 256)
    heads_g = jnp.transpose(heads_g, (1, 0, 2, 3))
    last_small = jnp.sum(last_sums[:, :, COLS:], axis=0)
    return (
        layer_out,
        input_grad[None],
        last_small[:, 64],
        heads_g[..., :128].reshape(8, 1024),
        heads_g[..., 128:192].reshape(8, 512),
        heads_g[..., 192:].reshape(8, 512),
        last_small[0, 0:8],
        last_small[0, 8:12],
        grad_out,
        first_small[:, 64],
        first_small[:, :EXPERTS],
        grad_gate_up[0][None],
        grad_gate_up[1][None],
        grad_down,
    )


def solution(mesh):
    row = P("fsdp", "ctx", None)
    flat = P(("ctx", "fsdp"))
    dense = P(("ctx", "fsdp"), None)
    expert = P("ctx", "fsdp", None)
    in_specs = (
        row,
        P("fsdp", "ctx"),
        P("fsdp", None),
        row,
        row,
        flat,
        dense,
        dense,
        dense,
        flat,
        flat,
        dense,
        flat,
        dense,
        expert,
        expert,
        expert,
        row,
    )
    out_specs = (
        row,
        row,
        flat,
        dense,
        dense,
        dense,
        flat,
        flat,
        dense,
        flat,
        dense,
        expert,
        expert,
        expert,
    )
    return jax.shard_map(shards, mesh=mesh, in_specs=in_specs, out_specs=out_specs, check_vma=False)
```

```python
import jax
import jax.numpy as jnp
from jax import lax
from jax.experimental import pallas as pl
from jax.experimental.pallas import tpu as pltpu
from jax.sharding import PartitionSpec as P

D = 1024
HEADS = 16
KVH = 8
HD = 64
EXPERTS = 32
TOPK = 8
TOK = 128
CAP = 32
N_CTX = 32
EPSILON = 1e-05
THETA = 10000.0
BF = jnp.bfloat16
F32 = jnp.float32

PARTS = 2
PART_HEADS = KVH // PARTS
COLS = PART_HEADS * 256
FEATURES = PART_HEADS * 128
ROWS = PARTS * TOK
QUARTERS = 4
PACK = TOK + TOK // QUARTERS
KEYS = N_CTX * TOK
QUERIES = KEYS // QUARTERS
KEY_TILE = 512
VMEM_LIMIT = 62 << 20
TOK_TILE = 128
TILES = QUERIES // TOK_TILE


def dot(a, b, dims=((1,), (0,))):
    return lax.dot_general(a, b, (dims, ((), ())), preferred_element_type=F32)


def swap(array, j):
    return lax.ppermute(array, "fsdp", [(i, i ^ j) for i in range(4)]) if j else array


def swapped(pieces):
    return [swap(piece, j) for j, piece in enumerate(pieces)]


def sum_parts(value):
    step = 1
    while step < PARTS:
        value = value + swap(jnp.stack([value[:, j ^ step] for j in range(PARTS)], 1), step)
        step *= 2
    return value


def exchange(array, axis):
    return lax.all_to_all(array, axis, split_axis=0, concat_axis=0, tiled=True)


def lanes(shape):
    return lax.broadcasted_iota(jnp.int32, shape, len(shape) - 1)


def swap_halves(value):
    first = lanes(value.shape) % HD < HD // 2
    up = pltpu.roll(value, value.shape[1] - HD // 2, 1)
    down = pltpu.roll(value, HD // 2, 1)
    return jnp.where(first, up, down)


def call_near(kernel, inputs, outputs, name, micros=2, mib=12):
    vmem = pl.BlockSpec(memory_space=pltpu.VMEM)
    return pl.pallas_call(
        kernel,
        in_specs=[vmem] * len(inputs),
        out_specs=[pl.BlockSpec() if sent else vmem for _, _, sent in outputs],
        out_shape=[jax.ShapeDtypeStruct(shape, dtype) for shape, dtype, _ in outputs],
        compiler_params=pltpu.CompilerParams(vmem_limit_bytes=mib << 20),
        cost_estimate=estimate(micros),
        name=name,
    )(*inputs)


class Held:
    def __init__(self, buffer, copy):
        self.buffer, self.copy = buffer, copy

    def wait(self):
        if self.copy is not None:
            self.copy.wait()
            self.copy = None

    def __getitem__(self, index):
        self.wait()
        return self.buffer[index]


class Made:
    def __init__(self, buffer, target, sems, first):
        self.buffer, self.target, self.sems, self.first = buffer, target, sems, first
        self.copies = []

    def __getitem__(self, index):
        return self.buffer[index]

    def __setitem__(self, index, value):
        self.buffer[index] = value

    def send(self, rows=None):
        source, target = self.buffer, self.target
        if rows is not None:
            source, target = source.at[rows], target.at[rows]
        copy = pltpu.make_async_copy(source, target, self.sems.at[self.first + len(self.copies)])
        copy.start()
        self.copies.append(copy)


SENDS = 4


def far(array, rows=None, at=None, cut=None):
    return (array, rows, at, cut)


def call(kernel, inputs, outputs, name, micros=2, ids=None):
    hbm = pl.BlockSpec(memory_space=pltpu.HBM)
    inputs = [i if isinstance(i, tuple) else far(i) for i in inputs]
    scratch = []
    for array, rows, _, part in inputs:
        shape = array.shape if rows is None else (rows, *array.shape[1:])
        if part is not None:
            shape = tuple(p.stop - p.start for p in part) + array.shape[len(part) :]
        scratch.append(pltpu.VMEM(shape, array.dtype))
    scratch += [pltpu.VMEM(shape, dtype) for shape, dtype in outputs]
    scratch.append(pltpu.SemaphoreType.DMA((len(inputs) + SENDS * len(outputs),)))
    numbers = [] if ids is None else [ids]

    def body(*refs):
        refs = list(refs)
        own_ids = refs.pop(0) if numbers else None
        ins, outs = refs[: len(inputs)], refs[len(inputs) : len(inputs) + len(outputs)]
        buffers = refs[len(inputs) + len(outputs) :]
        sems = buffers[-1]
        given, results = [], []
        for k, (ref, (_, rows, at, part)) in enumerate(zip(ins, inputs)):
            if rows is not None:
                ref = ref.at[pl.ds(pl.multiple_of(own_ids[at] * rows, rows), rows)]
            elif part is not None:
                ref = ref.at[part]
            copy = pltpu.make_async_copy(ref, buffers[k], sems.at[k])
            copy.start()
            given.append(Held(buffers[k], copy))
        for k, ref in enumerate(outs):
            results.append(Made(buffers[len(inputs) + k], ref, sems, len(inputs) + SENDS * k))
        kernel(*([own_ids] if numbers else []), *given, *results)
        for held in given:
            held.wait()
        for made in results:
            if not made.copies:
                made.send()
        for made in results:
            for copy in made.copies:
                copy.wait()

    return pl.pallas_call(
        body,
        in_specs=[pl.BlockSpec(memory_space=pltpu.SMEM)] * len(numbers) + [hbm] * len(inputs),
        out_specs=[hbm] * len(outputs),
        out_shape=[jax.ShapeDtypeStruct(shape, dtype) for shape, dtype in outputs],
        scratch_shapes=scratch,
        compiler_params=pltpu.CompilerParams(vmem_limit_bytes=VMEM_LIMIT),
        cost_estimate=estimate(micros),
        name=name,
    )(*numbers, *[i[0] for i in inputs])


def estimate(micros):
    return pl.CostEstimate(flops=int(micros * 1.1e9), bytes_accessed=1 << 16, transcendentals=0)


def weights_kernel(w_query, w_key, w_value, w_router, attn, query, ffn, key, segments, out):
    row = lax.broadcasted_iota(jnp.int32, (8, 128), 0)
    lane = lanes((8, 128))
    middle = (lane >= 32) & (lane < 96)
    gains = [line[...].astype(F32) for line in (attn, query, ffn, key)]
    gains = jnp.concatenate(gains + [jnp.zeros((1, 100), F32)], axis=1)
    seg = segments[...]
    low, high = (seg & 255).astype(F32), (seg >> 8).astype(F32)
    small = jnp.zeros((8, 128), F32)
    lines = (
        pltpu.roll(low, 32, 1),
        pltpu.roll(low, 96, 1),
        pltpu.roll(high, 32, 1),
        pltpu.roll(high, 96, 1),
    )
    for r, line in enumerate(lines):
        small = jnp.where((row == r + 1) & middle, line, small)
    small = jnp.where((row == 0) & (lane >= 32), pltpu.roll(gains, 32, 1), small)
    router = jnp.concatenate([w_router[...].astype(F32), jnp.zeros((8, 96), F32)], axis=1)
    small = jnp.where(lane < 32, router, small)
    parts = []
    for p in range(PARTS):
        columns = []
        for h in range(PART_HEADS):
            at = p * PART_HEADS + h
            columns.append(w_query[:, at * 128 : at * 128 + 128].astype(F32))
            columns.append(w_key[:, at * HD : at * HD + HD].astype(F32))
            columns.append(w_value[:, at * HD : at * HD + HD].astype(F32))
        parts.append(jnp.concatenate(columns + [small], axis=1).astype(BF))
    for to in range(4 * N_CTX):
        out[to] = parts[to % PARTS]


def pack_kernel(qkv, scale_q, scale_k, gain, cosine, sine, out):
    for j in range(PARTS):
        rows = slice(j * TOK, (j + 1) * TOK)
        turn_c, turn_s = cosine[rows], sine[rows]
        cq, ck = scale_q[rows], scale_k[rows]
        for h in range(PART_HEADS):
            at = h * 256
            q = qkv[rows, at : at + 128] * cq * gain[:, at : at + 128]
            q = (q * turn_c + swap_halves(q) * turn_s).astype(BF)
            kv = qkv[rows, at + 128 : at + 256]
            k = kv * ck * gain[:, at + 128 : at + 256]
            k = k * turn_c + swap_halves(k) * turn_s
            kv = jnp.where(lanes(kv.shape) < HD, k, kv).astype(BF)
            for qd in range(QUARTERS):
                to = (j * PART_HEADS + h) * QUARTERS + qd
                out[to, 0:TOK, :] = kv
                out[to, TOK : TOK + 16, :] = q[qd * 16 : qd * 16 + 16]
                out[to, TOK + 16 : TOK + 32, :] = q[64 + qd * 16 : 64 + qd * 16 + 16]


def other_rows(value):
    return jnp.concatenate([value[TOK:], value[:TOK]], axis=0)


def unpack_kernel(grads, qkv, scales, gains, cosine, sine, out, sums, gain_grad):
    gain = gains[0:1, :]
    lines = [None] * (2 * PART_HEADS)
    for j in range(PARTS):
        rows = slice(j * TOK, (j + 1) * TOK)
        turn_c, turn_s = cosine[rows, :], sine[rows, :]
        cq, ck = scales[rows, 0:1], scales[rows, 1:2]
        sum_q = jnp.zeros((TOK, 128), F32)
        sum_k = jnp.zeros((TOK, 128), F32)
        for h in range(PART_HEADS):
            at = h * 256
            base = (j * PART_HEADS + h) * QUARTERS
            pieces = [
                grads[base + qd, TOK + 16 * half : TOK + 16 * half + 16, :]
                for half in range(2)
                for qd in range(QUARTERS)
            ]
            dq = jnp.concatenate(pieces, axis=0).astype(F32)
            dq = dq * turn_c - swap_halves(dq) * turn_s
            dkv = sum(grads[base + qd, 0:TOK, :].astype(F32) for qd in range(QUARTERS))
            dk = dkv * turn_c - swap_halves(dkv) * turn_s
            is_k = lanes(dkv.shape) < HD
            dkv = jnp.where(is_k, dk, dkv)
            a_q = qkv[rows, at : at + 128] * cq
            a_k = qkv[rows, at + 128 : at + 256] * ck
            through_q = dq * a_q
            through_k = jnp.where(is_k, dkv * a_k, 0.0)
            g_q = gain[:, at : at + 128]
            g_k = gain[:, at + 128 : at + 256]
            out[rows, at : at + 128] = dq * g_q
            out[rows, at + 128 : at + 256] = dkv * g_k
            sum_q = sum_q + through_q * g_q
            sum_k = sum_k + through_k * g_k
            for k, through in enumerate((through_q, through_k)):
                line = jnp.sum(through, axis=0, keepdims=True)
                known = lines[2 * h + k]
                lines[2 * h + k] = line if known is None else known + line
        out.send(rows)
        total_q = jnp.sum(sum_q, axis=1, keepdims=True)
        total_k = jnp.sum(sum_k, axis=1, keepdims=True)
        sums[rows, :] = jnp.where(lanes((TOK, 128)) == 0, total_q, total_k)
    gain_grad[...] = jnp.broadcast_to(jnp.concatenate(lines, axis=1), (8, COLS))


def finish_kernel(ids, through, qkv, scales, sums, sums_other, normed, weights, tokens, gain_grad, last, grad_normed):
    total = sums[...] + other_rows(sums_other[...])
    lane = lanes((TOK, COLS)) % 256
    is_q, is_k = lane < 128, (lane >= 128) & (lane < 192)
    grads = []
    for j in range(PARTS):
        rows = slice(j * TOK, (j + 1) * TOK)
        scale = jnp.where(is_q, scales[rows, 0:1], jnp.where(is_k, scales[rows, 1:2], 1.0))
        mean = jnp.where(is_q, total[rows, 0:1] / 1024, jnp.where(is_k, total[rows, 1:2] / 512, 0.0))
        grads.append((scale * (through[rows, :] - qkv[rows, :] * scale * mean)).astype(BF))
    grad = jnp.concatenate(grads, axis=0)
    normed_grad = dot(grad, weights[:, :COLS], ((1,), (1,)))
    grad_normed[...] = normed_grad
    grad_normed.send()
    value = tokens[...].astype(F32)
    products = (normed_grad * (value * inverse_rms(value))).astype(BF)
    ones = jnp.where(lanes((ROWS, 128)) == 64, 1.0, 0.0).astype(BF)
    last[:, COLS:] = dot(products, ones, ((0,), (0,))).astype(BF)
    row = lax.broadcasted_iota(jnp.int32, (TOK, TOK), 0) % 8
    for h in range(PART_HEADS):
        query, key = [gain_grad[0:1, h * 256 + k : h * 256 + k + 128] for k in (0, 128)]
        block = jnp.where(row == 0, query, jnp.where(row == 1, key, 0.0))
        block = jnp.where(row == 2, pltpu.roll(query, HD, 1), block)
        at = pl.ds(pl.multiple_of(ids[0] * FEATURES + h * TOK, TOK), TOK)
        known = last[at, COLS:].astype(F32)
        last[at, COLS:] = jnp.where(lanes((TOK, TOK)) < HD, block, known).astype(BF)
    tile = D // SENDS
    for t in range(SENDS):
        rows = slice(t * tile, (t + 1) * tile)
        last[rows, :COLS] = dot(normed[:, rows], grad, ((0,), (0,))).astype(BF)
        last.send(rows)


def heads_in_kernel(received, out):
    for j in range(PARTS):
        for h in range(PART_HEADS):
            for qd in range(QUARTERS):
                block = received[(j * PART_HEADS + h) * QUARTERS + qd]
                columns = slice(h * 128, h * 128 + 128)
                out[j, qd * 16 : qd * 16 + 16, columns] = block[:16]
                out[j, 64 + qd * 16 : 80 + qd * 16, columns] = block[16:]


def heads_out_kernel(*refs):
    out = refs[-1]
    for j in range(PARTS):
        for h in range(PART_HEADS):
            for qd in range(QUARTERS):
                to = (j * PART_HEADS + h) * QUARTERS + qd
                columns = slice(h * 128, h * 128 + 128)
                out[to, :16] = refs[j][qd * 16 : qd * 16 + 16, columns]
                out[to, 16:] = refs[j][64 + qd * 16 : 80 + qd * 16, columns]


def finish_out_kernel(attended, branch, routed, logits, products, out):
    out[:, :512] = dot(attended[...], branch[...], ((0,), (0,))).astype(BF)
    ones = jnp.where(lanes((TOK, 128)) == 64, 1.0, 0.0).astype(BF)
    small = dot(routed[...], logits[...], ((0,), (0,))) + dot(products[...], ones, ((0,), (0,)))
    out[:, 512:] = small.astype(BF)


def pick(first, rows_out):
    i = lax.broadcasted_iota(jnp.int32, (128, 128), 1 if rows_out else 0)
    j = lax.broadcasted_iota(jnp.int32, (128, 128), 0 if rows_out else 1)
    return (i == j % HD + first).astype(BF)


def head_rows(block):
    low_half = lanes(block.shape) < HD
    zero = jnp.zeros_like(block)
    return jnp.concatenate([jnp.where(low_half, block, zero), jnp.where(low_half, zero, block)], 0)


def query_rows(block):
    low_half = lanes(block.shape) < HD
    block = block.astype(F32) * HD**-0.5
    return jnp.concatenate(
        [
            jnp.where(low_half, block, 0.0),
            jnp.where(low_half, pltpu.roll(block, HD, 1), 0.0),
        ],
        axis=0,
    ).astype(BF)


def key_segments(seg_key, columns):
    for src in range(N_CTX):
        line = jnp.broadcast_to(seg_key[src : src + 1, :], (TOK, TOK))
        columns[src * TOK : (src + 1) * TOK, :] = line.T


def forward_kernel(packed, seg_key, seg_query, mixed, mixed_low, lse, kv, kv_t, columns, limits):
    src = TOK_TILE // 32
    kv[...] = packed[:, 0:TOK, :].reshape(KEYS, 128)
    i = lax.broadcasted_iota(jnp.int32, (128, 128), 0)
    kv_t[...] = dot((i == lanes((128, 128))).astype(BF), kv[...], ((1,), (1,))).astype(BF)
    key_segments(seg_key, columns)
    limits[...] = jnp.ones_like(limits)

    def tile_rows(tile):
        q = packed[pl.ds(tile * src, src), TOK:PACK, :].reshape(TOK_TILE, 128)
        return query_rows(q), jnp.concatenate([seg_query[tile], seg_query[tile]], axis=1)

    def scores(rows, seg_q, keys):
        s = dot(kv[keys, :], rows, ((1,), (1,)))
        seg_k = jnp.concatenate([columns[keys, :]] * (2 * TOK_TILE // 128), axis=1)
        return jnp.where(seg_k == seg_q, s, -1e30)

    def sums(p):
        return jnp.sum(p.reshape(KEY_TILE // 8, 8, 2 * TOK_TILE), axis=0)

    def store(tile, accum, total, top):
        out = (accum / total).T
        out = jnp.where(
            lanes((TOK_TILE, 128)) < HD, pltpu.roll(out[:TOK_TILE], HD, 1), out[TOK_TILE:]
        )
        mixed[pl.ds(tile * TOK_TILE, TOK_TILE), :] = out
        mixed_low[pl.ds(tile * src, src)] = out.astype(BF).reshape(src, 32, 128)
        lse[tile] = top + jnp.log(total)

    for tile in range(TILES):
        rows, seg_q = tile_rows(tile)
        total = jnp.zeros((8, 2 * TOK_TILE), F32)
        accum = jnp.zeros((128, 2 * TOK_TILE), F32)
        for t in range(KEYS // KEY_TILE):
            keys = slice(t * KEY_TILE, (t + 1) * KEY_TILE)
            p = jnp.exp(scores(rows, seg_q, keys))
            total = total + sums(p)
            accum = accum + dot(kv_t[:, keys], p.astype(BF))
        total = jnp.sum(total, axis=0, keepdims=True)
        store(tile, accum, total, jnp.zeros_like(total))
        limits[...] = jnp.maximum(limits[...], jnp.maximum(total, 1.0 / total))

    @pl.when(jnp.logical_not(jnp.max(limits[...]) < 1e25))
    def _():
        @pl.loop(0, TILES)
        def _(tile):
            rows, seg_q = tile_rows(tile)
            top = jnp.full((1, 2 * TOK_TILE), -1e30, F32)
            total = jnp.zeros((8, 2 * TOK_TILE), F32)
            accum = jnp.zeros((128, 2 * TOK_TILE), F32)
            for t in range(KEYS // KEY_TILE):
                keys = slice(t * KEY_TILE, (t + 1) * KEY_TILE)
                s = scores(rows, seg_q, keys)
                newest = jnp.maximum(top, jnp.max(s, axis=0, keepdims=True))
                fade = jnp.exp(top - newest)
                p = jnp.exp(s - newest)
                p = jnp.where(s > -1e29, p, 0.0)
                top = newest
                total = total * fade + sums(p)
                accum = accum * fade + dot(kv_t[:, keys], p.astype(BF))
            store(tile, accum, jnp.sum(total, axis=0, keepdims=True), top)


def backward_kernel(packed, seg_key, seg_query, upper, mixed, lse, out, k2, k2t, v2, dk, dv, columns):
    @pl.when(pl.program_id(0) == 0)
    def _():
        kv = packed[:, 0:TOK, :].reshape(KEYS, 128)
        k2[...] = dot(kv, pick(0, False)).astype(BF)
        k2t[...] = dot(pick(0, True), kv, ((1,), (1,))).astype(BF)
        v2[...] = dot(kv, pick(HD, False)).astype(BF)
        dk[...] = jnp.zeros_like(dk)
        dv[...] = jnp.zeros_like(dv)
        key_segments(seg_key, columns)

    tile = pl.program_id(0)
    src = TOK_TILE // 32
    q = packed[pl.ds(tile * src, src), TOK:PACK, :].reshape(TOK_TILE, 128)
    rows = head_rows(q * BF(HD**-0.5))
    upper_now = upper[...].reshape(TOK_TILE, 128)
    up = head_rows(upper_now)
    along = (upper_now.astype(F32) * mixed[...]).T
    delta = jnp.concatenate(
        [
            jnp.sum(along[:HD], axis=0, keepdims=True),
            jnp.sum(along[HD:], axis=0, keepdims=True),
        ],
        axis=1,
    )
    seg_q = jnp.concatenate([seg_query[tile], seg_query[tile]], axis=1)
    dq = jnp.zeros((128, 2 * TOK_TILE), F32)
    for t in range(KEYS // KEY_TILE):
        at = t * KEY_TILE
        keys = slice(at, at + KEY_TILE)
        s = dot(k2[keys, :], rows, ((1,), (1,)))
        seg_k = jnp.concatenate([columns[keys, :]] * (2 * TOK_TILE // 128), axis=1)
        p = jnp.where(seg_k == seg_q, jnp.exp(s - lse[0]), 0.0)
        dp = dot(v2[keys, :], up, ((1,), (1,)))
        ds = (p * (dp - delta)).astype(BF)
        dv[keys, :] += dot(p.astype(BF), up)
        dk[keys, :] += dot(ds, rows)
        dq = dq + dot(k2t[:, keys], ds)
    dq = (dq * HD**-0.5).T
    dq = jnp.where(lanes((TOK_TILE, 128)) < HD, dq[:TOK_TILE], dq[TOK_TILE:])
    out[pl.ds(tile * src, src), TOK:PACK, :] = dq.astype(BF).reshape(src, 32, 128)

    @pl.when(tile == pl.num_programs(0) - 1)
    def _():
        for t in range(KEYS // KEY_TILE):
            keys = slice(t * KEY_TILE, (t + 1) * KEY_TILE)
            low_half = lanes((KEY_TILE, 128)) < HD
            both_k = dk[keys, :] + pltpu.roll(dk[keys, :], HD, 1)
            both_v = dv[keys, :] + pltpu.roll(dv[keys, :], HD, 1)
            both = jnp.where(low_half, both_k, both_v).astype(BF).reshape(-1, TOK, 128)
            out[t * KEY_TILE // TOK : (t + 1) * KEY_TILE // TOK, 0:TOK, :] = both


def whole(shape):
    return pl.BlockSpec(shape, lambda i: (0,) * len(shape))


def attend(packed, seg_key, seg_query):
    vmem = pl.BlockSpec(memory_space=pltpu.VMEM)
    return pl.pallas_call(
        forward_kernel,
        in_specs=[vmem] * 3,
        out_specs=[vmem, pl.BlockSpec(), vmem],
        out_shape=[
            jax.ShapeDtypeStruct((QUERIES, 128), F32),
            jax.ShapeDtypeStruct((N_CTX, 32, 128), BF),
            jax.ShapeDtypeStruct((TILES, 1, 2 * TOK_TILE), F32),
        ],
        scratch_shapes=[
            pltpu.VMEM((KEYS, 128), BF),
            pltpu.VMEM((128, KEYS), BF),
            pltpu.VMEM((KEYS, 128), jnp.int32),
            pltpu.VMEM((1, 2 * TOK_TILE), F32),
        ],
        compiler_params=pltpu.CompilerParams(vmem_limit_bytes=24 << 20),
        cost_estimate=estimate(12),
        name="attend",
    )(packed, seg_key, seg_query)


def attend_back(packed, seg_key, seg_query, upper, mixed, lse):
    src = TOK_TILE // 32
    return pl.pallas_call(
        backward_kernel,
        grid=(TILES,),
        in_specs=[
            whole((N_CTX, PACK, 128)),
            whole((N_CTX, TOK)),
            whole((TILES, 1, TOK_TILE)),
            pl.BlockSpec((src, 32, 128), lambda i: (i, 0, 0)),
            pl.BlockSpec((TOK_TILE, 128), lambda i: (i, 0)),
            pl.BlockSpec((1, 1, 2 * TOK_TILE), lambda i: (i, 0, 0)),
        ],
        out_specs=whole((N_CTX, PACK, 128)),
        out_shape=jax.ShapeDtypeStruct((N_CTX, PACK, 128), BF),
        scratch_shapes=[
            pltpu.VMEM((KEYS, 128), BF),
            pltpu.VMEM((128, KEYS), BF),
            pltpu.VMEM((KEYS, 128), BF),
            pltpu.VMEM((KEYS, 128), F32),
            pltpu.VMEM((KEYS, 128), F32),
            pltpu.VMEM((KEYS, 128), jnp.int32),
        ],
        compiler_params=pltpu.CompilerParams(vmem_limit_bytes=32 << 20),
        cost_estimate=estimate(25),
        name="attend_back",
    )(packed, seg_key, seg_query, upper, mixed, lse)


def in_order(pieces, fsdp):
    pieces = jnp.stack(pieces)
    return jnp.concatenate(
        [lax.dynamic_index_in_dim(pieces, fsdp ^ p, keepdims=False) for p in range(4)], axis=0
    )


def inverse_rms(value):
    return lax.rsqrt(jnp.mean(value * value, axis=-1, keepdims=True) + EPSILON)


def after(value, *others):
    return lax.optimization_barrier((value, *others))[0]


def shards(
    hidden_in,
    segment_ids,
    block_order,
    expert_ids,
    pair_order,
    attn_norm,
    w_query,
    w_key,
    w_value,
    query_norm,
    key_norm,
    w_out,
    ffn_norm,
    w_router,
    w_gate,
    w_up,
    w_down,
    cotangent,
):
    place = lax.axis_index("ctx")
    fsdp = lax.axis_index("fsdp")
    core = fsdp % 2
    part = fsdp % PARTS
    both_axes = ("ctx", "fsdp")

    small_lines = [line[None] for line in (attn_norm, query_norm, ffn_norm, key_norm)]
    outgoing_w = call(
        weights_kernel,
        (w_query, w_key, w_value, w_router, *small_lines, segment_ids),
        [((4 * N_CTX, 8, COLS + 128), BF)],
        "weights",
    )[0]
    out_rows, outgoing_w = lax.optimization_barrier(
        ([swap(w_out, j) for j in range(4)], outgoing_w)
    )
    gathered = exchange(outgoing_w, both_axes)
    part_ids = jnp.stack([part ^ j for j in range(PARTS)]).astype(jnp.int32)

    tokens = hidden_in[0]
    order = block_order[0]
    blocks = lax.dynamic_slice_in_dim(order, place * 2, 2)
    tokens_all = [tokens, swap(tokens, 1)]
    blocks_all = [blocks, swap(blocks, 1)]
    tokens_all = jnp.concatenate(tokens_all, axis=0)

    proj_out = lax.all_gather(in_order(out_rows, fsdp), "ctx", axis=0, tiled=True)

    ids = expert_ids[0]
    experts = jnp.arange(EXPERTS, dtype=jnp.int32)
    named = ids.T[None, :, :] == experts[:, None, None]
    chosen = jnp.any(named, axis=1)
    ranks = pair_order[0, 0].reshape(TOK, TOPK).T
    rank = jnp.sum(jnp.where(named, ranks[None], 0), axis=1)
    earlier = chosen[:, :, None] & (rank[:, :, None] < rank[:, None, :])
    slot = jnp.sum(earlier.astype(jnp.int32), axis=1)
    kept = chosen & (slot < CAP)
    slot = jnp.where(kept, slot, -1)
    places = slot[:, None, :] == jnp.arange(CAP, dtype=jnp.int32)[None, :, None]
    one_hot = places.astype(BF).reshape(EXPERTS * CAP, TOK)

    lay = jnp.arange(TOK, dtype=jnp.int32)
    half = TOK // 2
    positions = (jnp.repeat(jnp.stack(blocks_all), half, axis=1) * half + lay % half).reshape(ROWS)
    freq = THETA ** (-jnp.arange(0, HD, 2).astype(F32) / HD)
    turned = positions.astype(F32)[:, None] * freq[None, :]
    cosine = jnp.tile(jnp.cos(turned), (1, 4))
    sine = jnp.sin(turned)
    sine = jnp.concatenate([-sine, sine, -sine, sine], axis=1)

    inputs_all = tokens_all.astype(F32)
    scale_in = inverse_rms(inputs_all)
    scaled_in = inputs_all * scale_in
    small = gathered[:, :, COLS:]
    lines = small[:, 0, 32:60].astype(F32)
    gain_attn = lines[:, 0:8].reshape(1, D)
    gain_query = lines[:, 8:16].reshape(D)
    gain_ffn = lines[:, 16:24].reshape(1, D)
    gain_key = lines[:, 24:28].reshape(512)
    gain_heads = jnp.concatenate(
        [
            lax.dynamic_slice_in_dim(gain_query, part * FEATURES, FEATURES).reshape(PART_HEADS, 128),
            lax.dynamic_slice_in_dim(gain_key, part * FEATURES // 2, FEATURES // 2).reshape(
                PART_HEADS, HD
            ),
            jnp.ones((PART_HEADS, HD), F32),
        ],
        axis=1,
    ).reshape(1, COLS)
    weights = gathered.reshape(D, COLS + 128)
    proj = weights[:, :COLS]
    proj_router = small[:, :, :EXPERTS].reshape(D, EXPERTS)

    normed_low = (scaled_in * gain_attn).astype(BF)
    qkv = dot(normed_low, proj)
    lane = jnp.arange(COLS)[None] % 256
    is_q, is_k = lane < 128, (lane >= 128) & (lane < 192)
    squares = qkv * qkv
    square_sums = jnp.stack(
        [
            jnp.sum(jnp.where(is_q, squares, 0.0), axis=1),
            jnp.sum(jnp.where(is_k, squares, 0.0), axis=1),
        ]
    )
    square_sums = sum_parts(square_sums.reshape(2, PARTS, TOK)).reshape(2, ROWS)
    scale_q = lax.rsqrt(square_sums[0] / 1024 + EPSILON)[:, None]
    scale_k = lax.rsqrt(square_sums[1] / 512 + EPSILON)[:, None]
    packed = call_near(
        pack_kernel,
        (qkv, scale_q, scale_k, gain_heads, cosine, sine),
        [((N_CTX, PACK, 128), BF, True)],
        "pack",
    )[0]
    packed = exchange(packed, "ctx")
    scales = jnp.where(jnp.arange(128)[None] == 0, scale_q, scale_k)
    gains = jnp.broadcast_to(gain_heads, (8, COLS))

    sequence = fsdp ^ (place // (N_CTX // PARTS))
    seg_small = lax.dynamic_index_in_dim(
        small.reshape(N_CTX, 4, 8, 128), sequence, axis=1, keepdims=False
    )[:, 1:5, 32:96].astype(jnp.int32)
    seg_all = (seg_small[:, 0:2] + 256 * seg_small[:, 2:4]).reshape(N_CTX, TOK)
    seg_query = lax.dynamic_index_in_dim(
        seg_all.reshape(N_CTX, 2, QUARTERS, 16), place % QUARTERS, axis=2, keepdims=False
    ).reshape(TILES, 1, TOK_TILE)

    packed, shard_gate, shard_up, shard_down = lax.optimization_barrier(
        (packed, w_gate[0], w_up[0], w_down[0])
    )
    shards_far = [swap(shard, 2) for shard in (shard_gate, shard_up, shard_down)]
    gate_w, up_w, down_w = [
        in_order([own, swap(own, 1), far, swap(far, 1)], fsdp)
        for own, far in zip((shard_gate, shard_up, shard_down), shards_far)
    ]

    mixed, mixed_low, lse = attend(packed, seg_all, seg_query)
    returned = exchange(mixed_low, "ctx")
    returned = call_near(heads_in_kernel, (returned,), [((PARTS, TOK, FEATURES), BF, False)], "heads_in", 1)[0]
    pieces = swapped([returned[j] for j in range(PARTS)])
    out_parts = proj_out.reshape(PARTS, FEATURES, D)
    out_parts = [
        lax.dynamic_index_in_dim(out_parts, part ^ j, keepdims=False) for j in range(PARTS)
    ]
    inputs = tokens.astype(F32)
    middle = inputs
    for piece, out_part in zip(pieces, out_parts):
        middle = middle + dot(piece, out_part)
    scale_mid = inverse_rms(middle)
    scaled_mid = middle * scale_mid
    routed_in = (scaled_mid * gain_ffn).astype(BF)
    logits = dot(proj_router, routed_in, ((0,), (1,)))
    logits = jnp.where(chosen, logits, -1e30)
    raised = jnp.where(chosen, jnp.exp(logits - jnp.max(logits, axis=0, keepdims=True)), 0.0)
    gates = raised / jnp.sum(raised, axis=0, keepdims=True)

    upstream_low = cotangent[0]
    upstream = upstream_low.astype(F32)
    rows_out = dot(one_hot, routed_in).astype(BF).reshape(EXPERTS, CAP, D)
    arrived = exchange(rows_out, "ctx").reshape(N_CTX * CAP, D)
    share = jnp.where(places, gates[:, None, :], 0.0)
    row_share = jnp.sum(share, axis=2).reshape(EXPERTS * CAP, 1)
    grads_out = (dot(one_hot, upstream_low) * row_share).astype(BF).reshape(EXPERTS, CAP, D)
    arrived, grads_out, gate_w, up_w, down_w = lax.optimization_barrier(
        (arrived, grads_out, gate_w, up_w, down_w)
    )
    arrived_grad = exchange(grads_out, "ctx").reshape(N_CTX * CAP, D)

    gate_act = dot(arrived, gate_w)
    up_act = dot(arrived, up_w)
    sigma = jax.nn.sigmoid(gate_act)
    silu_gate = gate_act * sigma
    inner = (silu_gate * up_act).astype(BF)
    produced = dot(inner, down_w).astype(BF).reshape(N_CTX, CAP, D)
    produced, arrived_grad = lax.optimization_barrier((produced, arrived_grad))
    produced_home = exchange(produced, "ctx").reshape(EXPERTS * CAP, D)

    grad_inner = dot(arrived_grad, down_w, ((1,), (1,)))
    grad_gate_act = (grad_inner * up_act * sigma * (1.0 + gate_act * (1.0 - sigma))).astype(BF)
    grad_up_act = (grad_inner * silu_gate).astype(BF)
    grad_rows = dot(grad_gate_act, gate_w, ((1,), (1,))) + dot(grad_up_act, up_w, ((1,), (1,)))
    grad_rows = grad_rows.astype(BF).reshape(N_CTX, CAP, D)
    produced_home, grad_rows = lax.optimization_barrier((produced_home, grad_rows))
    grad_home = exchange(grad_rows, "ctx").reshape(EXPERTS * CAP, D)

    grad_gate_w = dot(arrived, grad_gate_act, ((0,), (0,))).astype(BF)
    grad_up_w = dot(arrived, grad_up_act, ((0,), (0,))).astype(BF)
    grad_down_w = dot(inner, arrived_grad, ((0,), (0,))).astype(BF)
    grad_gate_up = jnp.stack([grad_gate_w, grad_up_w])
    grad_home, grad_down_w, grad_gate_up = lax.optimization_barrier(
        (grad_home, grad_down_w, grad_gate_up)
    )
    grad_down = lax.psum_scatter(
        grad_down_w[None], "fsdp", scatter_dimension=1, tiled=True
    ).astype(F32)

    share = share.reshape(EXPERTS * CAP, TOK)
    share_high = share.astype(BF)
    share_low = (share - share_high.astype(F32)).astype(BF)
    combined = dot(share_high, produced_home, ((0,), (0,)))
    combined = combined + dot(share_low, produced_home, ((0,), (0,)))
    layer_out = (middle + combined).astype(BF)[None]
    along = dot(produced_home, upstream_low, ((1,), (1,))).reshape(EXPERTS, CAP, TOK)
    grad_gates = jnp.sum(jnp.where(places, along, 0.0), axis=1)
    grad_chosen = gates * (grad_gates - jnp.sum(gates * grad_gates, axis=0, keepdims=True))
    grad_logits = grad_chosen.astype(BF)
    grad_routed = dot(grad_logits, proj_router, ((0,), (1,)))
    grad_routed = grad_routed + dot(one_hot, grad_home, ((0,), (0,)))
    through = grad_routed * gain_ffn
    grad_middle = upstream + scale_mid * (
        through - scaled_mid * jnp.mean(through * scaled_mid, axis=1, keepdims=True)
    )
    grad_branch = grad_middle.astype(BF)
    grad_mixed = [dot(grad_branch, out_part, ((1,), (1,))).astype(BF) for out_part in out_parts]
    upper = call_near(
        heads_out_kernel, tuple(swapped(grad_mixed)), [((N_CTX, 32, 128), BF, True)], "heads_out", 1
    )[0]
    upper = exchange(upper, "ctx")

    sorted_pieces = jnp.stack(pieces)
    attended = jnp.concatenate(
        [
            lax.dynamic_index_in_dim(sorted_pieces, part ^ p, keepdims=False)
            for p in range(PARTS)
        ],
        axis=1,
    )
    attended_2 = jnp.concatenate([attended, swap(attended, 1)], axis=0)
    branch_halves = jnp.stack([grad_branch[:, :512], grad_branch[:, 512:]])
    own_half = lax.dynamic_index_in_dim(branch_halves, core, keepdims=False)
    other_half = lax.dynamic_index_in_dim(branch_halves, 1 - core, keepdims=False)
    branch_2 = jnp.concatenate([own_half, swap(other_half, 1)], axis=0)
    late = call_near(
        finish_out_kernel,
        (
            attended_2,
            branch_2,
            routed_in,
            jnp.pad(grad_logits.T, ((0, 0), (0, 128 - EXPERTS))),
            (grad_routed * scaled_mid).astype(BF),
        ),
        [((D, 640), BF, True)],
        "finish_out",
    )[0]
    late, upper = lax.optimization_barrier((late, upper))
    first_sums = exchange(late.reshape(4 * N_CTX, 8, 640), both_axes)

    grads_home = attend_back(packed, seg_all, seg_query, upper, mixed, lse)
    grads_home, first_sums, grad_gate_up = lax.optimization_barrier(
        (grads_home, first_sums, grad_gate_up)
    )
    grad_gate_up = lax.psum_scatter(
        grad_gate_up, "fsdp", scatter_dimension=1, tiled=True
    ).astype(F32)
    grads_home = exchange(grads_home, "ctx")

    through_heads, sums, gain_grad = call(
        unpack_kernel,
        (grads_home, qkv, scales, gains, cosine, sine),
        [((ROWS, COLS), F32), ((ROWS, 128), F32), ((8, COLS), F32)],
        "unpack",
    )
    last, grad_normed = call(
        finish_kernel,
        (
            through_heads,
            qkv,
            scales,
            sums,
            swap(sums, 1),
            normed_low,
            weights,
            tokens_all,
            gain_grad,
        ),
        [((D, COLS + 128), BF), ((ROWS, D), F32)],
        "finish",
        4,
        part_ids,
    )
    last_sums = exchange(last.reshape(4 * N_CTX, 8, COLS + 128), both_axes)

    grad_normed = grad_normed.reshape(PARTS, TOK, D)
    grad_normed = sum(swapped([grad_normed[j] for j in range(PARTS)]))
    through_in = grad_normed * gain_attn
    scaled_own = scaled_in[:TOK]
    input_grad = grad_middle + scale_in[:TOK] * (
        through_in - scaled_own * jnp.mean(through_in * scaled_own, axis=1, keepdims=True)
    )

    first_sums = jnp.sum(first_sums.reshape(2 * N_CTX, 2, 8, 640).astype(F32), axis=0)
    grad_out = jnp.concatenate([first_sums[0, :, :512], first_sums[1, :, :512]], axis=1)
    first_small = first_sums[0, :, 512:] + first_sums[1, :, 512:]
    last_sums = jnp.sum(
        last_sums.reshape(4 * N_CTX // PARTS, PARTS, 8, COLS + 128).astype(F32), axis=0
    )
    heads_g = last_sums[:, :, :COLS].reshape(PARTS, 8, PART_HEADS, 256)
    heads_g = jnp.transpose(heads_g, (1, 0, 2, 3))
    last_small = jnp.sum(last_sums[:, :, COLS:], axis=0)
    index = 4 * place + fsdp
    query_gain = lax.dynamic_slice(
        last_small, (index % 16 // 8 * 2, index % 8 * 8), (1, 8)
    ).reshape(8)
    key_gain = lax.dynamic_slice(last_small, (1, index % 16 * 4), (1, 4)).reshape(4)
    return (
        layer_out,
        input_grad[None],
        last_small[:, 64],
        heads_g[..., :128].reshape(8, 1024),
        heads_g[..., 128:192].reshape(8, 512),
        heads_g[..., 192:].reshape(8, 512),
        query_gain,
        key_gain,
        grad_out,
        first_small[:, 64],
        first_small[:, :EXPERTS],
        grad_gate_up[0][None],
        grad_gate_up[1][None],
        grad_down,
    )


def solution(mesh):
    row = P("fsdp", "ctx", None)
    flat = P(("ctx", "fsdp"))
    dense = P(("ctx", "fsdp"), None)
    expert = P("ctx", "fsdp", None)
    in_specs = (
        row,
        P("fsdp", "ctx"),
        P("fsdp", None),
        row,
        row,
        flat,
        dense,
        dense,
        dense,
        flat,
        flat,
        dense,
        flat,
        dense,
        expert,
        expert,
        expert,
        row,
    )
    out_specs = (
        row,
        row,
        flat,
        dense,
        dense,
        dense,
        flat,
        flat,
        dense,
        flat,
        dense,
        expert,
        expert,
        expert,
    )
    return jax.shard_map(shards, mesh=mesh, in_specs=in_specs, out_specs=out_specs, check_vma=False)
```

```python
import jax
import jax.numpy as jnp
from jax import lax
from jax.experimental import pallas as pl
from jax.experimental.pallas import tpu as pltpu
from jax.sharding import PartitionSpec as P

D = 1024
HEADS = 16
KVH = 8
HD = 64
EXPERTS = 32
TOPK = 8
TOK = 128
CAP = 32
N_CTX = 32
EPSILON = 1e-05
THETA = 10000.0
BF = jnp.bfloat16
F32 = jnp.float32

PARTS = 2
PART_HEADS = KVH // PARTS
COLS = PART_HEADS * 256
FEATURES = PART_HEADS * 128
ROWS = PARTS * TOK
QUARTERS = 4
PACK = TOK + TOK // QUARTERS
KEYS = N_CTX * TOK
QUERIES = KEYS // QUARTERS
KEY_TILE = 512
VMEM_LIMIT = 62 << 20
TOK_TILE = 128
TILES = QUERIES // TOK_TILE


def dot(a, b, dims=((1,), (0,))):
    return lax.dot_general(a, b, (dims, ((), ())), preferred_element_type=F32)


def swap(array, j):
    return lax.ppermute(array, "fsdp", [(i, i ^ j) for i in range(4)]) if j else array


def swapped(pieces):
    return [swap(piece, j) for j, piece in enumerate(pieces)]


def sum_parts(value):
    step = 1
    while step < PARTS:
        value = value + swap(jnp.stack([value[:, j ^ step] for j in range(PARTS)], 1), step)
        step *= 2
    return value


def exchange(array, axis):
    return lax.all_to_all(array, axis, split_axis=0, concat_axis=0, tiled=True)


def lanes(shape):
    return lax.broadcasted_iota(jnp.int32, shape, len(shape) - 1)


def swap_halves(value):
    first = lanes(value.shape) % HD < HD // 2
    up = pltpu.roll(value, value.shape[1] - HD // 2, 1)
    down = pltpu.roll(value, HD // 2, 1)
    return jnp.where(first, up, down)


def call_near(kernel, inputs, outputs, name, micros=2, mib=12):
    vmem = pl.BlockSpec(memory_space=pltpu.VMEM)
    return pl.pallas_call(
        kernel,
        in_specs=[vmem] * len(inputs),
        out_specs=[pl.BlockSpec() if sent else vmem for _, _, sent in outputs],
        out_shape=[jax.ShapeDtypeStruct(shape, dtype) for shape, dtype, _ in outputs],
        compiler_params=pltpu.CompilerParams(vmem_limit_bytes=mib << 20),
        cost_estimate=estimate(micros),
        name=name,
    )(*inputs)


class Held:
    def __init__(self, buffer, copy):
        self.buffer, self.copy = buffer, copy

    def wait(self):
        if self.copy is not None:
            self.copy.wait()
            self.copy = None

    def __getitem__(self, index):
        self.wait()
        return self.buffer[index]


class Made:
    def __init__(self, buffer, target, columns, sems, first):
        self.buffer, self.target, self.columns = buffer, target, columns
        self.sems, self.first = sems, first
        self.copies = []

    def __getitem__(self, index):
        return self.buffer[index]

    def __setitem__(self, index, value):
        self.buffer[index] = value

    def send(self, rows=None):
        source, target = self.buffer, self.target
        if rows is not None:
            source = source.at[rows]
        if self.columns is not None:
            target = target.at[slice(None) if rows is None else rows, self.columns]
        elif rows is not None:
            target = target.at[rows]
        copy = pltpu.make_async_copy(source, target, self.sems.at[self.first + len(self.copies)])
        copy.start()
        self.copies.append(copy)


SENDS = 4


def far(array, rows=None, at=None, cut=None):
    return (array, rows, at, cut)


def call(kernel, inputs, outputs, name, micros=2, ids=None):
    made = []
    for k, (shape, dtype, *cuts) in enumerate(outputs):
        for columns in cuts[0] if cuts else (None,):
            wide = shape if columns is None else (shape[0], columns.stop - columns.start)
            made.append((k, wide, dtype, columns))
    hbm = pl.BlockSpec(memory_space=pltpu.HBM)
    inputs = [i if isinstance(i, tuple) else far(i) for i in inputs]
    scratch = []
    for array, rows, _, part in inputs:
        shape = array.shape if rows is None else (rows, *array.shape[1:])
        if part is not None:
            shape = tuple(p.stop - p.start for p in part) + array.shape[len(part) :]
        scratch.append(pltpu.VMEM(shape, array.dtype))
    scratch += [pltpu.VMEM(shape, dtype) for _, shape, dtype, _ in made]
    scratch.append(pltpu.SemaphoreType.DMA((len(inputs) + SENDS * len(made),)))
    numbers = [] if ids is None else [ids]

    def body(*refs):
        refs = list(refs)
        own_ids = refs.pop(0) if numbers else None
        ins, outs = refs[: len(inputs)], refs[len(inputs) : len(inputs) + len(outputs)]
        buffers = refs[len(inputs) + len(outputs) :]
        sems = buffers[-1]
        given, results = [], []
        for k, (ref, (_, rows, at, part)) in enumerate(zip(ins, inputs)):
            if rows is not None:
                ref = ref.at[pl.ds(pl.multiple_of(own_ids[at] * rows, rows), rows)]
            elif part is not None:
                ref = ref.at[part]
            copy = pltpu.make_async_copy(ref, buffers[k], sems.at[k])
            copy.start()
            given.append(Held(buffers[k], copy))
        for k, (number, _, _, columns) in enumerate(made):
            ref = outs[number]
            results.append(
                Made(buffers[len(inputs) + k], ref, columns, sems, len(inputs) + SENDS * k)
            )
        kernel(*([own_ids] if numbers else []), *given, *results)
        for held in given:
            held.wait()
        for result in results:
            if not result.copies:
                result.send()
        for result in results:
            for copy in result.copies:
                copy.wait()

    return pl.pallas_call(
        body,
        in_specs=[pl.BlockSpec(memory_space=pltpu.SMEM)] * len(numbers) + [hbm] * len(inputs),
        out_specs=[hbm] * len(outputs),
        out_shape=[jax.ShapeDtypeStruct(shape, dtype) for shape, dtype, *_ in outputs],
        scratch_shapes=scratch,
        compiler_params=pltpu.CompilerParams(vmem_limit_bytes=VMEM_LIMIT),
        cost_estimate=estimate(micros),
        name=name,
    )(*numbers, *[i[0] for i in inputs])


def estimate(micros):
    return pl.CostEstimate(flops=int(micros * 1.1e9), bytes_accessed=1 << 16, transcendentals=0)


def weights_kernel(w_query, w_key, w_value, w_router, attn, query, ffn, key, segments, out):
    row = lax.broadcasted_iota(jnp.int32, (8, 128), 0)
    lane = lanes((8, 128))
    middle = (lane >= 32) & (lane < 96)
    gains = [line[...].astype(F32) for line in (attn, query, ffn, key)]
    gains = jnp.concatenate(gains + [jnp.zeros((1, 100), F32)], axis=1)
    seg = segments[...]
    low, high = (seg & 255).astype(F32), (seg >> 8).astype(F32)
    small = jnp.zeros((8, 128), F32)
    lines = (
        pltpu.roll(low, 32, 1),
        pltpu.roll(low, 96, 1),
        pltpu.roll(high, 32, 1),
        pltpu.roll(high, 96, 1),
    )
    for r, line in enumerate(lines):
        small = jnp.where((row == r + 1) & middle, line, small)
    small = jnp.where((row == 0) & (lane >= 32), pltpu.roll(gains, 32, 1), small)
    router = jnp.concatenate([w_router[...].astype(F32), jnp.zeros((8, 96), F32)], axis=1)
    small = jnp.where(lane < 32, router, small)
    parts = []
    for p in range(PARTS):
        columns = []
        for h in range(PART_HEADS):
            at = p * PART_HEADS + h
            columns.append(w_query[:, at * 128 : at * 128 + 128].astype(F32))
            columns.append(w_key[:, at * HD : at * HD + HD].astype(F32))
            columns.append(w_value[:, at * HD : at * HD + HD].astype(F32))
        parts.append(jnp.concatenate(columns + [small], axis=1).astype(BF))
    for to in range(4 * N_CTX):
        out[to] = parts[to % PARTS]


def pack_kernel(qkv, scale_q, scale_k, gain, cosine, sine, out):
    for j in range(PARTS):
        rows = slice(j * TOK, (j + 1) * TOK)
        turn_c, turn_s = cosine[rows], sine[rows]
        cq, ck = scale_q[rows], scale_k[rows]
        for h in range(PART_HEADS):
            at = h * 256
            q = qkv[rows, at : at + 128] * cq * gain[:, at : at + 128]
            q = (q * turn_c + swap_halves(q) * turn_s).astype(BF)
            kv = qkv[rows, at + 128 : at + 256]
            k = kv * ck * gain[:, at + 128 : at + 256]
            k = k * turn_c + swap_halves(k) * turn_s
            kv = jnp.where(lanes(kv.shape) < HD, k, kv).astype(BF)
            for qd in range(QUARTERS):
                to = (j * PART_HEADS + h) * QUARTERS + qd
                out[to, 0:TOK, :] = kv
                out[to, TOK : TOK + 16, :] = q[qd * 16 : qd * 16 + 16]
                out[to, TOK + 16 : TOK + 32, :] = q[64 + qd * 16 : 64 + qd * 16 + 16]


def other_rows(value):
    return jnp.concatenate([value[TOK:], value[:TOK]], axis=0)


def unpack_kernel(grads, qkv, scales, gain, cosine, sine, out, sums, gain_grad):
    lines = [None] * (2 * PART_HEADS)
    for j in range(PARTS):
        rows = slice(j * TOK, (j + 1) * TOK)
        turn_c, turn_s = cosine[rows, :], sine[rows, :]
        cq, ck = scales[rows, 0:1], scales[rows, 1:2]
        sum_q = jnp.zeros((TOK, 128), F32)
        sum_k = jnp.zeros((TOK, 128), F32)
        for h in range(PART_HEADS):
            at = h * 256
            base = (j * PART_HEADS + h) * QUARTERS
            pieces = [
                grads[base + qd, TOK + 16 * half : TOK + 16 * half + 16, :]
                for half in range(2)
                for qd in range(QUARTERS)
            ]
            dq = jnp.concatenate(pieces, axis=0).astype(F32)
            dq = dq * turn_c - swap_halves(dq) * turn_s
            dkv = sum(grads[base + qd, 0:TOK, :].astype(F32) for qd in range(QUARTERS))
            dk = dkv * turn_c - swap_halves(dkv) * turn_s
            is_k = lanes(dkv.shape) < HD
            dkv = jnp.where(is_k, dk, dkv)
            a_q = qkv[rows, at : at + 128] * cq
            a_k = qkv[rows, at + 128 : at + 256] * ck
            through_q = dq * a_q
            through_k = jnp.where(is_k, dkv * a_k, 0.0)
            g_q = gain[:, at : at + 128]
            g_k = gain[:, at + 128 : at + 256]
            out[rows, at : at + 128] = dq * g_q
            out[rows, at + 128 : at + 256] = dkv * g_k
            sum_q = sum_q + through_q * g_q
            sum_k = sum_k + through_k * g_k
            for k, through in enumerate((through_q, through_k)):
                line = jnp.sum(through, axis=0, keepdims=True)
                known = lines[2 * h + k]
                lines[2 * h + k] = line if known is None else known + line
        out.send(rows)
        total_q = jnp.sum(sum_q, axis=1, keepdims=True)
        total_k = jnp.sum(sum_k, axis=1, keepdims=True)
        sums[rows, :] = jnp.where(lanes((TOK, 128)) == 0, total_q, total_k)
    gain_grad[...] = jnp.broadcast_to(jnp.concatenate(lines, axis=1), (8, COLS))


def finish_kernel(ids, through, qkv, scales, sums, sums_other, normed, weights, tokens, tokens_other, gain_grad, last, last_small, grad_normed):
    total = sums[...] + other_rows(sums_other[...])
    lane = lanes((TOK, COLS)) % 256
    is_q, is_k = lane < 128, (lane >= 128) & (lane < 192)
    grads = []
    for j in range(PARTS):
        rows = slice(j * TOK, (j + 1) * TOK)
        scale = jnp.where(is_q, scales[rows, 0:1], jnp.where(is_k, scales[rows, 1:2], 1.0))
        mean = jnp.where(is_q, total[rows, 0:1] / 1024, jnp.where(is_k, total[rows, 1:2] / 512, 0.0))
        grads.append((scale * (through[rows, :] - qkv[rows, :] * scale * mean)).astype(BF))
    grad = jnp.concatenate(grads, axis=0)
    tile = D // SENDS
    for t in range(SENDS):
        rows = slice(t * tile, (t + 1) * tile)
        last[rows, :] = dot(normed[:, rows], grad, ((0,), (0,))).astype(BF)
        last.send(rows)
    normed_grad = dot(grad, weights[...], ((1,), (1,)))
    grad_normed[...] = normed_grad
    grad_normed.send()
    value = jnp.concatenate([tokens[...], tokens_other[...]], axis=0).astype(F32)
    products = (normed_grad * (value * inverse_rms(value))).astype(BF)
    ones = jnp.where(lanes((ROWS, 128)) == 64, 1.0, 0.0).astype(BF)
    last_small[...] = dot(products, ones, ((0,), (0,))).astype(BF)
    row = lax.broadcasted_iota(jnp.int32, (TOK, TOK), 0) % 8
    for h in range(PART_HEADS):
        query, key = [gain_grad[0:1, h * 256 + k : h * 256 + k + 128] for k in (0, 128)]
        block = jnp.where(row == 0, query, jnp.where(row == 1, key, 0.0))
        block = jnp.where(row == 2, pltpu.roll(query, HD, 1), block)
        at = pl.ds(pl.multiple_of(ids[0] * FEATURES + h * TOK, TOK), TOK)
        known = last_small[at, :].astype(F32)
        last_small[at, :] = jnp.where(lanes((TOK, TOK)) < HD, block, known).astype(BF)


def final_kernel(ids, parts, query, key, value, attn_gain, query_gain, key_gain):
    def column(t):
        piece = parts[:, :, t * 128 : t * 128 + 128].astype(F32)
        return jnp.sum(piece.reshape(4 * N_CTX // PARTS, PARTS, 8, 128), axis=0)

    low_half = lanes((8, 128)) < HD
    for h in range(0, PART_HEADS, 2):
        first, second = column(2 * h), column(2 * h + 2)
        kv_first, kv_second = column(2 * h + 1), column(2 * h + 3)
        for p in range(PARTS):
            at = (p * PART_HEADS + h) * 128
            query[:, at : at + 128] = first[p]
            query[:, at + 128 : at + 256] = second[p]
            at = at // 2
            key[:, at : at + 128] = jnp.where(low_half, kv_first[p], pltpu.roll(kv_second[p], HD, 1))
            value[:, at : at + 128] = jnp.where(
                low_half, pltpu.roll(kv_first[p], HD, 1), kv_second[p]
            )
    small = jnp.sum(column(2 * PART_HEADS), axis=0)
    row = lax.broadcasted_iota(jnp.int32, (8, 128), 0)
    lane = lanes((8, 128))
    attn = jnp.sum(jnp.where(lane == 64, small, 0.0), axis=1, keepdims=True)
    attn_gain[...] = jnp.sum(jnp.where(row == lane, attn, 0.0), axis=0, keepdims=True)[:, :8]
    turned = pltpu.roll(small, ids[1], 1)
    query_gain[...] = jnp.where(ids[0] == 0, turned[0:1, :8], turned[2:3, :8])
    key_gain[...] = pltpu.roll(small, ids[2], 1)[1:2, :4]


def heads_in_kernel(received, out):
    for j in range(PARTS):
        for h in range(PART_HEADS):
            for qd in range(QUARTERS):
                block = received[(j * PART_HEADS + h) * QUARTERS + qd]
                columns = slice(h * 128, h * 128 + 128)
                out[j, qd * 16 : qd * 16 + 16, columns] = block[:16]
                out[j, 64 + qd * 16 : 80 + qd * 16, columns] = block[16:]


def heads_out_kernel(*refs):
    out = refs[-1]
    for j in range(PARTS):
        for h in range(PART_HEADS):
            for qd in range(QUARTERS):
                to = (j * PART_HEADS + h) * QUARTERS + qd
                columns = slice(h * 128, h * 128 + 128)
                out[to, :16] = refs[j][qd * 16 : qd * 16 + 16, columns]
                out[to, 16:] = refs[j][64 + qd * 16 : 80 + qd * 16, columns]


def finish_out_kernel(attended, branch, routed, logits, products, out):
    out[:, :512] = dot(attended[...], branch[...], ((0,), (0,))).astype(BF)
    ones = jnp.where(lanes((TOK, 128)) == 64, 1.0, 0.0).astype(BF)
    small = dot(routed[...], logits[...], ((0,), (0,))) + dot(products[...], ones, ((0,), (0,)))
    out[:, 512:] = small.astype(BF)


def pick(first, rows_out):
    i = lax.broadcasted_iota(jnp.int32, (128, 128), 1 if rows_out else 0)
    j = lax.broadcasted_iota(jnp.int32, (128, 128), 0 if rows_out else 1)
    return (i == j % HD + first).astype(BF)


def head_rows(block):
    low_half = lanes(block.shape) < HD
    zero = jnp.zeros_like(block)
    return jnp.concatenate([jnp.where(low_half, block, zero), jnp.where(low_half, zero, block)], 0)


def query_rows(block):
    low_half = lanes(block.shape) < HD
    block = block.astype(F32) * HD**-0.5
    return jnp.concatenate(
        [
            jnp.where(low_half, block, 0.0),
            jnp.where(low_half, pltpu.roll(block, HD, 1), 0.0),
        ],
        axis=0,
    ).astype(BF)


def key_segments(seg_key, columns):
    for src in range(N_CTX):
        line = jnp.broadcast_to(seg_key[src : src + 1, :], (TOK, TOK))
        columns[src * TOK : (src + 1) * TOK, :] = line.T


def forward_kernel(packed, seg_key, seg_query, mixed, lse, kv, kv_t, columns, limits):
    src = TOK_TILE // 32
    kv[...] = packed[:, 0:TOK, :].reshape(KEYS, 128)
    i = lax.broadcasted_iota(jnp.int32, (128, 128), 0)
    kv_t[...] = dot((i == lanes((128, 128))).astype(BF), kv[...], ((1,), (1,))).astype(BF)
    key_segments(seg_key, columns)
    limits[...] = jnp.ones_like(limits)

    def tile_rows(tile):
        q = packed[pl.ds(tile * src, src), TOK:PACK, :].reshape(TOK_TILE, 128)
        return query_rows(q), jnp.concatenate([seg_query[tile], seg_query[tile]], axis=1)

    def scores(rows, seg_q, keys):
        s = dot(kv[keys, :], rows, ((1,), (1,)))
        seg_k = jnp.concatenate([columns[keys, :]] * (2 * TOK_TILE // 128), axis=1)
        return jnp.where(seg_k == seg_q, s, -1e30)

    def sums(p):
        return jnp.sum(p.reshape(KEY_TILE // 8, 8, 2 * TOK_TILE), axis=0)

    def store(tile, accum, total, top):
        out = (accum / total).T
        out = jnp.where(
            lanes((TOK_TILE, 128)) < HD, pltpu.roll(out[:TOK_TILE], HD, 1), out[TOK_TILE:]
        )
        mixed[pl.ds(tile * src, src)] = out.astype(BF).reshape(src, 32, 128)
        lse[tile] = top + jnp.log(total)

    for tile in range(TILES):
        rows, seg_q = tile_rows(tile)
        total = jnp.zeros((8, 2 * TOK_TILE), F32)
        accum = jnp.zeros((128, 2 * TOK_TILE), F32)
        for t in range(KEYS // KEY_TILE):
            keys = slice(t * KEY_TILE, (t + 1) * KEY_TILE)
            p = jnp.exp(scores(rows, seg_q, keys))
            total = total + sums(p)
            accum = accum + dot(kv_t[:, keys], p.astype(BF))
        total = jnp.sum(total, axis=0, keepdims=True)
        store(tile, accum, total, jnp.zeros_like(total))
        limits[...] = jnp.maximum(limits[...], jnp.maximum(total, 1.0 / total))

    @pl.when(jnp.logical_not(jnp.max(limits[...]) < 1e25))
    def _():
        @pl.loop(0, TILES)
        def _(tile):
            rows, seg_q = tile_rows(tile)
            top = jnp.full((1, 2 * TOK_TILE), -1e30, F32)
            total = jnp.zeros((8, 2 * TOK_TILE), F32)
            accum = jnp.zeros((128, 2 * TOK_TILE), F32)
            for t in range(KEYS // KEY_TILE):
                keys = slice(t * KEY_TILE, (t + 1) * KEY_TILE)
                s = scores(rows, seg_q, keys)
                newest = jnp.maximum(top, jnp.max(s, axis=0, keepdims=True))
                fade = jnp.exp(top - newest)
                p = jnp.exp(s - newest)
                p = jnp.where(s > -1e29, p, 0.0)
                top = newest
                total = total * fade + sums(p)
                accum = accum * fade + dot(kv_t[:, keys], p.astype(BF))
            store(tile, accum, jnp.sum(total, axis=0, keepdims=True), top)


def probabilities_kernel(packed, seg_key, seg_query, lse, probs, kv_t, kv, columns):
    @pl.when(pl.program_id(0) == 0)
    def _():
        kv[...] = packed[:, 0:TOK, :].reshape(KEYS, 128)
        i = lax.broadcasted_iota(jnp.int32, (128, 128), 0)
        kv_t[...] = dot((i == lanes((128, 128))).astype(BF), kv[...], ((1,), (1,))).astype(BF)
        key_segments(seg_key, columns)

    tile = pl.program_id(0)
    src = TOK_TILE // 32
    q = packed[pl.ds(tile * src, src), TOK:PACK, :].reshape(TOK_TILE, 128)
    rows = query_rows(q)
    seg_q = jnp.concatenate([seg_query[tile], seg_query[tile]], axis=1)
    for t in range(KEYS // KEY_TILE):
        keys = slice(t * KEY_TILE, (t + 1) * KEY_TILE)
        s = dot(kv[keys, :], rows, ((1,), (1,)))
        seg_k = jnp.concatenate([columns[keys, :]] * (2 * TOK_TILE // 128), axis=1)
        s = jnp.where(seg_k == seg_q, s - lse[0], -1e30)
        probs[0, keys, :] = jnp.exp(s).astype(BF)


def value_rows(block):
    low_half = lanes(block.shape) < HD
    block = block.astype(F32)
    return jnp.concatenate(
        [
            jnp.where(low_half, 0.0, pltpu.roll(block, HD, 1)),
            jnp.where(low_half, 0.0, block),
        ],
        axis=0,
    ).astype(BF)


def backward_kernel(packed, probs, kv_t, upper, mixed, out, kv, dkv):
    tile = pl.program_id(0)

    @pl.when(tile == 0)
    def _():
        kv[...] = packed[:, 0:TOK, :].reshape(KEYS, 128)
        dkv[...] = jnp.zeros_like(dkv)

    src = TOK_TILE // 32
    q = packed[pl.ds(tile * src, src), TOK:PACK, :].reshape(TOK_TILE, 128)
    upper_now = upper[...].reshape(TOK_TILE, 128)
    up = value_rows(upper_now)
    both = jnp.concatenate([up, query_rows(q)], axis=0)
    along = (upper_now.astype(F32) * mixed[...].reshape(TOK_TILE, 128).astype(F32)).T
    delta = jnp.concatenate(
        [
            jnp.sum(along[:HD], axis=0, keepdims=True),
            jnp.sum(along[HD:], axis=0, keepdims=True),
        ],
        axis=1,
    )
    dq = jnp.zeros((128, 2 * TOK_TILE), F32)
    for t in range(KEYS // KEY_TILE):
        keys = slice(t * KEY_TILE, (t + 1) * KEY_TILE)
        p = probs[0, keys, :]
        dp = dot(kv[keys, :], up, ((1,), (1,)))
        ds = (p.astype(F32) * (dp - delta)).astype(BF)
        dkv[keys, :] += dot(jnp.concatenate([p, ds], axis=1), both)
        dq = dq + dot(kv_t[:, keys], ds)
    dq = (dq * HD**-0.5).T
    dq = jnp.where(lanes((TOK_TILE, 128)) < HD, dq[:TOK_TILE], pltpu.roll(dq[TOK_TILE:], HD, 1))
    out[pl.ds(tile * src, src), TOK:PACK, :] = dq.astype(BF).reshape(src, 32, 128)

    @pl.when(tile == pl.num_programs(0) - 1)
    def _():
        out[:, 0:TOK, :] = dkv[...].astype(BF).reshape(N_CTX, TOK, 128)


def whole(shape):
    return pl.BlockSpec(shape, lambda i: (0,) * len(shape))


def attend(packed, seg_key, seg_query):
    vmem = pl.BlockSpec(memory_space=pltpu.VMEM)
    return pl.pallas_call(
        forward_kernel,
        in_specs=[vmem] * 3,
        out_specs=[pl.BlockSpec(), vmem],
        out_shape=[
            jax.ShapeDtypeStruct((N_CTX, 32, 128), BF),
            jax.ShapeDtypeStruct((TILES, 1, 2 * TOK_TILE), F32),
        ],
        scratch_shapes=[
            pltpu.VMEM((KEYS, 128), BF),
            pltpu.VMEM((128, KEYS), BF),
            pltpu.VMEM((KEYS, 128), jnp.int32),
            pltpu.VMEM((1, 2 * TOK_TILE), F32),
        ],
        compiler_params=pltpu.CompilerParams(vmem_limit_bytes=24 << 20),
        cost_estimate=estimate(12),
        name="attend",
    )(packed, seg_key, seg_query)


def probabilities(packed, seg_key, seg_query, lse):
    width = 2 * TOK_TILE
    return pl.pallas_call(
        probabilities_kernel,
        grid=(TILES,),
        in_specs=[
            whole((N_CTX, PACK, 128)),
            whole((N_CTX, TOK)),
            whole((TILES, 1, TOK_TILE)),
            pl.BlockSpec((1, 1, width), lambda i: (i, 0, 0)),
        ],
        out_specs=[pl.BlockSpec((1, KEYS, width), lambda i: (i, 0, 0)), whole((128, KEYS))],
        out_shape=[
            jax.ShapeDtypeStruct((TILES, KEYS, width), BF),
            jax.ShapeDtypeStruct((128, KEYS), BF),
        ],
        scratch_shapes=[pltpu.VMEM((KEYS, 128), BF), pltpu.VMEM((KEYS, 128), jnp.int32)],
        compiler_params=pltpu.CompilerParams(vmem_limit_bytes=32 << 20),
        cost_estimate=estimate(11),
        name="probabilities",
    )(packed, seg_key, seg_query, lse)


def attend_back(packed, probs, kv_t, upper, mixed):
    src = TOK_TILE // 32
    piece = pl.BlockSpec((src, 32, 128), lambda i: (i, 0, 0))
    return pl.pallas_call(
        backward_kernel,
        grid=(TILES,),
        in_specs=[
            whole((N_CTX, PACK, 128)),
            pl.BlockSpec((1, KEYS, 2 * TOK_TILE), lambda i: (i, 0, 0)),
            whole((128, KEYS)),
            piece,
            piece,
        ],
        out_specs=whole((N_CTX, PACK, 128)),
        out_shape=jax.ShapeDtypeStruct((N_CTX, PACK, 128), BF),
        scratch_shapes=[pltpu.VMEM((KEYS, 128), BF), pltpu.VMEM((KEYS, 128), F32)],
        compiler_params=pltpu.CompilerParams(vmem_limit_bytes=40 << 20),
        cost_estimate=estimate(21),
        name="attend_back",
    )(packed, probs, kv_t, upper, mixed)


def in_order(pieces, fsdp):
    pieces = jnp.stack(pieces)
    return jnp.concatenate(
        [lax.dynamic_index_in_dim(pieces, fsdp ^ p, keepdims=False) for p in range(4)], axis=0
    )


def inverse_rms(value):
    return lax.rsqrt(jnp.mean(value * value, axis=-1, keepdims=True) + EPSILON)


def after(value, *others):
    return lax.optimization_barrier((value, *others))[0]


def shards(
    hidden_in,
    segment_ids,
    block_order,
    expert_ids,
    pair_order,
    attn_norm,
    w_query,
    w_key,
    w_value,
    query_norm,
    key_norm,
    w_out,
    ffn_norm,
    w_router,
    w_gate,
    w_up,
    w_down,
    cotangent,
):
    place = lax.axis_index("ctx")
    fsdp = lax.axis_index("fsdp")
    core = fsdp % 2
    part = fsdp % PARTS
    both_axes = ("ctx", "fsdp")

    small_lines = [line[None] for line in (attn_norm, query_norm, ffn_norm, key_norm)]
    outgoing_w = call(
        weights_kernel,
        (w_query, w_key, w_value, w_router, *small_lines, segment_ids),
        [((4 * N_CTX, 8, COLS + 128), BF)],
        "weights",
    )[0]
    out_rows, outgoing_w = lax.optimization_barrier(
        ([swap(w_out, j) for j in range(4)], outgoing_w)
    )
    gathered = exchange(outgoing_w, both_axes)
    part_ids = jnp.stack([part ^ j for j in range(PARTS)]).astype(jnp.int32)

    tokens = hidden_in[0]
    order = block_order[0]
    blocks = lax.dynamic_slice_in_dim(order, place * 2, 2)
    tokens_other = swap(tokens, 1)
    tokens_all = [tokens, tokens_other]
    blocks_all = [blocks, swap(blocks, 1)]
    tokens_all = jnp.concatenate(tokens_all, axis=0)

    proj_out = lax.all_gather(in_order(out_rows, fsdp), "ctx", axis=0, tiled=True)

    ids = expert_ids[0]
    experts = jnp.arange(EXPERTS, dtype=jnp.int32)
    named = ids.T[None, :, :] == experts[:, None, None]
    chosen = jnp.any(named, axis=1)
    ranks = pair_order[0, 0].reshape(TOK, TOPK).T
    rank = jnp.sum(jnp.where(named, ranks[None], 0), axis=1)
    earlier = chosen[:, :, None] & (rank[:, :, None] < rank[:, None, :])
    slot = jnp.sum(earlier.astype(jnp.int32), axis=1)
    kept = chosen & (slot < CAP)
    slot = jnp.where(kept, slot, -1)
    places = slot[:, None, :] == jnp.arange(CAP, dtype=jnp.int32)[None, :, None]
    one_hot = places.astype(BF).reshape(EXPERTS * CAP, TOK)

    lay = jnp.arange(TOK, dtype=jnp.int32)
    half = TOK // 2
    positions = (jnp.repeat(jnp.stack(blocks_all), half, axis=1) * half + lay % half).reshape(ROWS)
    freq = THETA ** (-jnp.arange(0, HD, 2).astype(F32) / HD)
    turned = positions.astype(F32)[:, None] * freq[None, :]
    cosine = jnp.tile(jnp.cos(turned), (1, 4))
    sine = jnp.sin(turned)
    sine = jnp.concatenate([-sine, sine, -sine, sine], axis=1)

    inputs_all = tokens_all.astype(F32)
    scale_in = inverse_rms(inputs_all)
    scaled_in = inputs_all * scale_in
    small = gathered[:, :, COLS:]
    lines = small[:, 0, 32:60].astype(F32)
    gain_attn = lines[:, 0:8].reshape(1, D)
    gain_query = lines[:, 8:16].reshape(D)
    gain_ffn = lines[:, 16:24].reshape(1, D)
    gain_key = lines[:, 24:28].reshape(512)
    gain_heads = jnp.concatenate(
        [
            lax.dynamic_slice_in_dim(gain_query, part * FEATURES, FEATURES).reshape(PART_HEADS, 128),
            lax.dynamic_slice_in_dim(gain_key, part * FEATURES // 2, FEATURES // 2).reshape(
                PART_HEADS, HD
            ),
            jnp.ones((PART_HEADS, HD), F32),
        ],
        axis=1,
    ).reshape(1, COLS)
    weights = gathered.reshape(D, COLS + 128)
    proj = weights[:, :COLS]
    proj_router = small[:, :, :EXPERTS].reshape(D, EXPERTS)

    normed_low = (scaled_in * gain_attn).astype(BF)
    qkv = dot(normed_low, proj)
    lane = jnp.arange(COLS)[None] % 256
    is_q, is_k = lane < 128, (lane >= 128) & (lane < 192)
    squares = qkv * qkv
    square_sums = jnp.stack(
        [
            jnp.sum(jnp.where(is_q, squares, 0.0), axis=1),
            jnp.sum(jnp.where(is_k, squares, 0.0), axis=1),
        ]
    )
    square_sums = sum_parts(square_sums.reshape(2, PARTS, TOK)).reshape(2, ROWS)
    scale_q = lax.rsqrt(square_sums[0] / 1024 + EPSILON)[:, None]
    scale_k = lax.rsqrt(square_sums[1] / 512 + EPSILON)[:, None]
    packed = call_near(
        pack_kernel,
        (qkv, scale_q, scale_k, gain_heads, cosine, sine),
        [((N_CTX, PACK, 128), BF, True)],
        "pack",
    )[0]
    packed = exchange(packed, "ctx")
    scales = jnp.where(jnp.arange(128)[None] == 0, scale_q, scale_k)
    packed, part_ids = lax.optimization_barrier((packed, part_ids))

    sequence = fsdp ^ (place // (N_CTX // PARTS))
    seg_small = lax.dynamic_index_in_dim(
        small.reshape(N_CTX, 4, 8, 128), sequence, axis=1, keepdims=False
    )[:, 1:5, 32:96].astype(jnp.int32)
    seg_all = (seg_small[:, 0:2] + 256 * seg_small[:, 2:4]).reshape(N_CTX, TOK)
    seg_query = lax.dynamic_index_in_dim(
        seg_all.reshape(N_CTX, 2, QUARTERS, 16), place % QUARTERS, axis=2, keepdims=False
    ).reshape(TILES, 1, TOK_TILE)

    packed, shard_gate, shard_up, shard_down = lax.optimization_barrier(
        (packed, w_gate[0], w_up[0], w_down[0])
    )
    shards_far = [swap(shard, 2) for shard in (shard_gate, shard_up, shard_down)]
    gate_w, up_w, down_w = [
        in_order([own, swap(own, 1), far, swap(far, 1)], fsdp)
        for own, far in zip((shard_gate, shard_up, shard_down), shards_far)
    ]

    mixed, lse = attend(packed, seg_all, seg_query)
    returned = exchange(mixed, "ctx")
    returned = call_near(heads_in_kernel, (returned,), [((PARTS, TOK, FEATURES), BF, False)], "heads_in", 1)[0]
    pieces = swapped([returned[j] for j in range(PARTS)])
    out_parts = proj_out.reshape(PARTS, FEATURES, D)
    out_parts = [
        lax.dynamic_index_in_dim(out_parts, part ^ j, keepdims=False) for j in range(PARTS)
    ]
    inputs = tokens.astype(F32)
    middle = inputs
    for piece, out_part in zip(pieces, out_parts):
        middle = middle + dot(piece, out_part)
    scale_mid = inverse_rms(middle)
    scaled_mid = middle * scale_mid
    routed_in = (scaled_mid * gain_ffn).astype(BF)
    logits = dot(proj_router, routed_in, ((0,), (1,)))
    logits = jnp.where(chosen, logits, -1e30)
    raised = jnp.where(chosen, jnp.exp(logits - jnp.max(logits, axis=0, keepdims=True)), 0.0)
    gates = raised / jnp.sum(raised, axis=0, keepdims=True)

    upstream_low = cotangent[0]
    upstream = upstream_low.astype(F32)
    rows_out = dot(one_hot, routed_in).astype(BF).reshape(EXPERTS, CAP, D)
    arrived = exchange(rows_out, "ctx").reshape(N_CTX * CAP, D)
    share = jnp.where(places, gates[:, None, :], 0.0)
    row_share = jnp.sum(share, axis=2).reshape(EXPERTS * CAP, 1)
    grads_out = (dot(one_hot, upstream_low) * row_share).astype(BF).reshape(EXPERTS, CAP, D)
    arrived, grads_out, gate_w, up_w, down_w = lax.optimization_barrier(
        (arrived, grads_out, gate_w, up_w, down_w)
    )
    arrived_grad = exchange(grads_out, "ctx").reshape(N_CTX * CAP, D)

    gate_act = dot(arrived, gate_w)
    up_act = dot(arrived, up_w)
    sigma = jax.nn.sigmoid(gate_act)
    silu_gate = gate_act * sigma
    inner = (silu_gate * up_act).astype(BF)
    produced = dot(inner, down_w).astype(BF).reshape(N_CTX, CAP, D)
    produced, arrived_grad = lax.optimization_barrier((produced, arrived_grad))
    produced_home = exchange(produced, "ctx").reshape(EXPERTS * CAP, D)

    grad_inner = dot(arrived_grad, down_w, ((1,), (1,)))
    grad_gate_act = (grad_inner * up_act * sigma * (1.0 + gate_act * (1.0 - sigma))).astype(BF)
    grad_up_act = (grad_inner * silu_gate).astype(BF)
    grad_rows = dot(grad_gate_act, gate_w, ((1,), (1,))) + dot(grad_up_act, up_w, ((1,), (1,)))
    grad_rows = grad_rows.astype(BF).reshape(N_CTX, CAP, D)
    probs, kv_t = probabilities(packed, seg_all, seg_query, lse)
    produced_home, grad_rows, probs, kv_t = lax.optimization_barrier(
        (produced_home, grad_rows, probs, kv_t)
    )
    grad_home = exchange(grad_rows, "ctx").reshape(EXPERTS * CAP, D)

    grad_gate_w = dot(arrived, grad_gate_act, ((0,), (0,))).astype(BF)
    grad_up_w = dot(arrived, grad_up_act, ((0,), (0,))).astype(BF)
    grad_down_w = dot(inner, arrived_grad, ((0,), (0,))).astype(BF)
    grad_gate_up = jnp.stack([grad_gate_w, grad_up_w])
    grad_home, grad_down_w, grad_gate_up = lax.optimization_barrier(
        (grad_home, grad_down_w, grad_gate_up)
    )
    grad_gate_up = lax.psum_scatter(
        grad_gate_up, "fsdp", scatter_dimension=1, tiled=True
    ).astype(F32)

    share = share.reshape(EXPERTS * CAP, TOK)
    share_high = share.astype(BF)
    share_low = (share - share_high.astype(F32)).astype(BF)
    combined = dot(share_high, produced_home, ((0,), (0,)))
    combined = combined + dot(share_low, produced_home, ((0,), (0,)))
    layer_out = (middle + combined).astype(BF)[None]
    along = dot(produced_home, upstream_low, ((1,), (1,))).reshape(EXPERTS, CAP, TOK)
    grad_gates = jnp.sum(jnp.where(places, along, 0.0), axis=1)
    grad_chosen = gates * (grad_gates - jnp.sum(gates * grad_gates, axis=0, keepdims=True))
    grad_logits = grad_chosen.astype(BF)
    grad_routed = dot(grad_logits, proj_router, ((0,), (1,)))
    grad_routed = grad_routed + dot(one_hot, grad_home, ((0,), (0,)))
    through = grad_routed * gain_ffn
    grad_middle = upstream + scale_mid * (
        through - scaled_mid * jnp.mean(through * scaled_mid, axis=1, keepdims=True)
    )
    grad_branch = grad_middle.astype(BF)
    grad_mixed = [dot(grad_branch, out_part, ((1,), (1,))).astype(BF) for out_part in out_parts]
    upper = call_near(
        heads_out_kernel, tuple(swapped(grad_mixed)), [((N_CTX, 32, 128), BF, True)], "heads_out", 1
    )[0]
    upper = exchange(upper, "ctx")

    sorted_pieces = jnp.stack(pieces)
    attended = jnp.concatenate(
        [
            lax.dynamic_index_in_dim(sorted_pieces, part ^ p, keepdims=False)
            for p in range(PARTS)
        ],
        axis=1,
    )
    attended_2 = jnp.concatenate([attended, swap(attended, 1)], axis=0)
    branch_halves = jnp.stack([grad_branch[:, :512], grad_branch[:, 512:]])
    own_half = lax.dynamic_index_in_dim(branch_halves, core, keepdims=False)
    other_half = lax.dynamic_index_in_dim(branch_halves, 1 - core, keepdims=False)
    branch_2 = jnp.concatenate([own_half, swap(other_half, 1)], axis=0)
    late = call_near(
        finish_out_kernel,
        (
            attended_2,
            branch_2,
            routed_in,
            jnp.pad(grad_logits.T, ((0, 0), (0, 128 - EXPERTS))),
            (grad_routed * scaled_mid).astype(BF),
        ),
        [((D, 640), BF, True)],
        "finish_out",
    )[0]
    late, upper = lax.optimization_barrier((late, upper))
    first_sums = exchange(late.reshape(4 * N_CTX, 8, 640), both_axes)

    grads_home = attend_back(packed, probs, kv_t, upper, mixed)
    grads_home, first_sums = lax.optimization_barrier((grads_home, first_sums))
    grads_home = exchange(grads_home, "ctx")
    grads_home, grad_down_w = lax.optimization_barrier((grads_home, grad_down_w))
    grad_down = lax.psum_scatter(
        grad_down_w[None], "fsdp", scatter_dimension=1, tiled=True
    ).astype(F32)

    through_heads, sums, gain_grad = call(
        unpack_kernel,
        (grads_home, qkv, scales, gain_heads, cosine, sine),
        [((ROWS, COLS), F32), ((ROWS, 128), F32), ((8, COLS), F32)],
        "unpack",
    )
    last, grad_normed = call(
        finish_kernel,
        (
            through_heads,
            qkv,
            scales,
            sums,
            swap(sums, 1),
            normed_low,
            far(weights, cut=(slice(0, D), slice(0, COLS))),
            tokens,
            tokens_other,
            gain_grad,
        ),
        [
            ((D, COLS + 128), BF, (slice(0, COLS), slice(COLS, COLS + 128))),
            ((ROWS, D), F32),
        ],
        "finish",
        4,
        part_ids,
    )
    last_sums = exchange(last.reshape(4 * N_CTX, 8, COLS + 128), both_axes)

    grad_normed = grad_normed.reshape(PARTS, TOK, D)
    grad_normed = sum(swapped([grad_normed[j] for j in range(PARTS)]))
    through_in = grad_normed * gain_attn
    scaled_own = scaled_in[:TOK]
    input_grad = grad_middle + scale_in[:TOK] * (
        through_in - scaled_own * jnp.mean(through_in * scaled_own, axis=1, keepdims=True)
    )

    first_sums = jnp.sum(first_sums.reshape(2 * N_CTX, 2, 8, 640).astype(F32), axis=0)
    grad_out = jnp.concatenate([first_sums[0, :, :512], first_sums[1, :, :512]], axis=1)
    first_small = first_sums[0, :, 512:] + first_sums[1, :, 512:]
    ready = (
        input_grad[None],
        grad_out,
        first_small[:, 64],
        first_small[:, :EXPERTS],
        grad_gate_up[0][None],
        grad_gate_up[1][None],
        grad_down,
    )
    index = 4 * place + fsdp
    final_ids = jnp.stack(
        [index % 16 // 8, (128 - index % 8 * 8) % 128, (128 - index % 16 * 4) % 128]
    ).astype(jnp.int32)
    last_sums, ready, final_ids = lax.optimization_barrier((last_sums, ready, final_ids))
    grad_query, grad_key, grad_value, attn_gain, query_gain, key_gain = call(
        final_kernel,
        (last_sums,),
        [
            ((8, 1024), F32),
            ((8, 512), F32),
            ((8, 512), F32),
            ((1, 8), F32),
            ((1, 8), F32),
            ((1, 4), F32),
        ],
        "final",
        2,
        final_ids,
    )
    return (
        layer_out,
        ready[0],
        attn_gain.reshape(8),
        grad_query,
        grad_key,
        grad_value,
        query_gain.reshape(8),
        key_gain.reshape(4),
        *ready[1:],
    )


def solution(mesh):
    row = P("fsdp", "ctx", None)
    flat = P(("ctx", "fsdp"))
    dense = P(("ctx", "fsdp"), None)
    expert = P("ctx", "fsdp", None)
    in_specs = (
        row,
        P("fsdp", "ctx"),
        P("fsdp", None),
        row,
        row,
        flat,
        dense,
        dense,
        dense,
        flat,
        flat,
        dense,
        flat,
        dense,
        expert,
        expert,
        expert,
        row,
    )
    out_specs = (
        row,
        row,
        flat,
        dense,
        dense,
        dense,
        flat,
        flat,
        dense,
        flat,
        dense,
        expert,
        expert,
        expert,
    )
    return jax.shard_map(shards, mesh=mesh, in_specs=in_specs, out_specs=out_specs, check_vma=False)
```

```python
import jax
import jax.numpy as jnp
from jax import lax
from jax.experimental import pallas as pl
from jax.experimental.pallas import tpu as pltpu
from jax.sharding import PartitionSpec as P

D = 1024
HEADS = 16
KVH = 8
HD = 64
EXPERTS = 32
TOPK = 8
TOK = 128
CAP = 32
N_CTX = 32
EPSILON = 1e-05
THETA = 10000.0
BF = jnp.bfloat16
F32 = jnp.float32

PARTS = 2
PART_HEADS = KVH // PARTS
COLS = PART_HEADS * 256
FEATURES = PART_HEADS * 128
ROWS = PARTS * TOK
QUARTERS = 4
PACK = TOK + TOK // QUARTERS
KEYS = N_CTX * TOK
QUERIES = KEYS // QUARTERS
KEY_TILE = 512
VMEM_LIMIT = 62 << 20
TOK_TILE = 128
TILES = QUERIES // TOK_TILE


def dot(a, b, dims=((1,), (0,))):
    return lax.dot_general(a, b, (dims, ((), ())), preferred_element_type=F32)


def swap(array, j):
    return lax.ppermute(array, "fsdp", [(i, i ^ j) for i in range(4)]) if j else array


def swapped(pieces):
    return [swap(piece, j) for j, piece in enumerate(pieces)]


def sum_parts(value):
    step = 1
    while step < PARTS:
        value = value + swap(jnp.stack([value[:, j ^ step] for j in range(PARTS)], 1), step)
        step *= 2
    return value


def exchange(array, axis):
    return lax.all_to_all(array, axis, split_axis=0, concat_axis=0, tiled=True)


def lanes(shape):
    return lax.broadcasted_iota(jnp.int32, shape, len(shape) - 1)


def swap_halves(value):
    first = lanes(value.shape) % HD < HD // 2
    up = pltpu.roll(value, value.shape[1] - HD // 2, 1)
    down = pltpu.roll(value, HD // 2, 1)
    return jnp.where(first, up, down)


def call_near(kernel, inputs, outputs, name, micros=2, mib=12):
    vmem = pl.BlockSpec(memory_space=pltpu.VMEM)
    return pl.pallas_call(
        kernel,
        in_specs=[vmem] * len(inputs),
        out_specs=[pl.BlockSpec() if sent else vmem for _, _, sent in outputs],
        out_shape=[jax.ShapeDtypeStruct(shape, dtype) for shape, dtype, _ in outputs],
        compiler_params=pltpu.CompilerParams(vmem_limit_bytes=mib << 20),
        cost_estimate=estimate(micros),
        name=name,
    )(*inputs)


class Held:
    def __init__(self, buffer, copy):
        self.buffer, self.copy = buffer, copy

    def wait(self):
        if self.copy is not None:
            self.copy.wait()
            self.copy = None

    def __getitem__(self, index):
        self.wait()
        return self.buffer[index]


class Made:
    def __init__(self, buffer, target, columns, sems, first):
        self.buffer, self.target, self.columns = buffer, target, columns
        self.sems, self.first = sems, first
        self.copies = []

    def __getitem__(self, index):
        return self.buffer[index]

    def __setitem__(self, index, value):
        self.buffer[index] = value

    def send(self, rows=None):
        source, target = self.buffer, self.target
        if rows is not None:
            source = source.at[rows]
        if self.columns is not None:
            target = target.at[slice(None) if rows is None else rows, self.columns]
        elif rows is not None:
            target = target.at[rows]
        copy = pltpu.make_async_copy(source, target, self.sems.at[self.first + len(self.copies)])
        copy.start()
        self.copies.append(copy)


SENDS = 4


def far(array, rows=None, at=None, cut=None):
    return (array, rows, at, cut)


def call(kernel, inputs, outputs, name, micros=2, ids=None):
    made = []
    for k, (shape, dtype, *cuts) in enumerate(outputs):
        for columns in cuts[0] if cuts else (None,):
            wide = shape if columns is None else (shape[0], columns.stop - columns.start)
            made.append((k, wide, dtype, columns))
    hbm = pl.BlockSpec(memory_space=pltpu.HBM)
    inputs = [i if isinstance(i, tuple) else far(i) for i in inputs]
    scratch = []
    for array, rows, _, part in inputs:
        shape = array.shape if rows is None else (rows, *array.shape[1:])
        if part is not None:
            shape = tuple(p.stop - p.start for p in part) + array.shape[len(part) :]
        scratch.append(pltpu.VMEM(shape, array.dtype))
    scratch += [pltpu.VMEM(shape, dtype) for _, shape, dtype, _ in made]
    scratch.append(pltpu.SemaphoreType.DMA((len(inputs) + SENDS * len(made),)))
    numbers = [] if ids is None else [ids]

    def body(*refs):
        refs = list(refs)
        own_ids = refs.pop(0) if numbers else None
        ins, outs = refs[: len(inputs)], refs[len(inputs) : len(inputs) + len(outputs)]
        buffers = refs[len(inputs) + len(outputs) :]
        sems = buffers[-1]
        given, results = [], []
        for k, (ref, (_, rows, at, part)) in enumerate(zip(ins, inputs)):
            if rows is not None:
                ref = ref.at[pl.ds(pl.multiple_of(own_ids[at] * rows, rows), rows)]
            elif part is not None:
                ref = ref.at[part]
            copy = pltpu.make_async_copy(ref, buffers[k], sems.at[k])
            copy.start()
            given.append(Held(buffers[k], copy))
        for k, (number, _, _, columns) in enumerate(made):
            ref = outs[number]
            results.append(
                Made(buffers[len(inputs) + k], ref, columns, sems, len(inputs) + SENDS * k)
            )
        kernel(*([own_ids] if numbers else []), *given, *results)
        for held in given:
            held.wait()
        for result in results:
            if not result.copies:
                result.send()
        for result in results:
            for copy in result.copies:
                copy.wait()

    return pl.pallas_call(
        body,
        in_specs=[pl.BlockSpec(memory_space=pltpu.SMEM)] * len(numbers) + [hbm] * len(inputs),
        out_specs=[hbm] * len(outputs),
        out_shape=[jax.ShapeDtypeStruct(shape, dtype) for shape, dtype, *_ in outputs],
        scratch_shapes=scratch,
        compiler_params=pltpu.CompilerParams(vmem_limit_bytes=VMEM_LIMIT),
        cost_estimate=estimate(micros),
        name=name,
    )(*numbers, *[i[0] for i in inputs])


def estimate(micros):
    return pl.CostEstimate(flops=int(micros * 1.1e9), bytes_accessed=1 << 16, transcendentals=0)


def weights_kernel(w_query, w_key, w_value, w_router, attn, query, ffn, key, segments, out):
    row = lax.broadcasted_iota(jnp.int32, (8, 128), 0)
    lane = lanes((8, 128))
    middle = (lane >= 32) & (lane < 96)
    gains = [line[...].astype(F32) for line in (attn, query, ffn, key)]
    gains = jnp.concatenate(gains + [jnp.zeros((1, 100), F32)], axis=1)
    seg = segments[...]
    low, high = (seg & 255).astype(F32), (seg >> 8).astype(F32)
    small = jnp.zeros((8, 128), F32)
    lines = (
        pltpu.roll(low, 32, 1),
        pltpu.roll(low, 96, 1),
        pltpu.roll(high, 32, 1),
        pltpu.roll(high, 96, 1),
    )
    for r, line in enumerate(lines):
        small = jnp.where((row == r + 1) & middle, line, small)
    small = jnp.where((row == 0) & (lane >= 32), pltpu.roll(gains, 32, 1), small)
    router = jnp.concatenate([w_router[...].astype(F32), jnp.zeros((8, 96), F32)], axis=1)
    small = jnp.where(lane < 32, router, small)
    parts = []
    for p in range(PARTS):
        columns = []
        for h in range(PART_HEADS):
            at = p * PART_HEADS + h
            columns.append(w_query[:, at * 128 : at * 128 + 128].astype(F32))
            columns.append(w_key[:, at * HD : at * HD + HD].astype(F32))
            columns.append(w_value[:, at * HD : at * HD + HD].astype(F32))
        parts.append(jnp.concatenate(columns + [small], axis=1).astype(BF))
    for to in range(4 * N_CTX):
        out[to] = parts[to % PARTS]


def pack_kernel(qkv, scale_q, scale_k, gain, cosine, sine, out):
    for j in range(PARTS):
        rows = slice(j * TOK, (j + 1) * TOK)
        turn_c, turn_s = cosine[rows], sine[rows]
        cq, ck = scale_q[rows], scale_k[rows]
        for h in range(PART_HEADS):
            at = h * 256
            q = qkv[rows, at : at + 128] * cq * gain[:, at : at + 128]
            q = (q * turn_c + swap_halves(q) * turn_s).astype(BF)
            kv = qkv[rows, at + 128 : at + 256]
            k = kv * ck * gain[:, at + 128 : at + 256]
            k = k * turn_c + swap_halves(k) * turn_s
            kv = jnp.where(lanes(kv.shape) < HD, k, kv).astype(BF)
            for qd in range(QUARTERS):
                to = (j * PART_HEADS + h) * QUARTERS + qd
                out[to, 0:TOK, :] = kv
                out[to, TOK : TOK + 16, :] = q[qd * 16 : qd * 16 + 16]
                out[to, TOK + 16 : TOK + 32, :] = q[64 + qd * 16 : 64 + qd * 16 + 16]


def other_rows(value):
    return jnp.concatenate([value[TOK:], value[:TOK]], axis=0)


def unpack_kernel(grads, qkv, scales, gain, cosine, sine, out, sums, gain_grad):
    lines = [None] * (2 * PART_HEADS)
    for j in range(PARTS):
        rows = slice(j * TOK, (j + 1) * TOK)
        turn_c, turn_s = cosine[rows, :], sine[rows, :]
        cq, ck = scales[rows, 0:1], scales[rows, 1:2]
        sum_q = jnp.zeros((TOK, 128), F32)
        sum_k = jnp.zeros((TOK, 128), F32)
        for h in range(PART_HEADS):
            at = h * 256
            base = (j * PART_HEADS + h) * QUARTERS
            pieces = [
                grads[base + qd, TOK + 16 * half : TOK + 16 * half + 16, :]
                for half in range(2)
                for qd in range(QUARTERS)
            ]
            dq = jnp.concatenate(pieces, axis=0).astype(F32)
            dq = dq * turn_c - swap_halves(dq) * turn_s
            dkv = sum(grads[base + qd, 0:TOK, :].astype(F32) for qd in range(QUARTERS))
            dk = dkv * turn_c - swap_halves(dkv) * turn_s
            is_k = lanes(dkv.shape) < HD
            dkv = jnp.where(is_k, dk, dkv)
            a_q = qkv[rows, at : at + 128] * cq
            a_k = qkv[rows, at + 128 : at + 256] * ck
            through_q = dq * a_q
            through_k = jnp.where(is_k, dkv * a_k, 0.0)
            g_q = gain[:, at : at + 128]
            g_k = gain[:, at + 128 : at + 256]
            out[rows, at : at + 128] = dq * g_q
            out[rows, at + 128 : at + 256] = dkv * g_k
            sum_q = sum_q + through_q * g_q
            sum_k = sum_k + through_k * g_k
            for k, through in enumerate((through_q, through_k)):
                line = jnp.sum(through, axis=0, keepdims=True)
                known = lines[2 * h + k]
                lines[2 * h + k] = line if known is None else known + line
        out.send(rows)
        total_q = jnp.sum(sum_q, axis=1, keepdims=True)
        total_k = jnp.sum(sum_k, axis=1, keepdims=True)
        sums[rows, :] = jnp.where(lanes((TOK, 128)) == 0, total_q, total_k)
    gain_grad[...] = jnp.broadcast_to(jnp.concatenate(lines, axis=1), (8, COLS))


def finish_kernel(ids, through, qkv, scales, sums, sums_other, normed, weights, tokens, tokens_other, gain_grad, last, last_small, grad_normed):
    total = sums[...] + other_rows(sums_other[...])
    lane = lanes((TOK, COLS)) % 256
    is_q, is_k = lane < 128, (lane >= 128) & (lane < 192)
    grads = []
    for j in range(PARTS):
        rows = slice(j * TOK, (j + 1) * TOK)
        scale = jnp.where(is_q, scales[rows, 0:1], jnp.where(is_k, scales[rows, 1:2], 1.0))
        mean = jnp.where(is_q, total[rows, 0:1] / 1024, jnp.where(is_k, total[rows, 1:2] / 512, 0.0))
        grads.append((scale * (through[rows, :] - qkv[rows, :] * scale * mean)).astype(BF))
    grad = jnp.concatenate(grads, axis=0)
    tile = D // SENDS
    for t in range(SENDS):
        rows = slice(t * tile, (t + 1) * tile)
        last[rows, :] = dot(normed[:, rows], grad, ((0,), (0,))).astype(BF)
        last.send(rows)
    normed_grad = dot(grad, weights[...], ((1,), (1,)))
    grad_normed[...] = normed_grad
    grad_normed.send()
    value = jnp.concatenate([tokens[...], tokens_other[...]], axis=0).astype(F32)
    products = (normed_grad * (value * inverse_rms(value))).astype(BF)
    ones = jnp.where(lanes((ROWS, 128)) == 64, 1.0, 0.0).astype(BF)
    last_small[...] = dot(products, ones, ((0,), (0,))).astype(BF)
    row = lax.broadcasted_iota(jnp.int32, (TOK, TOK), 0) % 8
    for h in range(PART_HEADS):
        query, key = [gain_grad[0:1, h * 256 + k : h * 256 + k + 128] for k in (0, 128)]
        block = jnp.where(row == 0, query, jnp.where(row == 1, key, 0.0))
        block = jnp.where(row == 2, pltpu.roll(query, HD, 1), block)
        at = pl.ds(pl.multiple_of(ids[0] * FEATURES + h * TOK, TOK), TOK)
        known = last_small[at, :].astype(F32)
        last_small[at, :] = jnp.where(lanes((TOK, TOK)) < HD, block, known).astype(BF)


def final_kernel(ids, *refs):
    pieces, (query, key, value, attn_gain, query_gain, key_gain) = refs[:-6], refs[-6:]
    sums = [0.0] * (COLS // 128 + 1)
    for piece in pieces:
        for t in range(len(sums)):
            block = piece[:, :, t * 128 : t * 128 + 128].astype(F32)
            sums[t] = sums[t] + jnp.sum(block.reshape(-1, PARTS, 8, 128), axis=0)
    column = sums.__getitem__
    low_half = lanes((8, 128)) < HD
    for h in range(0, PART_HEADS, 2):
        first, second = column(2 * h), column(2 * h + 2)
        kv_first, kv_second = column(2 * h + 1), column(2 * h + 3)
        for p in range(PARTS):
            at = (p * PART_HEADS + h) * 128
            query[:, at : at + 128] = first[p]
            query[:, at + 128 : at + 256] = second[p]
            at = at // 2
            key[:, at : at + 128] = jnp.where(low_half, kv_first[p], pltpu.roll(kv_second[p], HD, 1))
            value[:, at : at + 128] = jnp.where(
                low_half, pltpu.roll(kv_first[p], HD, 1), kv_second[p]
            )
    small = jnp.sum(column(2 * PART_HEADS), axis=0)
    row = lax.broadcasted_iota(jnp.int32, (8, 128), 0)
    lane = lanes((8, 128))
    attn = jnp.sum(jnp.where(lane == 64, small, 0.0), axis=1, keepdims=True)
    attn_gain[...] = jnp.sum(jnp.where(row == lane, attn, 0.0), axis=0, keepdims=True)[:, :8]
    turned = pltpu.roll(small, ids[1], 1)
    query_gain[...] = jnp.where(ids[0] == 0, turned[0:1, :8], turned[2:3, :8])
    key_gain[...] = pltpu.roll(small, ids[2], 1)[1:2, :4]


def heads_in_kernel(received, out):
    for j in range(PARTS):
        for h in range(PART_HEADS):
            for qd in range(QUARTERS):
                block = received[(j * PART_HEADS + h) * QUARTERS + qd]
                columns = slice(h * 128, h * 128 + 128)
                out[j, qd * 16 : qd * 16 + 16, columns] = block[:16]
                out[j, 64 + qd * 16 : 80 + qd * 16, columns] = block[16:]


def heads_out_kernel(*refs):
    out = refs[-1]
    for j in range(PARTS):
        for h in range(PART_HEADS):
            for qd in range(QUARTERS):
                to = (j * PART_HEADS + h) * QUARTERS + qd
                columns = slice(h * 128, h * 128 + 128)
                out[to, :16] = refs[j][qd * 16 : qd * 16 + 16, columns]
                out[to, 16:] = refs[j][64 + qd * 16 : 80 + qd * 16, columns]


def finish_out_kernel(attended, branch, routed, logits, products, out):
    out[:, :512] = dot(attended[...], branch[...], ((0,), (0,))).astype(BF)
    ones = jnp.where(lanes((TOK, 128)) == 64, 1.0, 0.0).astype(BF)
    small = dot(routed[...], logits[...], ((0,), (0,))) + dot(products[...], ones, ((0,), (0,)))
    out[:, 512:] = small.astype(BF)


def pick(first, rows_out):
    i = lax.broadcasted_iota(jnp.int32, (128, 128), 1 if rows_out else 0)
    j = lax.broadcasted_iota(jnp.int32, (128, 128), 0 if rows_out else 1)
    return (i == j % HD + first).astype(BF)


def head_rows(block):
    low_half = lanes(block.shape) < HD
    zero = jnp.zeros_like(block)
    return jnp.concatenate([jnp.where(low_half, block, zero), jnp.where(low_half, zero, block)], 0)


def query_rows(block):
    low_half = lanes(block.shape) < HD
    block = block.astype(F32) * HD**-0.5
    return jnp.concatenate(
        [
            jnp.where(low_half, block, 0.0),
            jnp.where(low_half, pltpu.roll(block, HD, 1), 0.0),
        ],
        axis=0,
    ).astype(BF)


def key_segments(seg_key, columns):
    for src in range(N_CTX):
        line = jnp.broadcast_to(seg_key[src : src + 1, :], (TOK, TOK))
        columns[src * TOK : (src + 1) * TOK, :] = line.T


def forward_kernel(packed, seg_key, seg_query, mixed, lse, kv, kv_t, columns, limits):
    src = TOK_TILE // 32
    kv[...] = packed[:, 0:TOK, :].reshape(KEYS, 128)
    i = lax.broadcasted_iota(jnp.int32, (128, 128), 0)
    kv_t[...] = dot((i == lanes((128, 128))).astype(BF), kv[...], ((1,), (1,))).astype(BF)
    key_segments(seg_key, columns)
    limits[...] = jnp.ones_like(limits)

    def tile_rows(tile):
        q = packed[pl.ds(tile * src, src), TOK:PACK, :].reshape(TOK_TILE, 128)
        return query_rows(q), jnp.concatenate([seg_query[tile], seg_query[tile]], axis=1)

    def scores(rows, seg_q, keys):
        s = dot(kv[keys, :], rows, ((1,), (1,)))
        seg_k = jnp.concatenate([columns[keys, :]] * (2 * TOK_TILE // 128), axis=1)
        return jnp.where(seg_k == seg_q, s, -1e30)

    def sums(p):
        return jnp.sum(p.reshape(KEY_TILE // 8, 8, 2 * TOK_TILE), axis=0)

    def store(tile, accum, total, top):
        out = (accum / total).T
        out = jnp.where(
            lanes((TOK_TILE, 128)) < HD, pltpu.roll(out[:TOK_TILE], HD, 1), out[TOK_TILE:]
        )
        mixed[pl.ds(tile * src, src)] = out.astype(BF).reshape(src, 32, 128)
        lse[tile] = top + jnp.log(total)

    for tile in range(TILES):
        rows, seg_q = tile_rows(tile)
        total = jnp.zeros((8, 2 * TOK_TILE), F32)
        accum = jnp.zeros((128, 2 * TOK_TILE), F32)
        for t in range(KEYS // KEY_TILE):
            keys = slice(t * KEY_TILE, (t + 1) * KEY_TILE)
            p = jnp.exp(scores(rows, seg_q, keys))
            total = total + sums(p)
            accum = accum + dot(kv_t[:, keys], p.astype(BF))
        total = jnp.sum(total, axis=0, keepdims=True)
        store(tile, accum, total, jnp.zeros_like(total))
        limits[...] = jnp.maximum(limits[...], jnp.maximum(total, 1.0 / total))

    @pl.when(jnp.logical_not(jnp.max(limits[...]) < 1e25))
    def _():
        @pl.loop(0, TILES)
        def _(tile):
            rows, seg_q = tile_rows(tile)
            top = jnp.full((1, 2 * TOK_TILE), -1e30, F32)
            total = jnp.zeros((8, 2 * TOK_TILE), F32)
            accum = jnp.zeros((128, 2 * TOK_TILE), F32)
            for t in range(KEYS // KEY_TILE):
                keys = slice(t * KEY_TILE, (t + 1) * KEY_TILE)
                s = scores(rows, seg_q, keys)
                newest = jnp.maximum(top, jnp.max(s, axis=0, keepdims=True))
                fade = jnp.exp(top - newest)
                p = jnp.exp(s - newest)
                p = jnp.where(s > -1e29, p, 0.0)
                top = newest
                total = total * fade + sums(p)
                accum = accum * fade + dot(kv_t[:, keys], p.astype(BF))
            store(tile, accum, jnp.sum(total, axis=0, keepdims=True), top)


def probabilities_kernel(packed, seg_key, seg_query, lse, probs, kv_t, kv, columns):
    @pl.when(pl.program_id(0) == 0)
    def _():
        kv[...] = packed[:, 0:TOK, :].reshape(KEYS, 128)
        i = lax.broadcasted_iota(jnp.int32, (128, 128), 0)
        kv_t[...] = dot((i == lanes((128, 128))).astype(BF), kv[...], ((1,), (1,))).astype(BF)
        key_segments(seg_key, columns)

    tile = pl.program_id(0)
    src = TOK_TILE // 32
    q = packed[pl.ds(tile * src, src), TOK:PACK, :].reshape(TOK_TILE, 128)
    rows = query_rows(q)
    seg_q = jnp.concatenate([seg_query[tile], seg_query[tile]], axis=1)
    for t in range(KEYS // KEY_TILE):
        keys = slice(t * KEY_TILE, (t + 1) * KEY_TILE)
        s = dot(kv[keys, :], rows, ((1,), (1,)))
        seg_k = jnp.concatenate([columns[keys, :]] * (2 * TOK_TILE // 128), axis=1)
        s = jnp.where(seg_k == seg_q, s - lse[0], -1e30)
        probs[0, keys, :] = jnp.exp(s).astype(BF)


def value_rows(block):
    low_half = lanes(block.shape) < HD
    block = block.astype(F32)
    return jnp.concatenate(
        [
            jnp.where(low_half, 0.0, pltpu.roll(block, HD, 1)),
            jnp.where(low_half, 0.0, block),
        ],
        axis=0,
    ).astype(BF)


def backward_kernel(packed, probs, kv_t, upper, mixed, out, kv, dkv):
    tile = pl.program_id(0)

    @pl.when(tile == 0)
    def _():
        kv[...] = packed[:, 0:TOK, :].reshape(KEYS, 128)
        dkv[...] = jnp.zeros_like(dkv)

    src = TOK_TILE // 32
    q = packed[pl.ds(tile * src, src), TOK:PACK, :].reshape(TOK_TILE, 128)
    upper_now = upper[...].reshape(TOK_TILE, 128)
    up = value_rows(upper_now)
    both = jnp.concatenate([up, query_rows(q)], axis=0)
    along = (upper_now.astype(F32) * mixed[...].reshape(TOK_TILE, 128).astype(F32)).T
    delta = jnp.concatenate(
        [
            jnp.sum(along[:HD], axis=0, keepdims=True),
            jnp.sum(along[HD:], axis=0, keepdims=True),
        ],
        axis=1,
    )
    dq = jnp.zeros((128, 2 * TOK_TILE), F32)
    for t in range(KEYS // KEY_TILE):
        keys = slice(t * KEY_TILE, (t + 1) * KEY_TILE)
        p = probs[0, keys, :]
        dp = dot(kv[keys, :], up, ((1,), (1,)))
        ds = (p.astype(F32) * (dp - delta)).astype(BF)
        dkv[keys, :] += dot(jnp.concatenate([p, ds], axis=1), both)
        dq = dq + dot(kv_t[:, keys], ds)
    dq = (dq * HD**-0.5).T
    dq = jnp.where(lanes((TOK_TILE, 128)) < HD, dq[:TOK_TILE], pltpu.roll(dq[TOK_TILE:], HD, 1))
    out[pl.ds(tile * src, src), TOK:PACK, :] = dq.astype(BF).reshape(src, 32, 128)

    @pl.when(tile == pl.num_programs(0) - 1)
    def _():
        out[:, 0:TOK, :] = dkv[...].astype(BF).reshape(N_CTX, TOK, 128)


def whole(shape):
    return pl.BlockSpec(shape, lambda i: (0,) * len(shape))


def attend(packed, seg_key, seg_query):
    vmem = pl.BlockSpec(memory_space=pltpu.VMEM)
    return pl.pallas_call(
        forward_kernel,
        in_specs=[vmem] * 3,
        out_specs=[pl.BlockSpec(), vmem],
        out_shape=[
            jax.ShapeDtypeStruct((N_CTX, 32, 128), BF),
            jax.ShapeDtypeStruct((TILES, 1, 2 * TOK_TILE), F32),
        ],
        scratch_shapes=[
            pltpu.VMEM((KEYS, 128), BF),
            pltpu.VMEM((128, KEYS), BF),
            pltpu.VMEM((KEYS, 128), jnp.int32),
            pltpu.VMEM((1, 2 * TOK_TILE), F32),
        ],
        compiler_params=pltpu.CompilerParams(vmem_limit_bytes=24 << 20),
        cost_estimate=estimate(12),
        name="attend",
    )(packed, seg_key, seg_query)


def probabilities(packed, seg_key, seg_query, lse):
    width = 2 * TOK_TILE
    return pl.pallas_call(
        probabilities_kernel,
        grid=(TILES,),
        in_specs=[
            whole((N_CTX, PACK, 128)),
            whole((N_CTX, TOK)),
            whole((TILES, 1, TOK_TILE)),
            pl.BlockSpec((1, 1, width), lambda i: (i, 0, 0)),
        ],
        out_specs=[pl.BlockSpec((1, KEYS, width), lambda i: (i, 0, 0)), whole((128, KEYS))],
        out_shape=[
            jax.ShapeDtypeStruct((TILES, KEYS, width), BF),
            jax.ShapeDtypeStruct((128, KEYS), BF),
        ],
        scratch_shapes=[pltpu.VMEM((KEYS, 128), BF), pltpu.VMEM((KEYS, 128), jnp.int32)],
        compiler_params=pltpu.CompilerParams(vmem_limit_bytes=32 << 20),
        cost_estimate=estimate(11),
        name="probabilities",
    )(packed, seg_key, seg_query, lse)


def attend_back(packed, probs, kv_t, upper, mixed):
    src = TOK_TILE // 32
    piece = pl.BlockSpec((src, 32, 128), lambda i: (i, 0, 0))
    return pl.pallas_call(
        backward_kernel,
        grid=(TILES,),
        in_specs=[
            whole((N_CTX, PACK, 128)),
            pl.BlockSpec((1, KEYS, 2 * TOK_TILE), lambda i: (i, 0, 0)),
            whole((128, KEYS)),
            piece,
            piece,
        ],
        out_specs=whole((N_CTX, PACK, 128)),
        out_shape=jax.ShapeDtypeStruct((N_CTX, PACK, 128), BF),
        scratch_shapes=[pltpu.VMEM((KEYS, 128), BF), pltpu.VMEM((KEYS, 128), F32)],
        compiler_params=pltpu.CompilerParams(vmem_limit_bytes=VMEM_LIMIT),
        cost_estimate=estimate(21),
        name="attend_back",
    )(packed, probs, kv_t, upper, mixed)


def in_order(pieces, fsdp):
    pieces = jnp.stack(pieces)
    return jnp.concatenate(
        [lax.dynamic_index_in_dim(pieces, fsdp ^ p, keepdims=False) for p in range(4)], axis=0
    )


def inverse_rms(value):
    return lax.rsqrt(jnp.mean(value * value, axis=-1, keepdims=True) + EPSILON)


def after(value, *others):
    return lax.optimization_barrier((value, *others))[0]


def shards(
    hidden_in,
    segment_ids,
    block_order,
    expert_ids,
    pair_order,
    attn_norm,
    w_query,
    w_key,
    w_value,
    query_norm,
    key_norm,
    w_out,
    ffn_norm,
    w_router,
    w_gate,
    w_up,
    w_down,
    cotangent,
):
    place = lax.axis_index("ctx")
    fsdp = lax.axis_index("fsdp")
    core = fsdp % 2
    part = fsdp % PARTS
    both_axes = ("ctx", "fsdp")

    small_lines = [line[None] for line in (attn_norm, query_norm, ffn_norm, key_norm)]
    outgoing_w = call(
        weights_kernel,
        (w_query, w_key, w_value, w_router, *small_lines, segment_ids),
        [((4 * N_CTX, 8, COLS + 128), BF)],
        "weights",
    )[0]
    out_rows, outgoing_w = lax.optimization_barrier(
        ([swap(w_out, j) for j in range(4)], outgoing_w)
    )
    gathered = exchange(outgoing_w, both_axes)
    part_ids = jnp.stack([part ^ j for j in range(PARTS)]).astype(jnp.int32)

    tokens = hidden_in[0]
    order = block_order[0]
    blocks = lax.dynamic_slice_in_dim(order, place * 2, 2)
    tokens_other = swap(tokens, 1)
    tokens_all = [tokens, tokens_other]
    blocks_all = [blocks, swap(blocks, 1)]
    tokens_all = jnp.concatenate(tokens_all, axis=0)

    proj_out = lax.all_gather(in_order(out_rows, fsdp), "ctx", axis=0, tiled=True)

    ids = expert_ids[0]
    experts = jnp.arange(EXPERTS, dtype=jnp.int32)
    named = ids.T[None, :, :] == experts[:, None, None]
    chosen = jnp.any(named, axis=1)
    ranks = pair_order[0, 0].reshape(TOK, TOPK).T
    rank = jnp.sum(jnp.where(named, ranks[None], 0), axis=1)
    earlier = chosen[:, :, None] & (rank[:, :, None] < rank[:, None, :])
    slot = jnp.sum(earlier.astype(jnp.int32), axis=1)
    kept = chosen & (slot < CAP)
    slot = jnp.where(kept, slot, -1)
    places = slot[:, None, :] == jnp.arange(CAP, dtype=jnp.int32)[None, :, None]
    one_hot = places.astype(BF).reshape(EXPERTS * CAP, TOK)

    lay = jnp.arange(TOK, dtype=jnp.int32)
    half = TOK // 2
    positions = (jnp.repeat(jnp.stack(blocks_all), half, axis=1) * half + lay % half).reshape(ROWS)
    freq = THETA ** (-jnp.arange(0, HD, 2).astype(F32) / HD)
    turned = positions.astype(F32)[:, None] * freq[None, :]
    cosine = jnp.tile(jnp.cos(turned), (1, 4))
    sine = jnp.sin(turned)
    sine = jnp.concatenate([-sine, sine, -sine, sine], axis=1)

    inputs_all = tokens_all.astype(F32)
    scale_in = inverse_rms(inputs_all)
    scaled_in = inputs_all * scale_in
    small = gathered[:, :, COLS:]
    lines = small[:, 0, 32:60].astype(F32)
    gain_attn = lines[:, 0:8].reshape(1, D)
    gain_query = lines[:, 8:16].reshape(D)
    gain_ffn = lines[:, 16:24].reshape(1, D)
    gain_key = lines[:, 24:28].reshape(512)
    gain_heads = jnp.concatenate(
        [
            lax.dynamic_slice_in_dim(gain_query, part * FEATURES, FEATURES).reshape(PART_HEADS, 128),
            lax.dynamic_slice_in_dim(gain_key, part * FEATURES // 2, FEATURES // 2).reshape(
                PART_HEADS, HD
            ),
            jnp.ones((PART_HEADS, HD), F32),
        ],
        axis=1,
    ).reshape(1, COLS)
    weights = gathered.reshape(D, COLS + 128)
    proj = weights[:, :COLS]
    proj_router = small[:, :, :EXPERTS].reshape(D, EXPERTS)

    normed_low = (scaled_in * gain_attn).astype(BF)
    qkv = dot(normed_low, proj)
    lane = jnp.arange(COLS)[None] % 256
    is_q, is_k = lane < 128, (lane >= 128) & (lane < 192)
    squares = qkv * qkv
    square_sums = jnp.stack(
        [
            jnp.sum(jnp.where(is_q, squares, 0.0), axis=1),
            jnp.sum(jnp.where(is_k, squares, 0.0), axis=1),
        ]
    )
    square_sums = sum_parts(square_sums.reshape(2, PARTS, TOK)).reshape(2, ROWS)
    scale_q = lax.rsqrt(square_sums[0] / 1024 + EPSILON)[:, None]
    scale_k = lax.rsqrt(square_sums[1] / 512 + EPSILON)[:, None]
    packed = call_near(
        pack_kernel,
        (qkv, scale_q, scale_k, gain_heads, cosine, sine),
        [((N_CTX, PACK, 128), BF, True)],
        "pack",
    )[0]
    packed = exchange(packed, "ctx")
    scales = jnp.where(jnp.arange(128)[None] == 0, scale_q, scale_k)
    packed, part_ids = lax.optimization_barrier((packed, part_ids))

    sequence = fsdp ^ (place // (N_CTX // PARTS))
    seg_small = lax.dynamic_index_in_dim(
        small.reshape(N_CTX, 4, 8, 128), sequence, axis=1, keepdims=False
    )[:, 1:5, 32:96].astype(jnp.int32)
    seg_all = (seg_small[:, 0:2] + 256 * seg_small[:, 2:4]).reshape(N_CTX, TOK)
    seg_query = lax.dynamic_index_in_dim(
        seg_all.reshape(N_CTX, 2, QUARTERS, 16), place % QUARTERS, axis=2, keepdims=False
    ).reshape(TILES, 1, TOK_TILE)

    packed, shard_gate, shard_up, shard_down = lax.optimization_barrier(
        (packed, w_gate[0], w_up[0], w_down[0])
    )
    shards_far = [swap(shard, 2) for shard in (shard_gate, shard_up, shard_down)]
    gate_w, up_w, down_w = [
        in_order([own, swap(own, 1), far, swap(far, 1)], fsdp)
        for own, far in zip((shard_gate, shard_up, shard_down), shards_far)
    ]

    mixed, lse = attend(packed, seg_all, seg_query)
    returned = exchange(mixed, "ctx")
    returned = call_near(heads_in_kernel, (returned,), [((PARTS, TOK, FEATURES), BF, False)], "heads_in", 1)[0]
    pieces = swapped([returned[j] for j in range(PARTS)])
    out_parts = proj_out.reshape(PARTS, FEATURES, D)
    out_parts = [
        lax.dynamic_index_in_dim(out_parts, part ^ j, keepdims=False) for j in range(PARTS)
    ]
    inputs = tokens.astype(F32)
    middle = inputs
    for piece, out_part in zip(pieces, out_parts):
        middle = middle + dot(piece, out_part)
    scale_mid = inverse_rms(middle)
    scaled_mid = middle * scale_mid
    routed_in = (scaled_mid * gain_ffn).astype(BF)
    logits = dot(proj_router, routed_in, ((0,), (1,)))
    logits = jnp.where(chosen, logits, -1e30)
    raised = jnp.where(chosen, jnp.exp(logits - jnp.max(logits, axis=0, keepdims=True)), 0.0)
    gates = raised / jnp.sum(raised, axis=0, keepdims=True)

    upstream_low = cotangent[0]
    upstream = upstream_low.astype(F32)
    rows_out = dot(one_hot, routed_in).astype(BF).reshape(EXPERTS, CAP, D)
    arrived = exchange(rows_out, "ctx").reshape(N_CTX * CAP, D)
    share = jnp.where(places, gates[:, None, :], 0.0)
    row_share = jnp.sum(share, axis=2).reshape(EXPERTS * CAP, 1)
    grads_out = (dot(one_hot, upstream_low) * row_share).astype(BF).reshape(EXPERTS, CAP, D)
    arrived, grads_out, gate_w, up_w, down_w = lax.optimization_barrier(
        (arrived, grads_out, gate_w, up_w, down_w)
    )
    arrived_grad = exchange(grads_out, "ctx").reshape(N_CTX * CAP, D)

    gate_act = dot(arrived, gate_w)
    up_act = dot(arrived, up_w)
    sigma = jax.nn.sigmoid(gate_act)
    silu_gate = gate_act * sigma
    inner = (silu_gate * up_act).astype(BF)
    produced = dot(inner, down_w).astype(BF).reshape(N_CTX, CAP, D)
    produced, arrived_grad = lax.optimization_barrier((produced, arrived_grad))
    produced_home = exchange(produced, "ctx").reshape(EXPERTS * CAP, D)

    grad_inner = dot(arrived_grad, down_w, ((1,), (1,)))
    grad_gate_act = (grad_inner * up_act * sigma * (1.0 + gate_act * (1.0 - sigma))).astype(BF)
    grad_up_act = (grad_inner * silu_gate).astype(BF)
    grad_rows = dot(grad_gate_act, gate_w, ((1,), (1,))) + dot(grad_up_act, up_w, ((1,), (1,)))
    grad_rows = grad_rows.astype(BF).reshape(N_CTX, CAP, D)
    probs, kv_t = probabilities(packed, seg_all, seg_query, lse)
    produced_home, grad_rows, probs, kv_t = lax.optimization_barrier(
        (produced_home, grad_rows, probs, kv_t)
    )
    grad_home = exchange(grad_rows, "ctx").reshape(EXPERTS * CAP, D)

    grad_gate_w = dot(arrived, grad_gate_act, ((0,), (0,))).astype(BF)
    grad_up_w = dot(arrived, grad_up_act, ((0,), (0,))).astype(BF)
    grad_down_w = dot(inner, arrived_grad, ((0,), (0,))).astype(BF)
    grad_gate_up = jnp.stack([grad_gate_w, grad_up_w])
    grad_home, grad_down_w, grad_gate_up = lax.optimization_barrier(
        (grad_home, grad_down_w, grad_gate_up)
    )
    grad_gate_up = lax.psum_scatter(
        grad_gate_up, "fsdp", scatter_dimension=1, tiled=True
    ).astype(F32)

    share = share.reshape(EXPERTS * CAP, TOK)
    share_high = share.astype(BF)
    share_low = (share - share_high.astype(F32)).astype(BF)
    combined = dot(share_high, produced_home, ((0,), (0,)))
    combined = combined + dot(share_low, produced_home, ((0,), (0,)))
    layer_out = (middle + combined).astype(BF)[None]
    along = dot(produced_home, upstream_low, ((1,), (1,))).reshape(EXPERTS, CAP, TOK)
    grad_gates = jnp.sum(jnp.where(places, along, 0.0), axis=1)
    grad_chosen = gates * (grad_gates - jnp.sum(gates * grad_gates, axis=0, keepdims=True))
    grad_logits = grad_chosen.astype(BF)
    grad_routed = dot(grad_logits, proj_router, ((0,), (1,)))
    grad_routed = grad_routed + dot(one_hot, grad_home, ((0,), (0,)))
    through = grad_routed * gain_ffn
    grad_middle = upstream + scale_mid * (
        through - scaled_mid * jnp.mean(through * scaled_mid, axis=1, keepdims=True)
    )
    grad_branch = grad_middle.astype(BF)
    grad_mixed = [dot(grad_branch, out_part, ((1,), (1,))).astype(BF) for out_part in out_parts]
    upper = call_near(
        heads_out_kernel, tuple(swapped(grad_mixed)), [((N_CTX, 32, 128), BF, True)], "heads_out", 1
    )[0]
    upper = exchange(upper, "ctx")

    sorted_pieces = jnp.stack(pieces)
    attended = jnp.concatenate(
        [
            lax.dynamic_index_in_dim(sorted_pieces, part ^ p, keepdims=False)
            for p in range(PARTS)
        ],
        axis=1,
    )
    attended_2 = jnp.concatenate([attended, swap(attended, 1)], axis=0)
    branch_halves = jnp.stack([grad_branch[:, :512], grad_branch[:, 512:]])
    own_half = lax.dynamic_index_in_dim(branch_halves, core, keepdims=False)
    other_half = lax.dynamic_index_in_dim(branch_halves, 1 - core, keepdims=False)
    branch_2 = jnp.concatenate([own_half, swap(other_half, 1)], axis=0)
    late = call_near(
        finish_out_kernel,
        (
            attended_2,
            branch_2,
            routed_in,
            jnp.pad(grad_logits.T, ((0, 0), (0, 128 - EXPERTS))),
            (grad_routed * scaled_mid).astype(BF),
        ),
        [((D, 640), BF, True)],
        "finish_out",
    )[0]
    late, upper = lax.optimization_barrier((late, upper))
    first_sums = exchange(late.reshape(4 * N_CTX, 8, 640), both_axes)

    grads_home = attend_back(packed, probs, kv_t, upper, mixed)
    grads_home, first_sums = lax.optimization_barrier((grads_home, first_sums))
    grads_home = exchange(grads_home, "ctx")
    grads_home, grad_down_w = lax.optimization_barrier((grads_home, grad_down_w))
    grad_down = lax.psum_scatter(
        grad_down_w[None], "fsdp", scatter_dimension=1, tiled=True
    ).astype(F32)

    through_heads, sums, gain_grad = call(
        unpack_kernel,
        (grads_home, qkv, scales, gain_heads, cosine, sine),
        [((ROWS, COLS), F32), ((ROWS, 128), F32), ((8, COLS), F32)],
        "unpack",
    )
    last, grad_normed = call(
        finish_kernel,
        (
            through_heads,
            qkv,
            scales,
            sums,
            swap(sums, 1),
            normed_low,
            far(weights, cut=(slice(0, D), slice(0, COLS))),
            tokens,
            tokens_other,
            gain_grad,
        ),
        [
            ((D, COLS + 128), BF, (slice(0, COLS), slice(COLS, COLS + 128))),
            ((ROWS, D), F32),
        ],
        "finish",
        4,
        part_ids,
    )
    last_sums = exchange(last.reshape(4 * N_CTX, 8, COLS + 128), both_axes)

    grad_normed = grad_normed.reshape(PARTS, TOK, D)
    grad_normed = sum(swapped([grad_normed[j] for j in range(PARTS)]))
    through_in = grad_normed * gain_attn
    scaled_own = scaled_in[:TOK]
    input_grad = grad_middle + scale_in[:TOK] * (
        through_in - scaled_own * jnp.mean(through_in * scaled_own, axis=1, keepdims=True)
    )

    first_sums = jnp.sum(first_sums.reshape(2 * N_CTX, 2, 8, 640).astype(F32), axis=0)
    grad_out = jnp.concatenate([first_sums[0, :, :512], first_sums[1, :, :512]], axis=1)
    first_small = first_sums[0, :, 512:] + first_sums[1, :, 512:]
    ready = (
        input_grad[None],
        grad_out,
        first_small[:, 64],
        first_small[:, :EXPERTS],
        grad_gate_up[0][None],
        grad_gate_up[1][None],
        grad_down,
    )
    index = 4 * place + fsdp
    final_ids = jnp.stack(
        [index % 16 // 8, (128 - index % 8 * 8) % 128, (128 - index % 16 * 4) % 128]
    ).astype(jnp.int32)
    last_sums, ready, final_ids = lax.optimization_barrier((last_sums, ready, final_ids))
    grad_query, grad_key, grad_value, attn_gain, query_gain, key_gain = call(
        final_kernel,
        tuple(far(last_sums, cut=(slice(k * 32, k * 32 + 32),)) for k in range(4)),
        [
            ((8, 1024), F32),
            ((8, 512), F32),
            ((8, 512), F32),
            ((1, 8), F32),
            ((1, 8), F32),
            ((1, 4), F32),
        ],
        "final",
        2,
        final_ids,
    )
    return (
        layer_out,
        ready[0],
        attn_gain.reshape(8),
        grad_query,
        grad_key,
        grad_value,
        query_gain.reshape(8),
        key_gain.reshape(4),
        *ready[1:],
    )


def solution(mesh):
    row = P("fsdp", "ctx", None)
    flat = P(("ctx", "fsdp"))
    dense = P(("ctx", "fsdp"), None)
    expert = P("ctx", "fsdp", None)
    in_specs = (
        row,
        P("fsdp", "ctx"),
        P("fsdp", None),
        row,
        row,
        flat,
        dense,
        dense,
        dense,
        flat,
        flat,
        dense,
        flat,
        dense,
        expert,
        expert,
        expert,
        row,
    )
    out_specs = (
        row,
        row,
        flat,
        dense,
        dense,
        dense,
        flat,
        flat,
        dense,
        flat,
        dense,
        expert,
        expert,
        expert,
    )
    return jax.shard_map(shards, mesh=mesh, in_specs=in_specs, out_specs=out_specs, check_vma=False)
```
